128 devices in a mesh: seq: 8 (over x, core), dp: 4 (over z), tensor: 4 (over y).
Axes of the slice: x: 4, y: 4, z: 4, core: 2. Of those that a mesh axis runs over, the one named last changes fastest.
Arguments:
- tokens: bfloat16 [16, 1024, 2048], P('dp', 'seq'), may hold values from -6 to 6
- init_state: float32 [16, 2560], P('dp', 'tensor'), may hold values from -6 to 6
- conv_state: bfloat16 [16, 3, 2560], P('dp', None, 'tensor'), may hold values from -6 to 6
- fresh_rows: int32 [16], P('dp'), may hold values 0 or 1
- doc_start: int32 [16], P('dp'), may hold values from 1 to 1024, as said below
- norm_gains: bfloat16 [2, 2048], replicated, may hold values from 0.5 to 1.5
- mix_in: bfloat16 [2, 2048, 2560], P(None, ('seq', 'dp'), 'tensor'), may hold values from -0.125 to 0.125
- mix_out: bfloat16 [2560, 2048], P('tensor', ('seq', 'dp')), may hold values from -0.25 to 0.25
- conv_weight: bfloat16 [4, 2560], P(None, 'tensor'), may hold values from -3 to 3
- conv_bias: bfloat16 [2560], P('tensor'), may hold values from -3 to 3
- gate_blocks: bfloat16 [2, 16, 160, 160], P(None, 'tensor'), may hold values from -0.5 to 0.5
- gate_bias: bfloat16 [2, 2560], P(None, 'tensor'), may hold values from -4 to 4
- decay_param: bfloat16 [2560], P('tensor'), may hold values from -8 to -3
- mlp_in: bfloat16 [2, 2048, 6144], P(None, ('seq', 'dp'), 'tensor'), may hold values from -0.125 to 0.125
- mlp_out: bfloat16 [6144, 2048], P('tensor', ('seq', 'dp')), may hold values from -0.078125 to 0.078125
- cotangent: bfloat16 [16, 1024, 2048], P('dp', 'seq'), may hold values from -6 to 6
Outputs:
- block_out: bfloat16 [16, 1024, 2048], P('dp', 'seq')
- lru_states: float32 [16, 1024, 2560], P('dp', 'seq', 'tensor')
- grad_tokens: bfloat16 [16, 1024, 2048], P('dp', 'seq')
- grad_gains: float32 [2, 2048], replicated
- grad_mix_in: float32 [2, 2048, 2560], P(None, ('seq', 'dp'), 'tensor')
- grad_mix_out: float32 [2560, 2048], P('tensor', ('seq', 'dp'))
- grad_conv_weight: float32 [4, 2560], P(None, 'tensor')
- grad_conv_bias: float32 [2560], P('tensor')
- grad_gate_blocks: float32 [2, 16, 160, 160], P(None, 'tensor')
- grad_gate_bias: float32 [2, 2560], P(None, 'tensor')
- grad_decay: float32 [2560], P('tensor')
- grad_mlp_in: float32 [2, 2048, 6144], P(None, ('seq', 'dp'), 'tensor')
- grad_mlp_out: float32 [6144, 2048], P('tensor', ('seq', 'dp'))
The draws below stay inside these ranges and needn't reach their ends.
Inputs may be any that keep to these rules, and one draw needn't show every extreme that they name: Positions at (doc_start) and later form a second document that starts from zero states; 1024 means the sequence holds one document. Among the 4 sequences of each index of dp, one has 1024. `fresh_rows`: 1 marks a sequence whose initial recurrence and convolution states are zero whatever init_state and conv_state hold.
All inputs are finite; a program needn't handle non-finite values. No bound on the sum of `fresh_rows` on one device may be relied on, other than what follows from the above.
Results may differ from the reference program's by a relative error of at most 0.025.
Values may be sent and summed in bfloat16 or wider, within the bound.
A program may use at most 192 MiB of HBM per device.

```python
import jax
import jax.numpy as jnp
from jax import lax

D = 2048
R = 2560
FF = 6144
HEADS = 16
CONV = 4
LEN = 1024
ROWS = 4
BLK = 160
ROWS_ALL = 16


def draw_doc_start(key, part):
    key = jax.random.fold_in(key, 11)
    key_begin, key_pick = jax.random.split(key)
    begin_at = jax.random.randint(key_begin, (ROWS_ALL,), 1, LEN + 1)
    chosen = jax.random.randint(key_pick, (ROWS_ALL // ROWS,), 0, ROWS)
    row_ids = jnp.arange(ROWS_ALL)
    single_doc = row_ids % ROWS == chosen[row_ids // ROWS]
    return jnp.where(single_doc, LEN, begin_at).astype(jnp.int32)


def touch_ends(values, own_key, least, high):
    dims = values.shape
    index_at = [jax.random.randint(jax.random.fold_in(own_key, axis), (), 0, dims[axis]) for axis in range(len(dims))]
    values = values.at[tuple(index_at)].set(least)
    longest = dims.index(max(dims))
    index_at[longest] = (index_at[longest] + 1) % dims[longest]
    return values.at[tuple(index_at)].set(high)


def level_of(stream_key, shape, shards, smallest, top_value):
    def one(dim, blocks):
        heights = jax.random.uniform(jax.random.fold_in(jax.random.fold_in(stream_key, 6), dim), (blocks,), jnp.float32, smallest / len(shards), top_value / len(shards))
        return jnp.repeat(jnp.exp(heights), shape[dim] // blocks).reshape((-1,) + (1,) * (len(shape) - dim - 1))

    gain = one(*shards[0])
    for cut in shards[1:]:
        gain = gain * one(*cut)
    return gain


def centred(rng, shape, spread, bound, shards=(), kind=jnp.bfloat16):
    factor_of = level_of(rng, shape, shards, -0.22, 0.18) if shards else 1.0
    drawn = jax.random.normal(rng, shape, jnp.float32) * spread * factor_of
    return jnp.minimum(jnp.maximum(drawn, -bound), bound).astype(kind)


def setup_inputs(seed: int = 0) -> dict:
    arg_keys = jax.random.split(jax.random.key(seed), 17)
    tokens = centred(arg_keys[0], (ROWS_ALL, LEN, D), 1.0, 6.0, ((0, 4), (1, 8)))
    init_state = centred(arg_keys[1], (ROWS_ALL, R), 1.0, 6.0, ((0, 4), (1, 4)), jnp.float32)
    conv_state = centred(arg_keys[2], (ROWS_ALL, CONV - 1, R), 1.0, 6.0, ((0, 4), (2, 4)))
    fresh_rows = touch_ends((jax.random.randint(arg_keys[3], (ROWS_ALL,), 0, 3) < 1).astype(jnp.int32), jax.random.fold_in(arg_keys[3], 1), 0, 1)
    doc_start = draw_doc_start(jax.random.fold_in(arg_keys[16], 71), 0)
    norm_gains = jnp.clip(1.0 + 0.1 * jax.random.normal(arg_keys[5], (2, D), jnp.float32), 0.5, 1.5).astype(jnp.bfloat16)
    mix_in = centred(arg_keys[6], (2, D, R), D ** -0.5, 0.125, ((1, 32), (2, 4)))
    mix_out = centred(arg_keys[7], (R, D), (R // 4) ** -0.5, 0.25, ((0, 4), (1, 32)))
    conv_weight = centred(arg_keys[8], (CONV, R), CONV ** -0.5, 3.0, ((1, 4),))
    conv_bias = centred(arg_keys[9], (R,), 0.5, 3.0, ((0, 4),))
    gate_blocks = centred(arg_keys[10], (2, HEADS, BLK, BLK), BLK ** -0.5, 0.5, ((1, 4),))
    gate_bias = centred(arg_keys[11], (2, R), 1.0, 4.0, ((1, 4),))
    decay_param = jnp.clip(-8.0 + 5.0 * jax.random.uniform(arg_keys[12], (R,), jnp.float32) ** level_of(arg_keys[12], (R,), ((0, 4),), -0.2, 0.2), -8.0, -3.0).astype(jnp.bfloat16)
    mlp_in = centred(arg_keys[13], (2, D, FF), D ** -0.5, 0.125, ((1, 32), (2, 4)))
    mlp_out = centred(arg_keys[14], (FF, D), FF ** -0.5, 0.078125, ((0, 4), (1, 32)))
    cotangent = centred(arg_keys[15], (ROWS_ALL, LEN, D), 1.0, 6.0, ((0, 4), (1, 8)))
    return {"tokens": tokens, "init_state": init_state, "conv_state": conv_state, "fresh_rows": fresh_rows, "doc_start": doc_start, "norm_gains": norm_gains, "mix_in": mix_in, "mix_out": mix_out, "conv_weight": conv_weight, "conv_bias": conv_bias, "gate_blocks": gate_blocks, "gate_bias": gate_bias, "decay_param": decay_param, "mlp_in": mlp_in, "mlp_out": mlp_out, "cotangent": cotangent}


@jax.custom_vjp
def low(v):
    return lax.optimization_barrier(v.astype(jnp.bfloat16)).astype(jnp.float32)

@jax.custom_vjp
def low_back(v):
    return v

def low_keep(v):
    return (low(v), None)

def low_pass(kept, grad):
    return (grad,)

def back_keep(v):
    return (v, None)

def back_low(kept, grad):
    return (low(grad),)
low.defvjp(low_keep, low_pass)
low_back.defvjp(back_keep, back_low)
epsilon = 1e-06
root_floor = 0.001
rate_scale = 8.0

def smooth_gate(values):
    return jax.nn.gelu(values, approximate=True)

def rms_scale(stream, gain_row):
    return stream * lax.rsqrt(lax.optimization_barrier(jnp.mean(stream * stream, axis=-1, keepdims=True)) + epsilon) * gain_row

def matmul_hi(left_side, right_side):
    return jnp.dot(left_side, right_side, precision=lax.Precision.HIGHEST)

def linear_step(earlier, later_pair):
    return (earlier[0] * later_pair[0], later_pair[0] * earlier[1] + later_pair[1])

def row_forward(stream, start_state, start_conv, doc_begin, norm_gains, mix_in, mix_out, conv_weight, conv_bias, gate_blocks, gate_bias, decay_param, mlp_in, mlp_out):
    length = stream.shape[0]
    lru_width = mix_out.shape[0]
    head_count = gate_blocks.shape[1]
    block_size = gate_blocks.shape[2]
    rim_len = CONV - 1
    normed_in = low(rms_scale(stream, norm_gains[0]))
    branch_pre = low_back(matmul_hi(normed_in, mix_in[0]))
    conv_input = low(low_back(matmul_hi(normed_in, mix_in[1])))
    extended = jnp.concatenate([start_conv, conv_input], axis=0)
    places = jnp.arange(-rim_len, length)
    in_second = places >= doc_begin
    conv_sum = conv_bias + jnp.zeros_like(conv_input)
    for tap_index in range(CONV):
        same_doc = (in_second[tap_index:tap_index + length] == in_second[rim_len:]).astype(jnp.float32)
        conv_sum = conv_sum + conv_weight[tap_index] * extended[tap_index:tap_index + length] * same_doc[:, None]
    conv_out = low(conv_sum)
    grouped = conv_out.reshape(length, head_count, block_size)
    decay_pre = low_back(jnp.einsum('thi,hij->thj', grouped, gate_blocks[0], precision=lax.Precision.HIGHEST).reshape(length, lru_width)) + gate_bias[0]
    input_pre = low_back(jnp.einsum('thi,hij->thj', grouped, gate_blocks[1], precision=lax.Precision.HIGHEST).reshape(length, lru_width)) + gate_bias[1]
    decay_gate = jax.nn.sigmoid(decay_pre)
    input_gate = jax.nn.sigmoid(input_pre)
    decay_now = jnp.exp(-rate_scale * decay_gate * jax.nn.softplus(decay_param))
    input_root = jnp.sqrt(jnp.maximum(1.0 - decay_now * decay_now, root_floor))
    fed_value = input_root * input_gate * conv_out
    keep_step = (jnp.arange(length) != doc_begin).astype(jnp.float32)
    carried = decay_now * keep_step[:, None]
    first_row = fed_value[:1] + carried[:1] * start_state[None, :]
    fed_value = jnp.concatenate([first_row, fed_value[1:]], axis=0)
    states = lax.associative_scan(linear_step, (carried, fed_value), axis=0)[1]
    mixed_low = low(states * smooth_gate(branch_pre))
    after_mix = stream + low_back(matmul_hi(mixed_low, mix_out))
    normed_mid = low(rms_scale(after_mix, norm_gains[1]))
    gate_in = low_back(matmul_hi(normed_mid, mlp_in[0]))
    up_in = low_back(matmul_hi(normed_mid, mlp_in[1]))
    hidden = low(smooth_gate(gate_in) * up_in)
    result = after_mix + low_back(matmul_hi(hidden, mlp_out))
    return (result, states)

def reference(tokens, init_state, conv_state, fresh_rows, doc_start, norm_gains, mix_in, mix_out, conv_weight, conv_bias, gate_blocks, gate_bias, decay_param, mlp_in, mlp_out, cotangent):
    params = tuple((weight_arg.astype(jnp.float32) for weight_arg in (norm_gains, mix_in, mix_out, conv_weight, conv_bias, gate_blocks, gate_bias, decay_param, mlp_in, mlp_out)))

    def one_row(totals, row_data):
        stream, start_state, start_conv, fresh_flag, doc_begin, row_cot = row_data
        keep_init = 1.0 - fresh_flag.astype(jnp.float32)

        def forward(stream_in, *weights):
            return row_forward(stream_in, start_state * keep_init, start_conv * keep_init, doc_begin, *weights)
        (result, states), pull_back = jax.vjp(forward, stream, *params)
        gradients = pull_back((row_cot, jnp.zeros_like(states)))
        totals = tuple((summed + gradient for summed, gradient in zip(totals, gradients[1:])))
        return (totals, (result.astype(jnp.bfloat16), states, gradients[0].astype(jnp.bfloat16)))
    zero_sums = tuple((jnp.zeros_like(weight_arg) for weight_arg in params))
    totals, (block_out, lru_states, grad_tokens) = lax.scan(one_row, zero_sums, (tokens.astype(jnp.float32), init_state, conv_state.astype(jnp.float32), fresh_rows, doc_start, cotangent.astype(jnp.float32)))
    return (block_out, lru_states, grad_tokens, totals[0], totals[1], totals[2], totals[3], totals[4], totals[5], totals[6], totals[7], totals[8], totals[9])
```

```python
import functools

import jax
import jax.numpy as jnp
from jax import lax
from jax.experimental import pallas as pl
from jax.experimental.pallas import tpu as pltpu
from jax.sharding import PartitionSpec as P

MESH = pl.DeviceIdType.MESH
F32 = jnp.float32
BF16 = jnp.bfloat16
VMEM_BYTES = 60 * 2**20

CONV = 4
ROWS = 4
SPAN = 128
TOKENS = ROWS * SPAN
WIDTH = 2048
CHAN = 640
HEADS = 4
BLK = 160
MLP = 1536
MIX_COLS = 3 * CHAN
MLP_COLS = 3 * MLP
LANES = 128
GROUPS = CHAN // LANES
PAD = 8

epsilon = 1e-06
root_floor = 0.001
rate_scale = 8.0


class Place:
    def __init__(self):
        self.s = lax.axis_index("seq")
        self.z = lax.axis_index("dp")
        self.y = lax.axis_index("tensor")
        self.x, self.c = lax.div(self.s, 2), lax.rem(self.s, 2)
        x, c, z, y = self.x, self.c, self.z, self.y
        self.xr, self.xl = lax.rem(x + 1, 4), lax.rem(x + 3, 4)
        self.zr, self.zl = lax.rem(z + 1, 4), lax.rem(z + 3, 4)
        self.yr, self.yl, self.y2 = lax.rem(y + 1, 4), lax.rem(y + 3, 4), lax.rem(y + 2, 4)
        self.XR, self.XL = {"seq": self.xr * 2 + c}, {"seq": self.xl * 2 + c}
        self.ZR, self.ZL = {"dp": self.zr}, {"dp": self.zl}
        self.YR, self.YL = {"tensor": self.yr}, {"tensor": self.yl}
        self.SIB = {"seq": x * 2 + 1 - c}

    def seq_at(self, distance):
        return {"seq": lax.rem(self.s + distance + 8, 8)}


def greet(devices):
    barrier = pltpu.get_barrier_semaphore()
    for device in devices:
        pl.semaphore_signal(barrier, inc=1, device_id=device, device_id_type=MESH)
    pl.semaphore_wait(barrier, len(devices))


class Links:
    def __init__(self, send, recv):
        self.send, self.recv = send, recv
        self.count = 0
        self.started = []

    def go(self, src, dst, device):
        k = self.count
        self.count += 1
        copy = pltpu.make_async_remote_copy(
            src_ref=src,
            dst_ref=dst,
            send_sem=self.send.at[k],
            recv_sem=self.recv.at[k],
            device_id=device,
            device_id_type=MESH,
        )
        copy.start()
        self.started.append(copy)
        return k

    def arrived(self, view, k, device):
        pltpu.make_async_remote_copy(
            src_ref=view,
            dst_ref=view,
            send_sem=self.send.at[k],
            recv_sem=self.recv.at[k],
            device_id=device,
            device_id_type=MESH,
        ).wait_recv()

    def drain(self):
        for copy in self.started:
            copy.wait_send()
        self.started = []


class Gather:
    def __init__(self, links, place, out):
        self.links, self.p, self.out = links, place, out
        self.to_sibling = []

    def _pass_on(self, view_of):
        k = self.links.go(view_of(self.p.c), view_of(self.p.c), self.p.SIB)
        self.to_sibling.append((view_of, k))

    def _ring(self, blk, i, right, left, base):
        links, p = self.links, self.p
        c = p.c
        ir, il, i2 = lax.rem(i + 1, 4), lax.rem(i + 3, 4), lax.rem(i + 2, 4)
        a, b = pl.ds(base, 16), pl.ds(base + 16, 16)
        k0 = links.go(blk(c, i, a), blk(c, i, a), right)
        k1 = links.go(blk(c, i, b), blk(c, i, b), left)
        k2 = links.go(blk(c, i, b), blk(c, i, b), right)
        k3 = links.go(blk(c, i, a), blk(c, i, a), left)

        def middle():
            links.arrived(blk(c, il, a), k0, left)
            k4 = links.go(blk(c, il, a), blk(c, il, a), right)
            links.arrived(blk(c, ir, b), k1, right)
            k5 = links.go(blk(c, ir, b), blk(c, ir, b), left)
            self._pass_on(lambda cc: blk(cc, il, a))
            self._pass_on(lambda cc: blk(cc, ir, b))
            return k4, k5

        def finish(later):
            for view, k, source in (
                (lambda cc: blk(cc, il, b), k2, left),
                (lambda cc: blk(cc, ir, a), k3, right),
                (lambda cc: blk(cc, i2, a), later[0], left),
                (lambda cc: blk(cc, i2, b), later[1], right),
            ):
                links.arrived(view(c), k, source)
                self._pass_on(view)

        return middle, finish

    def first(self):
        p, out = self.p, self.out
        self.x_ring = self._ring(lambda cc, j, r: out.at[j, cc, p.z, r], p.x, p.XR, p.XL, 0)
        self.z_ring = self._ring(lambda cc, j, r: out.at[p.x, cc, j, r], p.z, p.ZR, p.ZL, 32)
        self._pass_on(lambda cc: out.at[p.x, cc, p.z])

    def second(self):
        p, out = self.p, self.out
        self.x_ring = self._ring(lambda cc, j, r: out.at[:, cc, j, r], p.z, p.ZR, p.ZL, 0)
        self.z_ring = self._ring(lambda cc, j, r: out.at[j, cc, :, r], p.x, p.XR, p.XL, 32)

    def middle(self):
        self.later = (self.x_ring[0](), self.z_ring[0]())

    def finish(self):
        self.x_ring[1](self.later[0])
        self.z_ring[1](self.later[1])

    def settle(self):
        for view_of, k in self.to_sibling:
            self.links.arrived(view_of(1 - self.p.c), k, self.p.SIB)


CA, CB = pl.ds(0, WIDTH // 2), pl.ds(WIDTH // 2, WIDTH // 2)
HALF = WIDTH // 2


class Reduce:
    def __init__(self, links, place, part, far, near):
        self.links, self.p, self.part, self.far, self.near = links, place, part, far, near

    def send_far(self):
        p, part = self.p, self.part
        self.k0 = self.links.go(part.at[p.y2, :, CA], self.far.at[0], p.YR)
        self.k1 = self.links.go(part.at[p.y2, :, CB], self.far.at[1], p.YL)

    def send_near(self):
        p, part, near = self.p, self.part, self.near
        self.k2 = self.links.go(part.at[p.yr, :, CB], near.at[0, :, CB], p.YR)
        self.k3 = self.links.go(part.at[p.yl, :, CA], near.at[1, :, CA], p.YL)

    def merge(self):
        p, part, near, far = self.p, self.part, self.near, self.far
        self.links.arrived(far.at[0], self.k0, p.YL)
        far[0] = (far[0].astype(F32) + part[p.yr, :, 0:HALF].astype(F32)).astype(BF16)
        self.k4 = self.links.go(far.at[0], near.at[0, :, CA], p.YR)
        self.links.arrived(far.at[1], self.k1, p.YR)
        far[1] = (far[1].astype(F32) + part[p.yl, :, HALF:WIDTH].astype(F32)).astype(BF16)
        self.k5 = self.links.go(far.at[1], near.at[1, :, CB], p.YL)

    def settle(self):
        p, near = self.p, self.near
        self.links.arrived(near.at[0, :, CB], self.k2, p.YL)
        self.links.arrived(near.at[1, :, CA], self.k3, p.YR)
        self.links.arrived(near.at[0, :, CA], self.k4, p.YL)
        self.links.arrived(near.at[1, :, CB], self.k5, p.YR)


class Spread:
    def __init__(self, links, place, out):
        self.links, self.p, self.out = links, place, out

    def start(self):
        go, out, y, p = self.links.go, self.out, self.p.y, self.p
        self.k0 = go(out.at[y, :, CA], out.at[y, :, CA], p.YR)
        self.k1 = go(out.at[y, :, CB], out.at[y, :, CB], p.YL)
        self.k2 = go(out.at[y, :, CB], out.at[y, :, CB], p.YR)
        self.k3 = go(out.at[y, :, CA], out.at[y, :, CA], p.YL)

    def forward(self):
        go, out, p, arrived = self.links.go, self.out, self.p, self.links.arrived
        arrived(out.at[p.yl, :, CA], self.k0, p.YL)
        self.k4 = go(out.at[p.yl, :, CA], out.at[p.yl, :, CA], p.YR)
        arrived(out.at[p.yr, :, CB], self.k1, p.YR)
        self.k5 = go(out.at[p.yr, :, CB], out.at[p.yr, :, CB], p.YL)

    def near(self):
        out, p, arrived = self.out, self.p, self.links.arrived
        arrived(out.at[p.yl, :, CB], self.k2, p.YL)
        arrived(out.at[p.yr, :, CA], self.k3, p.YR)

    def far(self):
        out, p, arrived = self.out, self.p, self.links.arrived
        arrived(out.at[p.y2, :, CA], self.k4, p.YL)
        arrived(out.at[p.y2, :, CB], self.k5, p.YR)


def dot(a, b):
    return jnp.dot(a, b, preferred_element_type=F32)


def dot_nt(a, b):
    return lax.dot_general(a, b, (((1,), (1,)), ((), ())), preferred_element_type=F32)


def dot_tn(a, b):
    return lax.dot_general(a, b, (((0,), (0,)), ((), ())), preferred_element_type=F32)


GELU_C = 0.7978845608028654
GELU_A = 0.044715


def gelu(v):
    return 0.5 * v * (1.0 + jnp.tanh(GELU_C * (v + GELU_A * v * v * v)))


def gelu_pair(v):
    t = jnp.tanh(GELU_C * (v + GELU_A * v * v * v))
    value = 0.5 * v * (1.0 + t)
    slope = 0.5 * (1.0 + t) + 0.5 * v * (1.0 - t * t) * (GELU_C * (1.0 + 3.0 * GELU_A * v * v))
    return value, slope


def tile_scan(a, b, reverse):
    row = lax.broadcasted_iota(jnp.int32, a.shape, 1)
    for step in (1, 2, 4):
        if reverse:
            shift, valid = 8 - step, row < 8 - step
        else:
            shift, valid = step, row >= step
        a_near, b_near = pltpu.roll(a, shift, 1), pltpu.roll(b, shift, 1)
        b = jnp.where(valid, a * b_near + b, b)
        a = jnp.where(valid, a * a_near, a)
    return a, b


def row_scan(a, b, reverse):
    tiles = SPAN // 8
    a, b = tile_scan(a.reshape(tiles, 8, LANES), b.reshape(tiles, 8, LANES), reverse)
    edge = 0 if reverse else 7
    order = range(tiles - 1, -1, -1) if reverse else range(tiles)
    out_a, out_b = [None] * tiles, [None] * tiles
    carry_a = carry_b = None
    for k in order:
        ak, bk = a[k], b[k]
        if carry_a is not None:
            bk = ak * carry_b + bk
            ak = ak * carry_a
        out_a[k], out_b[k] = ak, bk
        carry_a, carry_b = ak[edge : edge + 1], bk[edge : edge + 1]
    return jnp.concatenate(out_a, axis=0), jnp.concatenate(out_b, axis=0), carry_a, carry_b


def put_pair(ref, at, r, first, second):
    row = lax.broadcasted_iota(jnp.int32, (8, LANES), 0)
    ref[:, at] = jnp.where(row == r, first, jnp.where(row == ROWS + r, second, ref[:, at]))


def take_row(ref, at, r):
    row = lax.broadcasted_iota(jnp.int32, (8, LANES), 0)
    return jnp.sum(jnp.where(row == r, ref[:, at], 0.0), axis=0, keepdims=True)


def mix_forward_kernel(
    tokens,
    mix_shard,
    mlp_shard,
    init_state,
    conv_start,
    doc_start,
    gains,
    vectors,
    gate_w,
    mix_full_out,
    mlp_full,
    states_out,
    pre_out,
    ext_out,
    decay_out,
    input_out,
    conv_out,
    mixed_out,
    normed_in_out,
    entering_out,
    normed_mid,
    after_own,
    mix_full,
    normed_in,
    pre,
    ext,
    decay_g,
    input_g,
    conv_low,
    cum_a,
    loc_b,
    states,
    mixed,
    rim_send,
    rim_recv,
    totals,
    totals_in,
    entering,
    part,
    far,
    near,
    local,
    send,
    recv,
):
    p = Place()
    links = Links(send, recv)
    own_mix = pltpu.make_async_copy(mix_shard, mix_full.at[p.x, p.c, p.z], local.at[0])
    own_mlp = pltpu.make_async_copy(mlp_shard, mlp_full.at[p.x, p.c, p.z], local.at[1])
    own_mix.start()
    own_mlp.start()
    greet([p.seq_at(d) for d in range(1, 8)] + [p.ZR, p.ZL, p.YR, p.YL])
    own_mix.wait()
    mix_gather = Gather(links, p, mix_full)
    mix_gather.first()

    def norm_rows(first, last):
        def one(k, carry):
            at = pl.ds(pl.multiple_of(k * 32, 32), 32)
            stream = tokens[at, :].astype(F32)
            scale = lax.rsqrt(jnp.mean(stream * stream, axis=-1, keepdims=True) + epsilon)
            normed_in[at, :] = (stream * scale * gains[0:1, :]).astype(BF16)
            return carry

        lax.fori_loop(first, last, one, 0)

    norm_rows(0, 8)
    mix_gather.middle()
    mix_gather.finish()
    mix_gather.second()
    own_mlp.wait()
    norm_rows(8, 16)
    mix_gather.middle()
    mlp_gather = Gather(links, p, mlp_full)
    mlp_gather.first()
    mix_gather.finish()
    mix_gather.settle()
    saves = []

    def save(src, dst):
        copy = pltpu.make_async_copy(src, dst, local.at[2 + len(saves)])
        copy.start()
        saves.append(copy)

    save(mix_full, mix_full_out)
    save(normed_in, normed_in_out)

    def project(n, carry):
        at = pl.ds(pl.multiple_of(n * 256, 256), 256)
        pre[:, at] = dot(normed_in[...], mix_full[:, :, :, :, at].reshape(WIDTH, 256))
        return carry

    lax.fori_loop(0, 5, project, 0)
    mlp_gather.middle()
    mlp_gather.finish()
    mlp_gather.second()
    save(pre.at[:, pl.ds(0, CHAN)], pre_out)

    for r in range(ROWS):
        ext[r, PAD:, :] = pre[r * SPAN : (r + 1) * SPAN, CHAN : 2 * CHAN].astype(BF16).astype(F32)
        rim_send[r] = ext[r, SPAN : SPAN + PAD, :]
    k_rim = links.go(rim_send, rim_recv, p.seq_at(1))
    links.arrived(rim_recv, k_rim, p.seq_at(-1))
    at_start = p.s == 0
    for r in range(ROWS):
        ext[r, 0:PAD, :] = jnp.where(at_start, conv_start[r], rim_recv[r])
    offset = p.s * SPAN

    def conv_chunk(i, carry):
        r, g = lax.rem(i, ROWS), lax.div(i, ROWS)
        at = pl.ds(pl.multiple_of(g * LANES, LANES), LANES)
        place = offset + lax.broadcasted_iota(jnp.int32, (SPAN, LANES), 0)
        begin = doc_start[r]
        here = place >= begin
        total = jnp.zeros((SPAN, LANES), F32) + vectors[4:5, at]
        for k in range(CONV):
            value = ext[r, PAD - 3 + k : PAD - 3 + k + SPAN, at]
            same = (place - (3 - k) >= begin) == here
            total = total + vectors[k : k + 1, at] * jnp.where(same, value, 0.0)
        rows = pl.ds(pl.multiple_of(r * SPAN, SPAN), SPAN)
        conv_low[rows, at] = total.astype(BF16)
        return carry

    lax.fori_loop(0, ROWS * GROUPS, conv_chunk, 0)
    mlp_gather.middle()
    save(ext, ext_out)
    save(conv_low, conv_out)

    for j, target in ((0, decay_g), (1, input_g)):
        held = None
        for g in range(GROUPS):
            total = held
            if g < HEADS:
                product = dot(conv_low[:, g * LANES : g * LANES + 256], gate_w[j, g])
                total = product[:, :LANES] if held is None else held + product[:, :LANES]
                held = product[:, LANES:]
            target[:, g * LANES : (g + 1) * LANES] = total

    def gate_chunk(i, carry):
        r, g = lax.rem(i, ROWS), lax.div(i, ROWS)
        at = pl.ds(pl.multiple_of(g * LANES, LANES), LANES)
        rows = pl.ds(pl.multiple_of(r * SPAN, SPAN), SPAN)
        gate_d = jax.nn.sigmoid(decay_g[rows, at] + vectors[5:6, at])
        gate_i = jax.nn.sigmoid(input_g[rows, at] + vectors[6:7, at])
        decay_g[rows, at] = gate_d
        input_g[rows, at] = gate_i
        decay_now = jnp.exp(gate_d * vectors[7:8, at])
        root = jnp.sqrt(jnp.maximum(1.0 - decay_now * decay_now, root_floor))
        fed = root * gate_i * conv_low[rows, at].astype(F32)
        place = offset + lax.broadcasted_iota(jnp.int32, (SPAN, LANES), 0)
        carried = jnp.where(place == doc_start[r], 0.0, decay_now)
        a, b, last_a, last_b = row_scan(carried, fed, False)
        cum_a[rows, at] = a
        loc_b[rows, at] = b
        put_pair(totals, at, r, last_a, last_b)
        return carry

    totals[...] = jnp.zeros_like(totals)
    lax.fori_loop(0, ROWS * GROUPS, gate_chunk, 0)
    keys = [links.go(totals, totals_in.at[p.s], p.seq_at(d)) for d in range(1, 8)]
    save(decay_g, decay_out)
    save(input_g, input_out)
    mlp_gather.finish()
    state = init_state[...]
    for d in range(1, 8):
        links.arrived(totals_in.at[p.seq_at(-d)["seq"]], keys[d - 1], p.seq_at(-d))
    totals_in[p.s] = totals[...]
    for source in range(7):
        both = totals_in[source]
        state = jnp.where(source < p.s, both[0:ROWS] * state + both[ROWS:], state)
    entering[0:ROWS, :] = state
    entering[ROWS:, :] = jnp.zeros((8 - ROWS, CHAN), F32)

    def state_chunk(i, carry):
        r, g = lax.rem(i, ROWS), lax.div(i, ROWS)
        at = pl.ds(pl.multiple_of(g * LANES, LANES), LANES)
        rows = pl.ds(pl.multiple_of(r * SPAN, SPAN), SPAN)
        value = loc_b[rows, at] + cum_a[rows, at] * take_row(entering, at, r)
        states[rows, at] = value
        mixed[rows, at] = (value * gelu(pre[rows, at])).astype(BF16)
        return carry

    lax.fori_loop(0, ROWS * GROUPS, state_chunk, 0)
    save(states, states_out)
    save(mixed, mixed_out)
    save(entering, entering_out)

    def partial(row):
        left = mixed[pl.ds(pl.multiple_of(row * SPAN, SPAN), SPAN), :]

        def one(n, carry):
            weights = mix_full[lax.div(n, 2), lax.rem(n, 2), :, :, 2 * CHAN :].reshape(256, CHAN)
            part[row, :, pl.ds(pl.multiple_of(n * 256, 256), 256)] = dot_nt(left, weights).astype(BF16)
            return carry

        lax.fori_loop(0, 8, one, 0)

    reduce = Reduce(links, p, part, far, near)
    partial(p.y2)
    reduce.send_far()
    partial(p.yr)
    partial(p.yl)
    reduce.send_near()
    partial(p.y)
    reduce.merge()
    reduce.settle()

    def norm_mid(k, carry):
        at = pl.ds(pl.multiple_of(k * 16, 16), 16)
        total = part[p.y, at, :].astype(F32) + near[0, at, :].astype(F32) + near[1, at, :].astype(F32)
        row = pl.ds(pl.multiple_of(p.y * SPAN + k * 16, 16), 16)
        stream = tokens[row, :].astype(F32) + total
        scale = lax.rsqrt(jnp.mean(stream * stream, axis=-1, keepdims=True) + epsilon)
        after_own[at, :] = stream
        normed_mid[p.y, at, :] = (stream * scale * gains[1:2, :]).astype(BF16)
        return carry

    lax.fori_loop(0, SPAN // 16, norm_mid, 0)
    spread = Spread(links, p, normed_mid)
    spread.start()
    mlp_gather.settle()
    spread.forward()
    spread.near()
    spread.far()
    for copy in saves:
        copy.wait()
    links.drain()


def params(collective_id):
    return pltpu.CompilerParams(
        collective_id=collective_id, has_side_effects=True, vmem_limit_bytes=VMEM_BYTES
    )


def vmem():
    return pl.BlockSpec(memory_space=pltpu.VMEM)


def anyspace():
    return pl.BlockSpec(memory_space=pl.ANY)


def mix_forward(tokens, mix_shard, mlp_shard, init_state, conv_start, doc_start, gains, vectors, gate_w):
    shape = jax.ShapeDtypeStruct
    tc = (TOKENS, CHAN)
    ext_shape = (ROWS, PAD + SPAN, CHAN)
    outs = [
        shape((4, 2, 4, 64, MIX_COLS), BF16),
        shape((4, 2, 4, 64, MLP_COLS), BF16),
        shape(tc, F32),
        shape(tc, F32),
        shape(ext_shape, F32),
        shape(tc, F32),
        shape(tc, F32),
        shape(tc, BF16),
        shape(tc, BF16),
        shape((TOKENS, WIDTH), BF16),
        shape((8, CHAN), F32),
        shape((ROWS, SPAN, WIDTH), BF16),
        shape((SPAN, WIDTH), F32),
    ]
    scratch = [
        pltpu.VMEM((4, 2, 4, 64, MIX_COLS), BF16),
        pltpu.VMEM((TOKENS, WIDTH), BF16),
        pltpu.VMEM((TOKENS, 2 * CHAN), F32),
        pltpu.VMEM(ext_shape, F32),
        pltpu.VMEM(tc, F32),
        pltpu.VMEM(tc, F32),
        pltpu.VMEM(tc, BF16),
        pltpu.VMEM(tc, F32),
        pltpu.VMEM(tc, F32),
        pltpu.VMEM(tc, F32),
        pltpu.VMEM(tc, BF16),
        pltpu.VMEM((ROWS, PAD, CHAN), F32),
        pltpu.VMEM((ROWS, PAD, CHAN), F32),
        pltpu.VMEM((8, CHAN), F32),
        pltpu.VMEM((8, 8, CHAN), F32),
        pltpu.VMEM((8, CHAN), F32),
        pltpu.VMEM((ROWS, SPAN, WIDTH), BF16),
        pltpu.VMEM((2, SPAN, HALF), BF16),
        pltpu.VMEM((2, SPAN, WIDTH), BF16),
        pltpu.SemaphoreType.DMA((16,)),
        pltpu.SemaphoreType.DMA((128,)),
        pltpu.SemaphoreType.DMA((128,)),
    ]
    return pl.pallas_call(
        mix_forward_kernel,
        out_shape=outs,
        in_specs=[vmem(), anyspace(), anyspace(), vmem(), vmem(), pl.BlockSpec(memory_space=pltpu.SMEM)]
        + [vmem()] * 3,
        out_specs=[anyspace()] * 11 + [vmem()] * 2,
        scratch_shapes=scratch,
        compiler_params=params(0),
        name="mix_forward",
    )(tokens, mix_shard, mlp_shard, init_state, conv_start, doc_start, gains, vectors, gate_w)


def norm_back_rows(d_row, stream, gain_row):
    scale = lax.rsqrt(jnp.mean(stream * stream, axis=-1, keepdims=True) + epsilon)
    unit = stream * scale
    e = d_row * gain_row
    inner = jnp.mean(e * unit, axis=-1, keepdims=True)
    return scale * (e - unit * inner), d_row * unit


def own_sum(reduce, at):
    part, near = reduce.part, reduce.near
    return part[reduce.p.y, at, :].astype(F32) + near[0, at, :].astype(F32) + near[1, at, :].astype(F32)


def mid_back_kernel(
    part, after_own, upstream, gains, d_after_low, d_after_own, gain_mid, far, near, send, recv
):
    p = Place()
    links = Links(send, recv)
    greet([p.YR, p.YL])
    reduce = Reduce(links, p, part, far, near)
    reduce.send_far()
    reduce.send_near()
    gain_mid[...] = jnp.zeros_like(gain_mid)
    reduce.merge()
    reduce.settle()

    def one(k, carry):
        at = pl.ds(pl.multiple_of(k * 16, 16), 16)
        through, share = norm_back_rows(own_sum(reduce, at), after_own[at, :], gains[1:2, :])
        gain_mid[...] += share[0:8] + share[8:16]
        total = upstream[p.y, at, :].astype(F32) + through
        d_after_own[at, :] = total
        d_after_low[p.y, at, :] = total.astype(BF16)
        return carry

    lax.fori_loop(0, SPAN // 16, one, 0)
    spread = Spread(links, p, d_after_low)
    spread.start()
    spread.forward()
    spread.near()
    spread.far()
    links.drain()


def mid_back(part, after_own, upstream, gains):
    shape = jax.ShapeDtypeStruct
    return pl.pallas_call(
        mid_back_kernel,
        out_shape=[
            shape((ROWS, SPAN, WIDTH), BF16),
            shape((SPAN, WIDTH), F32),
            shape((8, WIDTH), F32),
        ],
        in_specs=[vmem()] * 4,
        out_specs=[vmem()] * 3,
        scratch_shapes=[
            pltpu.VMEM((2, SPAN, HALF), BF16),
            pltpu.VMEM((2, SPAN, WIDTH), BF16),
            pltpu.SemaphoreType.DMA((12,)),
            pltpu.SemaphoreType.DMA((12,)),
        ],
        compiler_params=params(1),
        name="mid_back",
    )(part, after_own, upstream, gains)


def mix_back_kernel(
    d_after_low,
    mix_full,
    states,
    pre,
    ext,
    decay_g,
    input_g,
    conv_low,
    entering,
    doc_start,
    vectors,
    gate_w,
    d_both,
    d_first,
    small,
    d_blocks,
    d_mixed,
    tail_a,
    d_gates,
    d_conv,
    body,
    rim_send,
    rim_recv,
    totals,
    totals_in,
    after,
    send,
    recv,
):
    p = Place()
    links = Links(send, recv)
    greet([p.seq_at(d) for d in range(1, 8)])
    for start, size in ((0, 256), (256, 256), (512, 128)):
        weights = mix_full[:, :, :, :, 2 * CHAN + start : 2 * CHAN + start + size].reshape(WIDTH, size)
        d_mixed[:, start : start + size] = dot(d_after_low[...], weights)
    small[...] = jnp.zeros_like(small)
    totals[...] = jnp.zeros_like(totals)
    offset = p.s * SPAN

    def chunk(i):
        r, g = lax.rem(i, ROWS), lax.div(i, ROWS)
        at = pl.ds(pl.multiple_of(g * LANES, LANES), LANES)
        rows = pl.ds(pl.multiple_of(r * SPAN, SPAN), SPAN)
        row = lax.broadcasted_iota(jnp.int32, (SPAN, LANES), 0)
        return r, g, at, rows, row

    def states_back(i, carry):
        r, g, at, rows, row = chunk(i)
        d_chunk = d_mixed[rows, at]
        value, slope = gelu_pair(pre[rows, at])
        d_both[rows, at] = (d_chunk * states[rows, at] * slope).astype(BF16)
        decay_now = jnp.exp(decay_g[rows, at] * vectors[7:8, at])
        carried = jnp.where(offset + row == doc_start[r], 0.0, decay_now)
        following = jnp.where(row == SPAN - 1, 1.0, pltpu.roll(carried, SPAN - 1, 0))
        a, b, first_a, first_b = row_scan(following, d_chunk * value, True)
        tail_a[rows, at] = a
        d_mixed[rows, at] = b
        put_pair(totals, at, r, carried[0:1] * first_a, carried[0:1] * first_b)
        return carry

    lax.fori_loop(0, ROWS * GROUPS, states_back, 0)
    keys = [links.go(totals, totals_in.at[p.s], p.seq_at(d)) for d in range(1, 8)]
    state = jnp.zeros((ROWS, CHAN), F32)
    for d in range(1, 8):
        links.arrived(totals_in.at[p.seq_at(-d)["seq"]], keys[d - 1], p.seq_at(-d))
    totals_in[p.s] = totals[...]
    for source in range(7, 0, -1):
        both = totals_in[source]
        state = jnp.where(source > p.s, both[0:ROWS] * state + both[ROWS:], state)
    after[0:ROWS, :] = state
    after[ROWS:, :] = jnp.zeros((8 - ROWS, CHAN), F32)

    def gates_back(i, carry):
        r, g, at, rows, row = chunk(i)
        grads = d_mixed[rows, at] + tail_a[rows, at] * take_row(after, at, r)
        held = states[rows, at]
        previous = jnp.where(row == 0, take_row(entering, at, r), pltpu.roll(held, 1, 0))
        gate_d, gate_i = decay_g[rows, at], input_g[rows, at]
        rate = vectors[7:8, at]
        decay_now = jnp.exp(gate_d * rate)
        headroom = 1.0 - decay_now * decay_now
        root = jnp.sqrt(jnp.maximum(headroom, root_floor))
        conv = conv_low[rows, at].astype(F32)
        d_decay = jnp.where(offset + row == doc_start[r], 0.0, grads * previous) - jnp.where(
            headroom > root_floor, grads * gate_i * conv * decay_now / root, 0.0
        )
        d_log = d_decay * decay_now
        d_zero = d_log * rate * gate_d * (1.0 - gate_d)
        fed = grads * root
        d_one = fed * conv * gate_i * (1.0 - gate_i)
        d_gates[rows, pl.ds(pl.multiple_of(g * LANES, LANES), LANES)] = d_zero.astype(BF16)
        d_gates[rows, pl.ds(pl.multiple_of(CHAN + g * LANES, LANES), LANES)] = d_one.astype(BF16)
        d_conv[rows, at] = fed * gate_i
        small[5:6, at] += jnp.sum(d_zero, axis=0, keepdims=True)
        small[6:7, at] += jnp.sum(d_one, axis=0, keepdims=True)
        small[7:8, at] += jnp.sum(d_log * (-rate_scale * gate_d), axis=0, keepdims=True)
        return carry

    lax.fori_loop(0, ROWS * GROUPS, gates_back, 0)

    held = None
    for g in range(GROUPS):
        total = d_conv[:, g * LANES : (g + 1) * LANES]
        if held is not None:
            total = total + held
        if g < HEADS:
            lo = g * LANES
            product = dot_nt(d_gates[:, lo : lo + 256], gate_w[0, g]) + dot_nt(
                d_gates[:, CHAN + lo : CHAN + lo + 256], gate_w[1, g]
            )
            total = total + product[:, :LANES]
            held = product[:, LANES:]
        d_conv[:, g * LANES : (g + 1) * LANES] = total

    def conv_back(i, carry):
        r, g, at, rows, row = chunk(i)
        d_chunk = d_conv[rows, at]
        begin = doc_start[r]
        place = offset + row
        here = place >= begin
        head = jnp.zeros((8, LANES), F32)
        total = jnp.zeros((SPAN, LANES), F32)
        for k in range(CONV):
            ahead = CONV - 1 - k
            same = (place - ahead >= begin) == here
            kept = jnp.where(same, d_chunk, 0.0)
            value = ext[r, PAD - ahead : PAD - ahead + SPAN, at]
            small[k : k + 1, at] += jnp.sum(kept * value, axis=0, keepdims=True)
            term = kept * vectors[k : k + 1, at]
            if ahead:
                total = total + jnp.where(row < SPAN - ahead, pltpu.roll(term, SPAN - ahead, 0), 0.0)
                head = head + jnp.where(row[0:8] >= 8 - ahead, pltpu.roll(term[0:8], 8 - ahead, 0), 0.0)
            else:
                total = total + term
        small[4:5, at] += jnp.sum(d_chunk, axis=0, keepdims=True)
        body[rows, at] = total
        rim_send[r, :, at] = head
        return carry

    lax.fori_loop(0, ROWS * GROUPS, conv_back, 0)
    k_rim = links.go(rim_send, rim_recv, p.seq_at(-1))
    for j in range(2):
        for h in range(HEADS):
            lo = h * LANES
            product = dot_tn(conv_low[:, lo : lo + 256], d_gates[:, j * CHAN + lo : j * CHAN + lo + 256])
            d_blocks[j, h] = product[32 * h : 32 * h + BLK, :]
    links.arrived(rim_recv, k_rim, p.seq_at(1))
    for r in range(ROWS):
        last = r * SPAN + SPAN - 8
        body[last : last + 8, :] += jnp.where(p.s == 7, 0.0, rim_recv[r])
    for r in range(ROWS):
        d_both[r * SPAN : (r + 1) * SPAN, CHAN:] = body[r * SPAN : (r + 1) * SPAN, :].astype(BF16)

    def first_part(n, carry):
        weights = mix_full[lax.div(n, 2), lax.rem(n, 2), :, :, 0 : 2 * CHAN].reshape(256, 2 * CHAN)
        d_first[:, pl.ds(pl.multiple_of(n * 256, 256), 256)] = dot_nt(d_both[...], weights).astype(BF16)
        return carry

    lax.fori_loop(0, 8, first_part, 0)
    links.drain()


def mix_back(d_after_low, saved, doc_start, vectors, gate_w):
    shape = jax.ShapeDtypeStruct
    tc = (TOKENS, CHAN)
    return pl.pallas_call(
        mix_back_kernel,
        out_shape=[
            shape((TOKENS, 2 * CHAN), BF16),
            shape((TOKENS, WIDTH), BF16),
            shape((8, CHAN), F32),
            shape((2, HEADS, BLK, 256), F32),
        ],
        in_specs=[vmem()] * 9 + [pl.BlockSpec(memory_space=pltpu.SMEM)] + [vmem()] * 2,
        out_specs=[vmem()] * 4,
        scratch_shapes=[
            pltpu.VMEM(tc, F32),
            pltpu.VMEM(tc, F32),
            pltpu.VMEM((TOKENS, 2 * CHAN), BF16),
            pltpu.VMEM(tc, F32),
            pltpu.VMEM(tc, F32),
            pltpu.VMEM((ROWS, PAD, CHAN), F32),
            pltpu.VMEM((ROWS, PAD, CHAN), F32),
            pltpu.VMEM((8, CHAN), F32),
            pltpu.VMEM((8, 8, CHAN), F32),
            pltpu.VMEM((8, CHAN), F32),
            pltpu.SemaphoreType.DMA((8,)),
            pltpu.SemaphoreType.DMA((8,)),
        ],
        compiler_params=params(2),
        name="mix_back",
    )(d_after_low, *saved, doc_start, vectors, gate_w)


def ends_kernel(
    first_part,
    out_part,
    tokens,
    after_own,
    d_after_own,
    gains,
    grad_tokens,
    block_out,
    gain_in,
    far_a,
    near_a,
    far_b,
    near_b,
    send,
    recv,
):
    p = Place()
    links = Links(send, recv)
    greet([p.YR, p.YL])
    back = Reduce(links, p, first_part, far_a, near_a)
    ahead = Reduce(links, p, out_part, far_b, near_b)
    back.send_far()
    back.send_near()
    ahead.send_far()
    ahead.send_near()
    gain_in[...] = jnp.zeros_like(gain_in)
    back.merge()
    back.settle()

    def back_rows(k, carry):
        at = pl.ds(pl.multiple_of(k * 16, 16), 16)
        through, share = norm_back_rows(
            own_sum(back, at), tokens[p.y, at, :].astype(F32), gains[0:1, :]
        )
        gain_in[...] += share[0:8] + share[8:16]
        grad_tokens[p.y, at, :] = (d_after_own[at, :] + through).astype(BF16)
        return carry

    lax.fori_loop(0, SPAN // 16, back_rows, 0)
    spread_a = Spread(links, p, grad_tokens)
    spread_a.start()
    ahead.merge()
    ahead.settle()

    def ahead_rows(k, carry):
        at = pl.ds(pl.multiple_of(k * 16, 16), 16)
        block_out[p.y, at, :] = (after_own[at, :] + own_sum(ahead, at)).astype(BF16)
        return carry

    lax.fori_loop(0, SPAN // 16, ahead_rows, 0)
    spread_b = Spread(links, p, block_out)
    spread_b.start()
    spread_a.forward()
    spread_b.forward()
    spread_a.near()
    spread_a.far()
    spread_b.near()
    spread_b.far()
    links.drain()


def ends(first_part, out_part, tokens, after_own, d_after_own, gains):
    shape = jax.ShapeDtypeStruct
    half = [pltpu.VMEM((2, SPAN, HALF), BF16), pltpu.VMEM((2, SPAN, WIDTH), BF16)]
    return pl.pallas_call(
        ends_kernel,
        out_shape=[
            shape((ROWS, SPAN, WIDTH), BF16),
            shape((ROWS, SPAN, WIDTH), BF16),
            shape((8, WIDTH), F32),
        ],
        in_specs=[vmem()] * 6,
        out_specs=[vmem()] * 3,
        scratch_shapes=half * 2 + [pltpu.SemaphoreType.DMA((24,)), pltpu.SemaphoreType.DMA((24,))],
        compiler_params=params(3),
        name="ends",
    )(first_part, out_part, tokens, after_own, d_after_own, gains)


def per_device(
    tokens,
    init_state,
    conv_state,
    fresh_rows,
    doc_start,
    norm_gains,
    mix_in,
    mix_out,
    conv_weight,
    conv_bias,
    gate_blocks,
    gate_bias,
    decay_param,
    mlp_in,
    mlp_out,
    cotangent,
):
    gains = norm_gains.astype(F32)
    keep = (1 - fresh_rows).astype(F32)
    decay_float = decay_param.astype(F32)
    mix_shard = jnp.concatenate([mix_in[0], mix_in[1], mix_out.T], axis=1)
    mlp_shard = jnp.concatenate([mlp_in[0], mlp_in[1], mlp_out.T], axis=1)
    conv_start = jnp.pad(conv_state.astype(F32) * keep[:, None, None], ((0, 0), (PAD - 3, 0), (0, 0)))
    vectors = jnp.concatenate(
        [
            conv_weight.astype(F32),
            conv_bias.astype(F32)[None],
            gate_bias.astype(F32),
            (-rate_scale * jax.nn.softplus(decay_float))[None],
        ],
        axis=0,
    )
    gate_w = jnp.stack(
        [
            jnp.pad(gate_blocks[:, h], ((0, 0), (32 * h, 96 - 32 * h), (32 * h, 96 - 32 * h)))
            for h in range(HEADS)
        ],
        axis=1,
    )
    rows = tokens.reshape(TOKENS, WIDTH)
    (
        mix_full,
        mlp_full,
        states,
        pre,
        ext,
        decay_g,
        input_g,
        conv_low,
        mixed,
        normed_in,
        entering,
        normed_mid,
        after_own,
    ) = mix_forward(
        rows, mix_shard, mlp_shard, init_state * keep[:, None], conv_start, doc_start, gains, vectors, gate_w
    )
    normed_mid = normed_mid.reshape(TOKENS, WIDTH)
    mlp_w = mlp_full.reshape(WIDTH, MLP_COLS)
    upstream = cotangent.reshape(TOKENS, WIDTH)

    gate_in = dot(normed_mid, mlp_w[:, :MLP])
    up_in = dot(normed_mid, mlp_w[:, MLP : 2 * MLP])
    d_hidden = dot(upstream, mlp_w[:, 2 * MLP :])
    act, slope = gelu_pair(gate_in)
    hidden = (act * up_in).astype(BF16)
    d_gate_up = jnp.concatenate(
        [(d_hidden * up_in * slope).astype(BF16), (d_hidden * act).astype(BF16)], axis=1
    )
    mid_part = dot_nt(d_gate_up, mlp_w[:, : 2 * MLP]).astype(BF16)
    out_part = dot_nt(hidden, mlp_w[:, 2 * MLP :]).astype(BF16)
    grad_mlp = jnp.concatenate(
        [dot_tn(normed_mid, d_gate_up).astype(BF16), dot_tn(upstream, hidden).astype(BF16)], axis=1
    )
    grad_mlp = lax.psum_scatter(grad_mlp, ("seq", "dp"), scatter_dimension=0, tiled=True).astype(F32)

    d_after_low, d_after_own, gain_mid = mid_back(
        mid_part.reshape(ROWS, SPAN, WIDTH), after_own, cotangent, gains
    )
    d_after_rows = d_after_low.reshape(TOKENS, WIDTH)
    d_both, d_first, small, d_blocks = mix_back(
        d_after_rows,
        (mix_full, states, pre, ext, decay_g, input_g, conv_low, entering),
        doc_start,
        vectors,
        gate_w,
    )
    grad_tokens, block_out, gain_in = ends(
        d_first.reshape(ROWS, SPAN, WIDTH),
        out_part.reshape(ROWS, SPAN, WIDTH),
        tokens,
        after_own,
        d_after_own,
        gains,
    )
    grad_mix = jnp.concatenate(
        [dot_tn(normed_in, d_both).astype(BF16), dot_tn(d_after_rows, mixed).astype(BF16)], axis=1
    )
    grad_mix = lax.psum_scatter(grad_mix, ("seq", "dp"), scatter_dimension=0, tiled=True).astype(F32)
    blocks = jnp.stack([d_blocks[:, h, :, 32 * h : 32 * h + BLK] for h in range(HEADS)], axis=1)
    small = lax.psum(small.astype(BF16), ("seq", "dp")).astype(F32)
    blocks = lax.psum(blocks.astype(BF16), ("seq", "dp")).astype(F32)
    grad_gains = jnp.stack([jnp.sum(gain_in, axis=0), jnp.sum(gain_mid, axis=0)])
    grad_gains = lax.psum(grad_gains.astype(BF16), ("seq", "dp", "tensor")).astype(F32)
    return (
        block_out,
        states.reshape(ROWS, SPAN, CHAN),
        grad_tokens,
        grad_gains,
        jnp.stack([grad_mix[:, :CHAN], grad_mix[:, CHAN : 2 * CHAN]]),
        grad_mix[:, 2 * CHAN :].T,
        small[0:4],
        small[4],
        blocks,
        small[5:7],
        small[7] * jax.nn.sigmoid(decay_float),
        jnp.stack([grad_mlp[:, :MLP], grad_mlp[:, MLP : 2 * MLP]]),
        grad_mlp[:, 2 * MLP :].T,
    )


def solution(mesh):
    in_specs = (
        P("dp", "seq", None),
        P("dp", "tensor"),
        P("dp", None, "tensor"),
        P("dp"),
        P("dp"),
        P(),
        P(None, ("seq", "dp"), "tensor"),
        P("tensor", ("seq", "dp")),
        P(None, "tensor"),
        P("tensor"),
        P(None, "tensor", None, None),
        P(None, "tensor"),
        P("tensor"),
        P(None, ("seq", "dp"), "tensor"),
        P("tensor", ("seq", "dp")),
        P("dp", "seq", None),
    )
    out_specs = (
        P("dp", "seq", None),
        P("dp", "seq", "tensor"),
        P("dp", "seq", None),
        P(),
        P(None, ("seq", "dp"), "tensor"),
        P("tensor", ("seq", "dp")),
        P(None, "tensor"),
        P("tensor"),
        P(None, "tensor", None, None),
        P(None, "tensor"),
        P("tensor"),
        P(None, ("seq", "dp"), "tensor"),
        P("tensor", ("seq", "dp")),
    )
    return jax.shard_map(
        per_device, mesh=mesh, in_specs=in_specs, out_specs=out_specs, check_vma=False
    )
```

```python
import functools

import jax
import jax.numpy as jnp
from jax import lax
from jax.experimental import pallas as pl
from jax.experimental.pallas import tpu as pltpu
from jax.sharding import PartitionSpec as P

MESH = pl.DeviceIdType.MESH
F32 = jnp.float32
BF16 = jnp.bfloat16
VMEM_BYTES = 60 * 2**20

CONV = 4
ROWS = 4
SPAN = 128
TOKENS = ROWS * SPAN
WIDTH = 2048
CHAN = 640
HEADS = 4
BLK = 160
MLP = 1536
MIX_COLS = 3 * CHAN
MLP_COLS = 3 * MLP
CHUNK = 256
CHUNKS = MLP // CHUNK
SMALL = 256
RS_COLS = MIX_COLS + SMALL
LANES = 128
GROUPS = CHAN // LANES
PAD = 8

epsilon = 1e-06
root_floor = 0.001
rate_scale = 8.0


class Place:
    def __init__(self):
        self.s = lax.axis_index("seq")
        self.z = lax.axis_index("dp")
        self.y = lax.axis_index("tensor")
        self.x, self.c = lax.div(self.s, 2), lax.rem(self.s, 2)
        x, c, z, y = self.x, self.c, self.z, self.y
        self.xr, self.xl = lax.rem(x + 1, 4), lax.rem(x + 3, 4)
        self.zr, self.zl = lax.rem(z + 1, 4), lax.rem(z + 3, 4)
        self.yr, self.yl, self.y2 = lax.rem(y + 1, 4), lax.rem(y + 3, 4), lax.rem(y + 2, 4)
        self.XR, self.XL = {"seq": self.xr * 2 + c}, {"seq": self.xl * 2 + c}
        self.ZR, self.ZL = {"dp": self.zr}, {"dp": self.zl}
        self.YR, self.YL = {"tensor": self.yr}, {"tensor": self.yl}
        self.SIB = {"seq": x * 2 + 1 - c}

    def seq_at(self, distance):
        return {"seq": lax.rem(self.s + distance + 8, 8)}


def greet(devices):
    barrier = pltpu.get_barrier_semaphore()
    for device in devices:
        pl.semaphore_signal(barrier, inc=1, device_id=device, device_id_type=MESH)
    pl.semaphore_wait(barrier, len(devices))


class Links:
    def __init__(self, send, recv):
        self.send, self.recv = send, recv
        self.count = 0
        self.started = []

    def go(self, src, dst, device):
        k = self.count
        self.count += 1
        copy = pltpu.make_async_remote_copy(
            src_ref=src,
            dst_ref=dst,
            send_sem=self.send.at[k],
            recv_sem=self.recv.at[k],
            device_id=device,
            device_id_type=MESH,
        )
        copy.start()
        self.started.append(copy)
        return k

    def arrived(self, view, k, device):
        pltpu.make_async_remote_copy(
            src_ref=view,
            dst_ref=view,
            send_sem=self.send.at[k],
            recv_sem=self.recv.at[k],
            device_id=device,
            device_id_type=MESH,
        ).wait_recv()

    def drain(self):
        for copy in self.started:
            copy.wait_send()
        self.started = []


class Gather:
    def __init__(self, links, place, out):
        self.links, self.p, self.out = links, place, out
        self.to_sibling = []

    def _pass_on(self, view_of):
        k = self.links.go(view_of(self.p.c), view_of(self.p.c), self.p.SIB)
        self.to_sibling.append((view_of, k))

    def _ring(self, blk, i, right, left, base):
        links, p = self.links, self.p
        c = p.c
        ir, il, i2 = lax.rem(i + 1, 4), lax.rem(i + 3, 4), lax.rem(i + 2, 4)
        a, b = pl.ds(base, 16), pl.ds(base + 16, 16)
        k0 = links.go(blk(c, i, a), blk(c, i, a), right)
        k1 = links.go(blk(c, i, b), blk(c, i, b), left)
        k2 = links.go(blk(c, i, b), blk(c, i, b), right)
        k3 = links.go(blk(c, i, a), blk(c, i, a), left)

        def middle():
            links.arrived(blk(c, il, a), k0, left)
            k4 = links.go(blk(c, il, a), blk(c, il, a), right)
            links.arrived(blk(c, ir, b), k1, right)
            k5 = links.go(blk(c, ir, b), blk(c, ir, b), left)
            self._pass_on(lambda cc: blk(cc, il, a))
            self._pass_on(lambda cc: blk(cc, ir, b))
            return k4, k5

        def finish(later):
            for view, k, source in (
                (lambda cc: blk(cc, il, b), k2, left),
                (lambda cc: blk(cc, ir, a), k3, right),
                (lambda cc: blk(cc, i2, a), later[0], left),
                (lambda cc: blk(cc, i2, b), later[1], right),
            ):
                links.arrived(view(c), k, source)
                self._pass_on(view)

        return middle, finish

    def first(self):
        p, out = self.p, self.out
        self.x_ring = self._ring(lambda cc, j, r: out.at[j, cc, p.z, r], p.x, p.XR, p.XL, 0)
        self.z_ring = self._ring(lambda cc, j, r: out.at[p.x, cc, j, r], p.z, p.ZR, p.ZL, 32)
        self._pass_on(lambda cc: out.at[p.x, cc, p.z])

    def second(self):
        p, out = self.p, self.out
        self.x_ring = self._ring(lambda cc, j, r: out.at[:, cc, j, r], p.z, p.ZR, p.ZL, 0)
        self.z_ring = self._ring(lambda cc, j, r: out.at[j, cc, :, r], p.x, p.XR, p.XL, 32)

    def middle(self):
        self.later = (self.x_ring[0](), self.z_ring[0]())

    def finish(self):
        self.x_ring[1](self.later[0])
        self.z_ring[1](self.later[1])

    def settle(self):
        for view_of, k in self.to_sibling:
            self.links.arrived(view_of(1 - self.p.c), k, self.p.SIB)


CA, CB = pl.ds(0, WIDTH // 2), pl.ds(WIDTH // 2, WIDTH // 2)
HALF = WIDTH // 2


class Reduce:
    def __init__(self, links, place, part, far, near):
        self.links, self.p, self.part, self.far, self.near = links, place, part, far, near

    def send_far(self):
        p, part = self.p, self.part
        self.k0 = self.links.go(part.at[p.y2, :, CA], self.far.at[0], p.YR)
        self.k1 = self.links.go(part.at[p.y2, :, CB], self.far.at[1], p.YL)

    def send_near(self):
        p, part, near = self.p, self.part, self.near
        self.k2 = self.links.go(part.at[p.yr, :, CB], near.at[0, :, CB], p.YR)
        self.k3 = self.links.go(part.at[p.yl, :, CA], near.at[1, :, CA], p.YL)

    def merge(self):
        p, part, near, far = self.p, self.part, self.near, self.far
        self.links.arrived(far.at[0], self.k0, p.YL)
        far[0] = (far[0].astype(F32) + part[p.yr, :, 0:HALF].astype(F32)).astype(BF16)
        self.k4 = self.links.go(far.at[0], near.at[0, :, CA], p.YR)
        self.links.arrived(far.at[1], self.k1, p.YR)
        far[1] = (far[1].astype(F32) + part[p.yl, :, HALF:WIDTH].astype(F32)).astype(BF16)
        self.k5 = self.links.go(far.at[1], near.at[1, :, CB], p.YL)

    def settle(self):
        p, near = self.p, self.near
        self.links.arrived(near.at[0, :, CB], self.k2, p.YL)
        self.links.arrived(near.at[1, :, CA], self.k3, p.YR)
        self.links.arrived(near.at[0, :, CA], self.k4, p.YL)
        self.links.arrived(near.at[1, :, CB], self.k5, p.YR)


class Spread:
    def __init__(self, links, place, out):
        self.links, self.p, self.out = links, place, out

    def start(self):
        go, out, y, p = self.links.go, self.out, self.p.y, self.p
        self.k0 = go(out.at[y, :, CA], out.at[y, :, CA], p.YR)
        self.k1 = go(out.at[y, :, CB], out.at[y, :, CB], p.YL)
        self.k2 = go(out.at[y, :, CB], out.at[y, :, CB], p.YR)
        self.k3 = go(out.at[y, :, CA], out.at[y, :, CA], p.YL)

    def forward(self):
        go, out, p, arrived = self.links.go, self.out, self.p, self.links.arrived
        arrived(out.at[p.yl, :, CA], self.k0, p.YL)
        self.k4 = go(out.at[p.yl, :, CA], out.at[p.yl, :, CA], p.YR)
        arrived(out.at[p.yr, :, CB], self.k1, p.YR)
        self.k5 = go(out.at[p.yr, :, CB], out.at[p.yr, :, CB], p.YL)

    def near(self):
        out, p, arrived = self.out, self.p, self.links.arrived
        arrived(out.at[p.yl, :, CB], self.k2, p.YL)
        arrived(out.at[p.yr, :, CA], self.k3, p.YR)

    def far(self):
        out, p, arrived = self.out, self.p, self.links.arrived
        arrived(out.at[p.y2, :, CA], self.k4, p.YL)
        arrived(out.at[p.y2, :, CB], self.k5, p.YR)


def dot(a, b):
    return jnp.dot(a, b, preferred_element_type=F32)


def dot_nt(a, b):
    return lax.dot_general(a, b, (((1,), (1,)), ((), ())), preferred_element_type=F32)


def dot_tn(a, b):
    return lax.dot_general(a, b, (((0,), (0,)), ((), ())), preferred_element_type=F32)


GELU_C = 0.7978845608028654
GELU_A = 0.044715


def gelu(v):
    return 0.5 * v * (1.0 + jnp.tanh(GELU_C * (v + GELU_A * v * v * v)))


def gelu_pair(v):
    t = jnp.tanh(GELU_C * (v + GELU_A * v * v * v))
    value = 0.5 * v * (1.0 + t)
    slope = 0.5 * (1.0 + t) + 0.5 * v * (1.0 - t * t) * (GELU_C * (1.0 + 3.0 * GELU_A * v * v))
    return value, slope


def tile_scan(a, b, reverse):
    row = lax.broadcasted_iota(jnp.int32, a.shape, 1)
    for step in (1, 2, 4):
        if reverse:
            shift, valid = 8 - step, row < 8 - step
        else:
            shift, valid = step, row >= step
        a_near, b_near = pltpu.roll(a, shift, 1), pltpu.roll(b, shift, 1)
        b = jnp.where(valid, a * b_near + b, b)
        a = jnp.where(valid, a * a_near, a)
    return a, b


def row_scan(a, b, reverse):
    tiles = SPAN // 8
    a, b = tile_scan(a.reshape(tiles, 8, LANES), b.reshape(tiles, 8, LANES), reverse)
    edge = 0 if reverse else 7
    order = range(tiles - 1, -1, -1) if reverse else range(tiles)
    out_a, out_b = [None] * tiles, [None] * tiles
    carry_a = carry_b = None
    for k in order:
        ak, bk = a[k], b[k]
        if carry_a is not None:
            bk = ak * carry_b + bk
            ak = ak * carry_a
        out_a[k], out_b[k] = ak, bk
        carry_a, carry_b = ak[edge : edge + 1], bk[edge : edge + 1]
    return jnp.concatenate(out_a, axis=0), jnp.concatenate(out_b, axis=0), carry_a, carry_b


def put_pair(ref, at, r, first, second):
    row = lax.broadcasted_iota(jnp.int32, (8, LANES), 0)
    ref[:, at] = jnp.where(row == r, first, jnp.where(row == ROWS + r, second, ref[:, at]))


def take_row(ref, at, r):
    row = lax.broadcasted_iota(jnp.int32, (8, LANES), 0)
    return jnp.sum(jnp.where(row == r, ref[:, at], 0.0), axis=0, keepdims=True)


def assemble_vectors(vectors, conv_weight, conv_bias, gate_bias, decay_param):
    vectors[0:4, :] = conv_weight[...].astype(F32)
    vectors[4:5, :] = conv_bias[...].astype(F32)
    vectors[5:7, :] = gate_bias[...].astype(F32)
    vectors[7:8, :] = -rate_scale * jnp.log1p(jnp.exp(decay_param[...].astype(F32)))


def mix_forward_kernel(
    tokens,
    mix_in,
    mix_out,
    mlp_in,
    mlp_out,
    init_state,
    conv_state,
    fresh_rows,
    doc_start,
    gain_rows,
    conv_weight,
    conv_bias,
    gate_bias,
    decay_param,
    gate_w,
    mix_full_out,
    mlp_full,
    states_out,
    pre_out,
    ext_out,
    decay_out,
    input_out,
    conv_out,
    mixed_out,
    normed_in_out,
    entering_out,
    vectors_out,
    normed_mid,
    after_own,
    mlp_own,
    gains,
    vectors,
    mix_full,
    normed_in,
    pre,
    ext,
    decay_g,
    input_g,
    conv_low,
    cum_a,
    loc_b,
    states,
    mixed,
    rim_send,
    rim_recv,
    totals,
    totals_in,
    entering,
    part,
    far,
    near,
    local,
    send,
    recv,
):
    p = Place()
    links = Links(send, recv)
    mine = mix_full.at[p.x, p.c, p.z]
    for j in range(2):
        mine[:, j * CHAN : (j + 1) * CHAN] = mix_in[j]
    mine[:, 2 * CHAN :] = mix_out[...].astype(F32).T.astype(BF16)
    greet([p.seq_at(d) for d in range(1, 8)] + [p.ZR, p.ZL, p.YR, p.YL])
    mix_gather = Gather(links, p, mix_full)
    mix_gather.first()
    down = mlp_out[...].astype(F32).T.astype(BF16)
    for f in range(CHUNKS):
        lo, to = f * CHUNK, 3 * f * CHUNK
        mlp_own[:, to : to + CHUNK] = mlp_in[0, :, lo : lo + CHUNK]
        mlp_own[:, to + CHUNK : to + 2 * CHUNK] = mlp_in[1, :, lo : lo + CHUNK]
        mlp_own[:, to + 2 * CHUNK : to + 3 * CHUNK] = down[:, lo : lo + CHUNK]
    own_mlp = pltpu.make_async_copy(mlp_own, mlp_full.at[p.x, p.c, p.z], local.at[0])
    own_mlp.start()
    gains[...] = gain_rows[...].astype(F32)
    assemble_vectors(vectors, conv_weight, conv_bias, gate_bias, decay_param)

    def norm_rows(first, last):
        def one(k, carry):
            at = pl.ds(pl.multiple_of(k * 32, 32), 32)
            stream = tokens[at, :].astype(F32)
            scale = lax.rsqrt(jnp.mean(stream * stream, axis=-1, keepdims=True) + epsilon)
            normed_in[at, :] = (stream * scale * gains[0:1, :]).astype(BF16)
            return carry

        lax.fori_loop(first, last, one, 0)

    norm_rows(0, 8)
    mix_gather.middle()
    mix_gather.finish()
    mix_gather.second()
    own_mlp.wait()
    norm_rows(8, 16)
    mix_gather.middle()
    mlp_gather = Gather(links, p, mlp_full)
    mlp_gather.first()
    mix_gather.finish()
    mix_gather.settle()
    saves = []

    def save(src, dst):
        copy = pltpu.make_async_copy(src, dst, local.at[2 + len(saves)])
        copy.start()
        saves.append(copy)

    save(mix_full, mix_full_out)
    save(normed_in, normed_in_out)
    save(vectors, vectors_out)

    def project(n, carry):
        at = pl.ds(pl.multiple_of(n * 256, 256), 256)
        pre[:, at] = dot(normed_in[...], mix_full[:, :, :, :, at].reshape(WIDTH, 256))
        return carry

    lax.fori_loop(0, 5, project, 0)
    mlp_gather.middle()
    mlp_gather.finish()
    mlp_gather.second()
    save(pre.at[:, pl.ds(0, CHAN)], pre_out)

    for r in range(ROWS):
        ext[r, PAD:, :] = pre[r * SPAN : (r + 1) * SPAN, CHAN : 2 * CHAN].astype(BF16).astype(F32)
        rim_send[r] = ext[r, SPAN : SPAN + PAD, :]
    k_rim = links.go(rim_send, rim_recv, p.seq_at(1))
    links.arrived(rim_recv, k_rim, p.seq_at(-1))
    at_start = p.s == 0
    for r in range(ROWS):
        keep = (1 - fresh_rows[r]).astype(F32)
        ext[r, 0:PAD, :] = jnp.where(at_start, 0.0, rim_recv[r])
        first_rim = conv_state[r].astype(F32) * keep
        ext[r, PAD - 3 : PAD, :] = jnp.where(at_start, first_rim, rim_recv[r, PAD - 3 : PAD, :])
    offset = p.s * SPAN

    def conv_chunk(i, carry):
        r, g = lax.rem(i, ROWS), lax.div(i, ROWS)
        at = pl.ds(pl.multiple_of(g * LANES, LANES), LANES)
        place = offset + lax.broadcasted_iota(jnp.int32, (SPAN, LANES), 0)
        begin = doc_start[r]
        here = place >= begin
        total = jnp.zeros((SPAN, LANES), F32) + vectors[4:5, at]
        for k in range(CONV):
            value = ext[r, PAD - 3 + k : PAD - 3 + k + SPAN, at]
            same = (place - (3 - k) >= begin) == here
            total = total + vectors[k : k + 1, at] * jnp.where(same, value, 0.0)
        rows = pl.ds(pl.multiple_of(r * SPAN, SPAN), SPAN)
        conv_low[rows, at] = total.astype(BF16)
        return carry

    lax.fori_loop(0, ROWS * GROUPS, conv_chunk, 0)
    save(ext, ext_out)
    save(conv_low, conv_out)

    for j, target in ((0, decay_g), (1, input_g)):
        held = None
        for g in range(GROUPS):
            total = held
            if g < HEADS:
                product = dot(conv_low[:, g * LANES : g * LANES + 256], gate_w[j, g])
                total = product[:, :LANES] if held is None else held + product[:, :LANES]
                held = product[:, LANES:]
            target[:, g * LANES : (g + 1) * LANES] = total

    def gate_chunk(i, carry):
        r, g = lax.rem(i, ROWS), lax.div(i, ROWS)
        at = pl.ds(pl.multiple_of(g * LANES, LANES), LANES)
        rows = pl.ds(pl.multiple_of(r * SPAN, SPAN), SPAN)
        gate_d = jax.nn.sigmoid(decay_g[rows, at] + vectors[5:6, at])
        gate_i = jax.nn.sigmoid(input_g[rows, at] + vectors[6:7, at])
        decay_g[rows, at] = gate_d
        input_g[rows, at] = gate_i
        decay_now = jnp.exp(gate_d * vectors[7:8, at])
        root = jnp.sqrt(jnp.maximum(1.0 - decay_now * decay_now, root_floor))
        fed = root * gate_i * conv_low[rows, at].astype(F32)
        place = offset + lax.broadcasted_iota(jnp.int32, (SPAN, LANES), 0)
        carried = jnp.where(place == doc_start[r], 0.0, decay_now)
        a, b, last_a, last_b = row_scan(carried, fed, False)
        cum_a[rows, at] = a
        loc_b[rows, at] = b
        put_pair(totals, at, r, last_a, last_b)
        return carry

    totals[...] = jnp.zeros_like(totals)
    lax.fori_loop(0, ROWS * GROUPS, gate_chunk, 0)
    keys = [links.go(totals, totals_in.at[p.s], p.seq_at(d)) for d in range(1, 8)]
    save(decay_g, decay_out)
    save(input_g, input_out)
    row = lax.broadcasted_iota(jnp.int32, (ROWS, CHAN), 0)
    kept = jnp.zeros((ROWS, CHAN), F32)
    for r in range(ROWS):
        kept = jnp.where(row == r, (1 - fresh_rows[r]).astype(F32), kept)
    state = init_state[...] * kept
    for d in range(1, 8):
        links.arrived(totals_in.at[p.seq_at(-d)["seq"]], keys[d - 1], p.seq_at(-d))
    totals_in[p.s] = totals[...]
    for source in range(7):
        both = totals_in[source]
        state = jnp.where(source < p.s, both[0:ROWS] * state + both[ROWS:], state)
    entering[0:ROWS, :] = state
    entering[ROWS:, :] = jnp.zeros((8 - ROWS, CHAN), F32)

    def state_chunk(i, carry):
        r, g = lax.rem(i, ROWS), lax.div(i, ROWS)
        at = pl.ds(pl.multiple_of(g * LANES, LANES), LANES)
        rows = pl.ds(pl.multiple_of(r * SPAN, SPAN), SPAN)
        value = loc_b[rows, at] + cum_a[rows, at] * take_row(entering, at, r)
        states[rows, at] = value
        mixed[rows, at] = (value * gelu(pre[rows, at])).astype(BF16)
        return carry

    lax.fori_loop(0, ROWS * GROUPS, state_chunk, 0)
    save(states, states_out)
    save(mixed, mixed_out)
    save(entering, entering_out)

    def partial(row):
        left = mixed[pl.ds(pl.multiple_of(row * SPAN, SPAN), SPAN), :]

        def one(n, carry):
            weights = mix_full[lax.div(n, 2), lax.rem(n, 2), :, :, 2 * CHAN :].reshape(256, CHAN)
            part[row, :, pl.ds(pl.multiple_of(n * 256, 256), 256)] = dot_nt(left, weights).astype(BF16)
            return carry

        lax.fori_loop(0, 8, one, 0)

    reduce = Reduce(links, p, part, far, near)
    partial(p.y2)
    reduce.send_far()
    partial(p.yr)
    partial(p.yl)
    reduce.send_near()
    partial(p.y)
    mlp_gather.middle()
    reduce.merge()
    reduce.settle()

    def norm_mid(k, carry):
        at = pl.ds(pl.multiple_of(k * 16, 16), 16)
        total = part[p.y, at, :].astype(F32) + near[0, at, :].astype(F32) + near[1, at, :].astype(F32)
        row = pl.ds(pl.multiple_of(p.y * SPAN + k * 16, 16), 16)
        stream = tokens[row, :].astype(F32) + total
        scale = lax.rsqrt(jnp.mean(stream * stream, axis=-1, keepdims=True) + epsilon)
        after_own[at, :] = stream
        normed_mid[p.y, at, :] = (stream * scale * gains[1:2, :]).astype(BF16)
        return carry

    lax.fori_loop(0, SPAN // 16, norm_mid, 0)
    spread = Spread(links, p, normed_mid)
    spread.start()
    spread.forward()
    mlp_gather.finish()
    spread.near()
    spread.far()
    mlp_gather.settle()
    for copy in saves:
        copy.wait()
    links.drain()


def params(collective_id):
    return pltpu.CompilerParams(
        collective_id=collective_id, has_side_effects=True, vmem_limit_bytes=VMEM_BYTES
    )


def vmem():
    return pl.BlockSpec(memory_space=pltpu.VMEM)


def smem():
    return pl.BlockSpec(memory_space=pltpu.SMEM)


def anyspace():
    return pl.BlockSpec(memory_space=pl.ANY)


def mix_forward(*operands):
    shape = jax.ShapeDtypeStruct
    tc = (TOKENS, CHAN)
    ext_shape = (ROWS, PAD + SPAN, CHAN)
    outs = [
        shape((4, 2, 4, 64, MIX_COLS), BF16),
        shape((4, 2, 4, 64, MLP_COLS), BF16),
        shape(tc, F32),
        shape(tc, F32),
        shape(ext_shape, F32),
        shape(tc, F32),
        shape(tc, F32),
        shape(tc, BF16),
        shape(tc, BF16),
        shape((TOKENS, WIDTH), BF16),
        shape((8, CHAN), F32),
        shape((8, CHAN), F32),
        shape((ROWS, SPAN, WIDTH), BF16),
        shape((SPAN, WIDTH), F32),
    ]
    scratch = [
        pltpu.VMEM((64, MLP_COLS), BF16),
        pltpu.VMEM((2, WIDTH), F32),
        pltpu.VMEM((8, CHAN), F32),
        pltpu.VMEM((4, 2, 4, 64, MIX_COLS), BF16),
        pltpu.VMEM((TOKENS, WIDTH), BF16),
        pltpu.VMEM((TOKENS, 2 * CHAN), F32),
        pltpu.VMEM(ext_shape, F32),
        pltpu.VMEM(tc, F32),
        pltpu.VMEM(tc, F32),
        pltpu.VMEM(tc, BF16),
        pltpu.VMEM(tc, F32),
        pltpu.VMEM(tc, F32),
        pltpu.VMEM(tc, F32),
        pltpu.VMEM(tc, BF16),
        pltpu.VMEM((ROWS, PAD, CHAN), F32),
        pltpu.VMEM((ROWS, PAD, CHAN), F32),
        pltpu.VMEM((8, CHAN), F32),
        pltpu.VMEM((8, 8, CHAN), F32),
        pltpu.VMEM((8, CHAN), F32),
        pltpu.VMEM((ROWS, SPAN, WIDTH), BF16),
        pltpu.VMEM((2, SPAN, HALF), BF16),
        pltpu.VMEM((2, SPAN, WIDTH), BF16),
        pltpu.SemaphoreType.DMA((16,)),
        pltpu.SemaphoreType.DMA((128,)),
        pltpu.SemaphoreType.DMA((128,)),
    ]
    return pl.pallas_call(
        mix_forward_kernel,
        out_shape=outs,
        in_specs=[vmem()] * 7 + [smem()] * 2 + [vmem()] * 6,
        out_specs=[anyspace()] * 12 + [vmem()] * 2,
        scratch_shapes=scratch,
        compiler_params=params(0),
        name="mix_forward",
    )(*operands)


def norm_back_rows(d_row, stream, gain_row):
    scale = lax.rsqrt(jnp.mean(stream * stream, axis=-1, keepdims=True) + epsilon)
    unit = stream * scale
    e = d_row * gain_row
    inner = jnp.mean(e * unit, axis=-1, keepdims=True)
    return scale * (e - unit * inner), d_row * unit


def own_sum(reduce, at):
    part, near = reduce.part, reduce.near
    return part[reduce.p.y, at, :].astype(F32) + near[0, at, :].astype(F32) + near[1, at, :].astype(F32)


def mid_back_kernel(
    part, after_own, upstream, gain_rows, d_after_low, d_after_own, gain_mid, far, near, send, recv
):
    p = Place()
    links = Links(send, recv)
    greet([p.YR, p.YL])
    reduce = Reduce(links, p, part, far, near)
    reduce.send_far()
    reduce.send_near()
    gain_mid[...] = jnp.zeros_like(gain_mid)
    gain = gain_rows[1:2, :].astype(F32)
    reduce.merge()
    reduce.settle()

    def one(k, carry):
        at = pl.ds(pl.multiple_of(k * 16, 16), 16)
        through, share = norm_back_rows(own_sum(reduce, at), after_own[at, :], gain)
        gain_mid[...] += share[0:8] + share[8:16]
        total = upstream[p.y, at, :].astype(F32) + through
        d_after_own[at, :] = total
        d_after_low[p.y, at, :] = total.astype(BF16)
        return carry

    lax.fori_loop(0, SPAN // 16, one, 0)
    spread = Spread(links, p, d_after_low)
    spread.start()
    spread.forward()
    spread.near()
    spread.far()
    links.drain()


def mid_back(part, after_own, upstream, gains):
    shape = jax.ShapeDtypeStruct
    return pl.pallas_call(
        mid_back_kernel,
        out_shape=[
            shape((ROWS, SPAN, WIDTH), BF16),
            shape((SPAN, WIDTH), F32),
            shape((8, WIDTH), F32),
        ],
        in_specs=[vmem()] * 4,
        out_specs=[vmem()] * 3,
        scratch_shapes=[
            pltpu.VMEM((2, SPAN, HALF), BF16),
            pltpu.VMEM((2, SPAN, WIDTH), BF16),
            pltpu.SemaphoreType.DMA((12,)),
            pltpu.SemaphoreType.DMA((12,)),
        ],
        compiler_params=params(1),
        name="mid_back",
    )(part, after_own, upstream, gains)


def mlp_kernel(
    normed, upstream, weights, mid_part, out_part, grads, normed_t, upstream_t, d_both, mid_sum, out_sum
):
    step = pl.program_id(0)

    @pl.when(step == 0)
    def _():
        def turn(n, carry):
            at = pl.ds(pl.multiple_of(n * 256, 256), 256)
            normed_t[at, :] = normed[:, at].T
            upstream_t[at, :] = upstream[:, at].T
            return carry

        lax.fori_loop(0, WIDTH // 256, turn, 0)
        mid_sum[...] = jnp.zeros_like(mid_sum)
        out_sum[...] = jnp.zeros_like(out_sum)

    gate = dot(normed[...], weights[:, 0:CHUNK])
    up = dot(normed[...], weights[:, CHUNK : 2 * CHUNK])
    d_hidden = dot(upstream[...], weights[:, 2 * CHUNK :])
    act, slope = gelu_pair(gate)
    hidden = (act * up).astype(BF16)
    d_both[:, 0:CHUNK] = (d_hidden * up * slope).astype(BF16)
    d_both[:, CHUNK : 2 * CHUNK] = (d_hidden * act).astype(BF16)
    d_both[:, 2 * CHUNK :] = hidden

    def tile(n, carry):
        at = pl.ds(pl.multiple_of(n * 256, 256), 256)
        grads[at, 0 : 2 * CHUNK] = dot(normed_t[at, :], d_both[:, 0 : 2 * CHUNK]).astype(BF16)
        grads[at, 2 * CHUNK :] = dot(upstream_t[at, :], d_both[:, 2 * CHUNK :]).astype(BF16)
        mid_sum[:, at] += dot_nt(d_both[:, 0 : 2 * CHUNK], weights[at, 0 : 2 * CHUNK])
        out_sum[:, at] += dot_nt(d_both[:, 2 * CHUNK :], weights[at, 2 * CHUNK :])
        return carry

    lax.fori_loop(0, WIDTH // 256, tile, 0)

    @pl.when(step == CHUNKS - 1)
    def _():
        mid_part[...] = mid_sum[...].astype(BF16)
        out_part[...] = out_sum[...].astype(BF16)


def mlp_all(normed, upstream, weights):
    shape = jax.ShapeDtypeStruct
    whole = pl.BlockSpec((TOKENS, WIDTH), lambda f: (0, 0))
    block = pl.BlockSpec((WIDTH, 3 * CHUNK), lambda f: (0, f))
    return pl.pallas_call(
        mlp_kernel,
        grid=(CHUNKS,),
        out_shape=[
            shape((TOKENS, WIDTH), BF16),
            shape((TOKENS, WIDTH), BF16),
            shape((WIDTH, MLP_COLS), BF16),
        ],
        in_specs=[whole, whole, block],
        out_specs=[whole, whole, block],
        scratch_shapes=[
            pltpu.VMEM((WIDTH, TOKENS), BF16),
            pltpu.VMEM((WIDTH, TOKENS), BF16),
            pltpu.VMEM((TOKENS, 3 * CHUNK), BF16),
            pltpu.VMEM((TOKENS, WIDTH), F32),
            pltpu.VMEM((TOKENS, WIDTH), F32),
        ],
        compiler_params=pltpu.CompilerParams(vmem_limit_bytes=VMEM_BYTES),
        cost_estimate=pl.CostEstimate(
            flops=18 * TOKENS * WIDTH * MLP, bytes_accessed=4 * WIDTH * MLP_COLS, transcendentals=TOKENS * MLP
        ),
        name="mlp_all",
    )(normed, upstream, weights)


class Scatter:
    def __init__(self, links, place, grads, sib, far, near, half_a, half_b, far_2, near_2):
        self.links, self.p = links, place
        self.grads, self.sib = grads, sib
        self.far, self.near, self.far_2, self.near_2 = far, near, far_2, near_2
        self.half_a, self.half_b = half_a, half_b
        self.sib_keys = {}

    def give(self, xx):
        p = self.p
        self.sib_keys[xx] = self.links.go(self.grads.at[xx, 1 - p.c], self.sib.at[xx], p.SIB)

    def take(self, xx):
        p, sib, grads = self.p, self.sib, self.grads
        self.links.arrived(sib.at[xx], self.sib_keys[xx], p.SIB)

        def one(j, carry):
            sib[xx, j] = (sib[xx, j].astype(F32) + grads[xx, p.c, j].astype(F32)).astype(BF16)
            return carry

        lax.fori_loop(0, 4, one, 0)

    def _ring(self, view, i, right, left, far, near, base):
        links = self.links
        ir, il, i2 = lax.rem(i + 1, 4), lax.rem(i + 3, 4), lax.rem(i + 2, 4)
        a, b = pl.ds(base, 16), pl.ds(base + 16, 16)
        na, nb = pl.ds(0, 16), pl.ds(16, 16)
        k0 = links.go(view(i2, a), far.at[0], right)
        k1 = links.go(view(i2, b), far.at[1], left)
        k2 = links.go(view(ir, b), near.at[0, :, nb], right)
        k3 = links.go(view(il, a), near.at[1, :, na], left)
        keys = []

        def merge():
            for way, k, row, at, source, target, to in (
                (0, k0, ir, a, left, right, na),
                (1, k1, il, b, right, left, nb),
            ):
                links.arrived(far.at[way], k, source)
                mine = view(row, at)

                def one(j, carry):
                    far[way, j] = (far[way, j].astype(F32) + mine[j].astype(F32)).astype(BF16)
                    return carry

                lax.fori_loop(0, far.shape[1], one, 0)
                keys.append(links.go(far.at[way], near.at[way, :, to], target))

        def settle():
            links.arrived(near.at[0, :, nb], k2, left)
            links.arrived(near.at[1, :, na], k3, right)
            links.arrived(near.at[0, :, na], keys[0], left)
            links.arrived(near.at[1, :, nb], keys[1], right)

        return merge, settle

    def first(self):
        p, sib = self.p, self.sib
        self.x_ring = self._ring(lambda j, r: sib.at[j, :, r], p.x, p.XR, p.XL, self.far.at[0], self.near.at[0], 0)
        self.z_ring = self._ring(lambda j, r: sib.at[:, j, r], p.z, p.ZR, p.ZL, self.far.at[1], self.near.at[1], 32)

    def merge(self):
        self.x_ring[0]()
        self.z_ring[0]()

    def turn(self):
        p, sib, near = self.p, self.sib, self.near
        self.x_ring[1]()

        def one_a(j, carry):
            total = sib[p.x, j, 0:32].astype(F32) + near[0, 0, j].astype(F32) + near[0, 1, j].astype(F32)
            self.half_a[j, 0] = total.astype(BF16)
            return carry

        lax.fori_loop(0, 4, one_a, 0)
        half_a, half_b = self.half_a, self.half_b
        self.ring_a = self._ring(
            lambda j, r: half_a.at[j, :, r], p.z, p.ZR, p.ZL, self.far_2.at[0], self.near_2.at[0], 0
        )
        self.z_ring[1]()

        def one_b(j, carry):
            total = sib[j, p.z, 32:64].astype(F32) + near[1, 0, j].astype(F32) + near[1, 1, j].astype(F32)
            self.half_b[j, 0] = total.astype(BF16)
            return carry

        lax.fori_loop(0, 4, one_b, 0)
        self.ring_b = self._ring(
            lambda j, r: half_b.at[j, :, r], p.x, p.XR, p.XL, self.far_2.at[1], self.near_2.at[1], 0
        )

    def merge_2(self):
        self.ring_a[0]()
        self.ring_b[0]()

    def finish(self, store):
        p, near = self.p, self.near_2
        self.ring_a[1]()
        store(0, self.half_a[p.z, 0].astype(F32) + near[0, 0, 0].astype(F32) + near[0, 1, 0].astype(F32))
        self.ring_b[1]()
        store(32, self.half_b[p.x, 0].astype(F32) + near[1, 0, 0].astype(F32) + near[1, 1, 0].astype(F32))

    @staticmethod
    def scratch(columns):
        return [
            pltpu.VMEM((4, 4, 64, columns), BF16),
            pltpu.VMEM((2, 2, 4, 16, columns), BF16),
            pltpu.VMEM((2, 2, 4, 32, columns), BF16),
            pltpu.VMEM((4, 1, 32, columns), BF16),
            pltpu.VMEM((4, 1, 32, columns), BF16),
            pltpu.VMEM((2, 2, 1, 16, columns), BF16),
            pltpu.VMEM((2, 2, 1, 32, columns), BF16),
        ]


def back_kernel(
    d_after_low,
    mix_full,
    states,
    pre,
    ext,
    decay_g,
    input_g,
    conv_low,
    entering,
    mixed,
    normed_in,
    out_part,
    tokens,
    after_own,
    d_after_own,
    gain_mid,
    gain_rows,
    vectors,
    gate_w,
    doc_start,
    grad_tokens,
    block_out,
    grad_mix,
    small_sums,
    block_sums,
    gain_sums,
    work,
    own_tokens,
    d_mixed,
    tail_a,
    d_gates,
    d_both,
    d_first,
    small,
    rim_send,
    rim_recv,
    totals,
    totals_in,
    after,
    far_a,
    near_a,
    far_b,
    near_b,
    sib,
    far_s,
    near_s,
    half_a,
    half_b,
    far_2,
    near_2,
    small_all,
    gain_in,
    gain_y,
    gain_s,
    gain_z,
    local,
    send,
    recv,
):
    p = Place()
    links = Links(send, recv)
    load = pltpu.make_async_copy(mix_full, work.at[:, :, :, :, pl.ds(0, MIX_COLS)], local.at[0])
    load.start()
    load_tokens = pltpu.make_async_copy(tokens.at[p.y], own_tokens, local.at[1])
    load_tokens.start()
    others_y = [{"tensor": lax.rem(p.y + d, 4)} for d in (1, 2, 3)]
    others_z = [{"dp": lax.rem(p.z + d, 4)} for d in (1, 2, 3)]
    greet([p.seq_at(d) for d in range(1, 8)] + others_y + others_z)
    ahead = Reduce(links, p, out_part, far_b, near_b)
    ahead.send_far()
    ahead.send_near()
    load.wait()
    rows_low = d_after_low.reshape(TOKENS, WIDTH)
    for start, size in ((0, 256), (256, 256), (512, 128)):
        weights = work[:, :, :, :, 2 * CHAN + start : 2 * CHAN + start + size].reshape(WIDTH, size)
        d_mixed[:, start : start + size] = dot(rows_low[...], weights)
    small[...] = jnp.zeros_like(small)
    totals[...] = jnp.zeros_like(totals)
    gain_in[...] = jnp.zeros_like(gain_in)
    offset = p.s * SPAN

    def chunk(i):
        r, g = lax.rem(i, ROWS), lax.div(i, ROWS)
        at = pl.ds(pl.multiple_of(g * LANES, LANES), LANES)
        rows = pl.ds(pl.multiple_of(r * SPAN, SPAN), SPAN)
        row = lax.broadcasted_iota(jnp.int32, (SPAN, LANES), 0)
        return r, g, at, rows, row

    def states_back(i, carry):
        r, g, at, rows, row = chunk(i)
        d_chunk = d_mixed[rows, at]
        value, slope = gelu_pair(pre[rows, at])
        d_both[rows, at] = (d_chunk * states[rows, at] * slope).astype(BF16)
        decay_now = jnp.exp(decay_g[rows, at] * vectors[7:8, at])
        carried = jnp.where(offset + row == doc_start[r], 0.0, decay_now)
        following = jnp.where(row == SPAN - 1, 1.0, pltpu.roll(carried, SPAN - 1, 0))
        a, b, first_a, first_b = row_scan(following, d_chunk * value, True)
        tail_a[rows, at] = a
        d_mixed[rows, at] = b
        put_pair(totals, at, r, carried[0:1] * first_a, carried[0:1] * first_b)
        return carry

    lax.fori_loop(0, ROWS * GROUPS, states_back, 0)
    keys = [links.go(totals, totals_in.at[p.s], p.seq_at(d)) for d in range(1, 8)]
    ahead.merge()
    state = jnp.zeros((ROWS, CHAN), F32)
    for d in range(1, 8):
        links.arrived(totals_in.at[p.seq_at(-d)["seq"]], keys[d - 1], p.seq_at(-d))
    totals_in[p.s] = totals[...]
    for source in range(7, 0, -1):
        both = totals_in[source]
        state = jnp.where(source > p.s, both[0:ROWS] * state + both[ROWS:], state)
    after[0:ROWS, :] = state
    after[ROWS:, :] = jnp.zeros((8 - ROWS, CHAN), F32)

    def gates_back(i, carry):
        r, g, at, rows, row = chunk(i)
        grads = d_mixed[rows, at] + tail_a[rows, at] * take_row(after, at, r)
        held = states[rows, at]
        previous = jnp.where(row == 0, take_row(entering, at, r), pltpu.roll(held, 1, 0))
        gate_d, gate_i = decay_g[rows, at], input_g[rows, at]
        rate = vectors[7:8, at]
        decay_now = jnp.exp(gate_d * rate)
        headroom = 1.0 - decay_now * decay_now
        root = jnp.sqrt(jnp.maximum(headroom, root_floor))
        conv = conv_low[rows, at].astype(F32)
        d_decay = jnp.where(offset + row == doc_start[r], 0.0, grads * previous) - jnp.where(
            headroom > root_floor, grads * gate_i * conv * decay_now / root, 0.0
        )
        d_log = d_decay * decay_now
        d_zero = d_log * rate * gate_d * (1.0 - gate_d)
        fed = grads * root
        d_one = fed * conv * gate_i * (1.0 - gate_i)
        d_gates[rows, pl.ds(pl.multiple_of(g * LANES, LANES), LANES)] = d_zero.astype(BF16)
        d_gates[rows, pl.ds(pl.multiple_of(CHAN + g * LANES, LANES), LANES)] = d_one.astype(BF16)
        tail_a[rows, at] = fed * gate_i
        small[5:6, at] += jnp.sum(d_zero, axis=0, keepdims=True)
        small[6:7, at] += jnp.sum(d_one, axis=0, keepdims=True)
        small[7:8, at] += jnp.sum(d_log * (-rate_scale * gate_d), axis=0, keepdims=True)
        return carry

    lax.fori_loop(0, ROWS * GROUPS, gates_back, 0)
    ahead.settle()

    def ahead_rows(k, carry):
        at = pl.ds(pl.multiple_of(k * 16, 16), 16)
        block_out[p.y, at, :] = (after_own[at, :] + own_sum(ahead, at)).astype(BF16)
        return carry

    lax.fori_loop(0, SPAN // 16, ahead_rows, 0)
    spread_b = Spread(links, p, block_out)
    spread_b.start()

    d_conv = tail_a
    held = None
    for g in range(GROUPS):
        total = d_conv[:, g * LANES : (g + 1) * LANES]
        if held is not None:
            total = total + held
        if g < HEADS:
            lo = g * LANES
            product = dot_nt(d_gates[:, lo : lo + 256], gate_w[0, g]) + dot_nt(
                d_gates[:, CHAN + lo : CHAN + lo + 256], gate_w[1, g]
            )
            total = total + product[:, :LANES]
            held = product[:, LANES:]
        d_conv[:, g * LANES : (g + 1) * LANES] = total

    body = d_mixed

    def conv_back(i, carry):
        r, g, at, rows, row = chunk(i)
        d_chunk = d_conv[rows, at]
        begin = doc_start[r]
        place = offset + row
        here = place >= begin
        head = jnp.zeros((8, LANES), F32)
        total = jnp.zeros((SPAN, LANES), F32)
        for k in range(CONV):
            before = CONV - 1 - k
            same = (place - before >= begin) == here
            kept = jnp.where(same, d_chunk, 0.0)
            value = ext[r, PAD - before : PAD - before + SPAN, at]
            small[k : k + 1, at] += jnp.sum(kept * value, axis=0, keepdims=True)
            term = kept * vectors[k : k + 1, at]
            if before:
                total = total + jnp.where(row < SPAN - before, pltpu.roll(term, SPAN - before, 0), 0.0)
                head = head + jnp.where(
                    row[0:8] >= 8 - before, pltpu.roll(term[0:8], 8 - before, 0), 0.0
                )
            else:
                total = total + term
        small[4:5, at] += jnp.sum(d_chunk, axis=0, keepdims=True)
        body[rows, at] = total
        rim_send[r, :, at] = head
        return carry

    lax.fori_loop(0, ROWS * GROUPS, conv_back, 0)
    k_rim = links.go(rim_send, rim_recv, p.seq_at(-1))
    spread_b.forward()
    links.arrived(rim_recv, k_rim, p.seq_at(1))
    for r in range(ROWS):
        last = r * SPAN + SPAN - 8
        body[last : last + 8, :] += jnp.where(p.s == 7, 0.0, rim_recv[r])
    for r in range(ROWS):
        d_both[r * SPAN : (r + 1) * SPAN, CHAN:] = body[r * SPAN : (r + 1) * SPAN, :].astype(BF16)

    def first_part(n, carry):
        weights = work[lax.div(n, 2), lax.rem(n, 2), :, :, 0 : 2 * CHAN].reshape(256, 2 * CHAN)
        product = dot_nt(d_both[...], weights).astype(BF16)
        d_first[:, :, pl.ds(pl.multiple_of(n * 256, 256), 256)] = product.reshape(ROWS, SPAN, 256)
        return carry

    lax.fori_loop(0, 8, first_part, 0)
    back = Reduce(links, p, d_first, far_a, near_a)
    back.send_far()
    back.send_near()

    def weight_grads(n):
        at = pl.ds(pl.multiple_of(n * 256, 256), 256)
        to = work.at[lax.div(n, 2), lax.rem(n, 2)]
        both = dot_tn(normed_in[:, at], d_both[...])
        to[:, :, 0 : 2 * CHAN] = both.astype(BF16).reshape(4, 64, 2 * CHAN)
        out = dot_tn(rows_low[:, at], mixed[...])
        to[:, :, 2 * CHAN : MIX_COLS] = out.astype(BF16).reshape(4, 64, CHAN)

    def blocks(j, h):
        lo = h * LANES
        product = dot_tn(conv_low[:, lo : lo + 256], d_gates[:, j * CHAN + lo : j * CHAN + lo + 256])
        for q in range(BLK // 32):
            row = (j * HEADS + h) * BLK + 32 * q
            n, inner = row // 64, row % 64
            piece = product[32 * (h + q) : 32 * (h + q + 1), :].astype(BF16)
            work[n // 8, (n // 4) % 2, n % 4, inner : inner + 32, MIX_COLS:] = piece

    for j in range(2):
        for h in range(HEADS):
            blocks(j, h)
    for n in range(20, 32):
        work[n // 8, (n // 4) % 2, n % 4, :, MIX_COLS:] = jnp.zeros((64, SMALL), BF16)
    for k, n in enumerate((20, 21, 22)):
        width = min(256, CHAN - 256 * k)
        both = jnp.concatenate([small[:, 256 * k : 256 * k + width], jnp.zeros((8, width), F32)], axis=0)
        work[n // 8, (n // 4) % 2, n % 4, 0:16, MIX_COLS : MIX_COLS + width] = both.astype(BF16)
    scatter = Scatter(links, p, work, sib, far_s, near_s, half_a, half_b, far_2, near_2)

    def give(xx, carry):
        weight_grads(xx * 2 + 1 - p.c)
        return carry

    def keep(xx, carry):
        weight_grads(xx * 2 + p.c)
        return carry

    lax.fori_loop(0, 4, give, 0)
    for xx in range(4):
        scatter.give(xx)
    back.merge()
    lax.fori_loop(0, 4, keep, 0)
    for xx in range(4):
        scatter.take(xx)
    scatter.first()
    back.settle()
    load_tokens.wait()
    gain = gain_rows[0:1, :].astype(F32)

    def back_rows(k, carry):
        at = pl.ds(pl.multiple_of(k * 16, 16), 16)
        through, share = norm_back_rows(own_sum(back, at), own_tokens[at, :].astype(F32), gain)
        gain_in[...] += share[0:8] + share[8:16]
        grad_tokens[p.y, at, :] = (d_after_own[at, :] + through).astype(BF16)
        return carry

    lax.fori_loop(0, SPAN // 16, back_rows, 0)
    spread_a = Spread(links, p, grad_tokens)
    spread_a.start()
    gain_y[p.y] = jnp.concatenate(
        [jnp.sum(gain_in[...], axis=0, keepdims=True), jnp.sum(gain_mid[...], axis=0, keepdims=True)], axis=0
    )
    y_keys = [links.go(gain_y.at[p.y], gain_y.at[p.y], device) for device in others_y]
    scatter.merge()
    for d in (1, 2, 3):
        links.arrived(gain_y.at[lax.rem(p.y + 4 - d, 4)], y_keys[d - 1], others_y[0])
    gain_z[p.z] = gain_y[0] + gain_y[1] + gain_y[2] + gain_y[3]
    z_keys = [links.go(gain_z.at[p.z], gain_z.at[p.z], device) for device in others_z]
    scatter.turn()
    for d in (1, 2, 3):
        links.arrived(gain_z.at[lax.rem(p.z + 4 - d, 4)], z_keys[d - 1], others_z[0])
    gain_s[p.s] = gain_z[0] + gain_z[1] + gain_z[2] + gain_z[3]
    s_keys = [links.go(gain_s.at[p.s], gain_s.at[p.s], p.seq_at(d)) for d in range(1, 8)]
    spread_a.forward()
    scatter.merge_2()
    for d in range(1, 8):
        links.arrived(gain_s.at[p.seq_at(-d)["seq"]], s_keys[d - 1], p.seq_at(-d))
    total = gain_s[0]
    for s in range(1, 8):
        total = total + gain_s[s]
    gain_sums[...] = total

    def store(base, value):
        grad_mix[base : base + 32, :] = value[:, :MIX_COLS]
        small_all[p.x, p.c, p.z, base : base + 32, :] = value[:, MIX_COLS:].astype(BF16)

    scatter.finish(store)
    small_gather = Gather(links, p, small_all)
    small_gather.first()
    spread_b.near()
    spread_b.far()
    small_gather.middle()
    small_gather.finish()
    small_gather.second()
    small_gather.middle()
    small_gather.finish()
    small_gather.settle()
    for k, n in enumerate((20, 21, 22)):
        width = min(256, CHAN - 256 * k)
        value = small_all[n // 8, (n // 4) % 2, n % 4, 0:16, 0:width].astype(F32)
        small_sums[:, 256 * k : 256 * k + width] = value[0:8]
    for n in range(20):
        value = small_all[n // 8, (n // 4) % 2, n % 4].astype(F32)
        block_sums[64 * n : 64 * (n + 1), :] = value
    spread_a.near()
    spread_a.far()
    links.drain()


def back_all(*operands):
    shape = jax.ShapeDtypeStruct
    tc = (TOKENS, CHAN)
    pair = [pltpu.VMEM((2, SPAN, HALF), BF16), pltpu.VMEM((2, SPAN, WIDTH), BF16)]
    return pl.pallas_call(
        back_kernel,
        out_shape=[
            shape((ROWS, SPAN, WIDTH), BF16),
            shape((ROWS, SPAN, WIDTH), BF16),
            shape((64, MIX_COLS), F32),
            shape((8, CHAN), F32),
            shape((2 * HEADS * BLK, 256), F32),
            shape((2, WIDTH), F32),
        ],
        in_specs=[vmem(), anyspace()] + [vmem()] * 10 + [anyspace()] + [vmem()] * 6 + [smem()],
        out_specs=[vmem()] * 6,
        scratch_shapes=[
            pltpu.VMEM((4, 2, 4, 64, RS_COLS), BF16),
            pltpu.VMEM((SPAN, WIDTH), BF16),
            pltpu.VMEM(tc, F32),
            pltpu.VMEM(tc, F32),
            pltpu.VMEM((TOKENS, 2 * CHAN), BF16),
            pltpu.VMEM((TOKENS, 2 * CHAN), BF16),
            pltpu.VMEM((ROWS, SPAN, WIDTH), BF16),
            pltpu.VMEM((8, CHAN), F32),
            pltpu.VMEM((ROWS, PAD, CHAN), F32),
            pltpu.VMEM((ROWS, PAD, CHAN), F32),
            pltpu.VMEM((8, CHAN), F32),
            pltpu.VMEM((8, 8, CHAN), F32),
            pltpu.VMEM((8, CHAN), F32),
        ]
        + pair * 2
        + Scatter.scratch(RS_COLS)
        + [
            pltpu.VMEM((4, 2, 4, 64, SMALL), BF16),
            pltpu.VMEM((8, WIDTH), F32),
            pltpu.VMEM((4, 2, WIDTH), F32),
            pltpu.VMEM((8, 2, WIDTH), F32),
            pltpu.VMEM((4, 2, WIDTH), F32),
            pltpu.SemaphoreType.DMA((2,)),
            pltpu.SemaphoreType.DMA((144,)),
            pltpu.SemaphoreType.DMA((144,)),
        ],
        compiler_params=params(2),
        name="back_all",
    )(*operands)


def per_device(
    tokens,
    init_state,
    conv_state,
    fresh_rows,
    doc_start,
    norm_gains,
    mix_in,
    mix_out,
    conv_weight,
    conv_bias,
    gate_blocks,
    gate_bias,
    decay_param,
    mlp_in,
    mlp_out,
    cotangent,
):
    gate_w = jnp.stack(
        [
            jnp.pad(gate_blocks[:, h], ((0, 0), (32 * h, 96 - 32 * h), (32 * h, 96 - 32 * h)))
            for h in range(HEADS)
        ],
        axis=1,
    )
    (
        mix_full,
        mlp_full,
        states,
        pre,
        ext,
        decay_g,
        input_g,
        conv_low,
        mixed,
        normed_in,
        entering,
        vectors,
        normed_mid,
        after_own,
    ) = mix_forward(
        tokens.reshape(TOKENS, WIDTH),
        mix_in,
        mix_out,
        mlp_in,
        mlp_out,
        init_state,
        conv_state,
        fresh_rows,
        doc_start,
        norm_gains,
        conv_weight,
        conv_bias[None],
        gate_bias,
        decay_param[None],
        gate_w,
    )
    mid_part, out_part, grad_mlp = mlp_all(
        normed_mid.reshape(TOKENS, WIDTH),
        cotangent.reshape(TOKENS, WIDTH),
        mlp_full.reshape(WIDTH, MLP_COLS),
    )
    grad_mlp = lax.psum_scatter(grad_mlp, ("seq", "dp"), scatter_dimension=0, tiled=True)
    d_after_low, d_after_own, gain_mid = mid_back(
        mid_part.reshape(ROWS, SPAN, WIDTH), after_own, cotangent, norm_gains
    )
    grad_tokens, block_out, grad_mix, small, blocks, grad_gains = back_all(
        d_after_low,
        mix_full,
        states,
        pre,
        ext,
        decay_g,
        input_g,
        conv_low,
        entering,
        mixed,
        normed_in,
        out_part.reshape(ROWS, SPAN, WIDTH),
        tokens,
        after_own,
        d_after_own,
        gain_mid,
        norm_gains,
        vectors,
        gate_w,
        doc_start,
    )
    blocks = blocks.reshape(2, HEADS, BLK, 256)
    blocks = jnp.stack([blocks[:, h, :, 32 * h : 32 * h + BLK] for h in range(HEADS)], axis=1)
    grad_mlp = grad_mlp.astype(F32).reshape(64, CHUNKS, 3, CHUNK)
    return (
        block_out,
        states.reshape(ROWS, SPAN, CHAN),
        grad_tokens,
        grad_gains,
        jnp.stack([grad_mix[:, :CHAN], grad_mix[:, CHAN : 2 * CHAN]]),
        grad_mix[:, 2 * CHAN :].T,
        small[0:4],
        small[4],
        blocks,
        small[5:7],
        small[7] * jax.nn.sigmoid(decay_param.astype(F32)),
        grad_mlp[:, :, 0:2].transpose(2, 0, 1, 3).reshape(2, 64, MLP),
        grad_mlp[:, :, 2].transpose(1, 2, 0).reshape(MLP, 64),
    )


def solution(mesh):
    in_specs = (
        P("dp", "seq", None),
        P("dp", "tensor"),
        P("dp", None, "tensor"),
        P("dp"),
        P("dp"),
        P(),
        P(None, ("seq", "dp"), "tensor"),
        P("tensor", ("seq", "dp")),
        P(None, "tensor"),
        P("tensor"),
        P(None, "tensor", None, None),
        P(None, "tensor"),
        P("tensor"),
        P(None, ("seq", "dp"), "tensor"),
        P("tensor", ("seq", "dp")),
        P("dp", "seq", None),
    )
    out_specs = (
        P("dp", "seq", None),
        P("dp", "seq", "tensor"),
        P("dp", "seq", None),
        P(),
        P(None, ("seq", "dp"), "tensor"),
        P("tensor", ("seq", "dp")),
        P(None, "tensor"),
        P("tensor"),
        P(None, "tensor", None, None),
        P(None, "tensor"),
        P("tensor"),
        P(None, ("seq", "dp"), "tensor"),
        P("tensor", ("seq", "dp")),
    )
    return jax.shard_map(
        per_device, mesh=mesh, in_specs=in_specs, out_specs=out_specs, check_vma=False
    )
```

```python
import functools

import jax
import jax.numpy as jnp
from jax import lax
from jax.experimental import pallas as pl
from jax.experimental.pallas import tpu as pltpu
from jax.sharding import PartitionSpec as P

MESH = pl.DeviceIdType.MESH
F32 = jnp.float32
BF16 = jnp.bfloat16
VMEM_BYTES = 60 * 2**20

CONV = 4
ROWS = 4
SPAN = 128
TOKENS = ROWS * SPAN
WIDTH = 2048
CHAN = 640
HEADS = 4
BLK = 160
MLP = 1536
MIX_COLS = 3 * CHAN
MLP_COLS = 3 * MLP
CHUNK = 256
CHUNKS = MLP // CHUNK
SMALL = 256
LANES = 128
GROUPS = CHAN // LANES
PAD = 8

epsilon = 1e-06
root_floor = 0.001
rate_scale = 8.0


class Place:
    def __init__(self):
        self.s = lax.axis_index("seq")
        self.z = lax.axis_index("dp")
        self.y = lax.axis_index("tensor")
        self.x, self.c = lax.div(self.s, 2), lax.rem(self.s, 2)
        x, c, z, y = self.x, self.c, self.z, self.y
        self.xr, self.xl = lax.rem(x + 1, 4), lax.rem(x + 3, 4)
        self.zr, self.zl = lax.rem(z + 1, 4), lax.rem(z + 3, 4)
        self.yr, self.yl, self.y2 = lax.rem(y + 1, 4), lax.rem(y + 3, 4), lax.rem(y + 2, 4)
        self.XR, self.XL = {"seq": self.xr * 2 + c}, {"seq": self.xl * 2 + c}
        self.ZR, self.ZL = {"dp": self.zr}, {"dp": self.zl}
        self.YR, self.YL = {"tensor": self.yr}, {"tensor": self.yl}
        self.SIB = {"seq": x * 2 + 1 - c}

    def seq_at(self, distance):
        return {"seq": lax.rem(self.s + distance + 8, 8)}


def greet(devices):
    barrier = pltpu.get_barrier_semaphore()
    for device in devices:
        pl.semaphore_signal(barrier, inc=1, device_id=device, device_id_type=MESH)
    pl.semaphore_wait(barrier, len(devices))


class Links:
    def __init__(self, send, recv):
        self.send, self.recv = send, recv
        self.count = 0
        self.started = []

    def go(self, src, dst, device):
        k = self.count
        self.count += 1
        copy = pltpu.make_async_remote_copy(
            src_ref=src,
            dst_ref=dst,
            send_sem=self.send.at[k],
            recv_sem=self.recv.at[k],
            device_id=device,
            device_id_type=MESH,
        )
        copy.start()
        self.started.append(copy)
        return k

    def arrived(self, view, k, device):
        pltpu.make_async_remote_copy(
            src_ref=view,
            dst_ref=view,
            send_sem=self.send.at[k],
            recv_sem=self.recv.at[k],
            device_id=device,
            device_id_type=MESH,
        ).wait_recv()

    def drain(self):
        for copy in self.started:
            copy.wait_send()
        self.started = []


class Gather:
    def __init__(self, links, place, out):
        self.links, self.p, self.out = links, place, out
        self.to_sibling = []

    def _pass_on(self, view_of):
        k = self.links.go(view_of(self.p.c), view_of(self.p.c), self.p.SIB)
        self.to_sibling.append((view_of, k))

    def _ring(self, blk, i, right, left, base):
        links, p = self.links, self.p
        c = p.c
        ir, il, i2 = lax.rem(i + 1, 4), lax.rem(i + 3, 4), lax.rem(i + 2, 4)
        a, b = pl.ds(base, 16), pl.ds(base + 16, 16)
        k0 = links.go(blk(c, i, a), blk(c, i, a), right)
        k1 = links.go(blk(c, i, b), blk(c, i, b), left)
        k2 = links.go(blk(c, i, b), blk(c, i, b), right)
        k3 = links.go(blk(c, i, a), blk(c, i, a), left)

        def middle():
            links.arrived(blk(c, il, a), k0, left)
            k4 = links.go(blk(c, il, a), blk(c, il, a), right)
            links.arrived(blk(c, ir, b), k1, right)
            k5 = links.go(blk(c, ir, b), blk(c, ir, b), left)
            self._pass_on(lambda cc: blk(cc, il, a))
            self._pass_on(lambda cc: blk(cc, ir, b))
            return k4, k5

        def finish(later):
            for view, k, source in (
                (lambda cc: blk(cc, il, b), k2, left),
                (lambda cc: blk(cc, ir, a), k3, right),
                (lambda cc: blk(cc, i2, a), later[0], left),
                (lambda cc: blk(cc, i2, b), later[1], right),
            ):
                links.arrived(view(c), k, source)
                self._pass_on(view)

        return middle, finish

    def first(self):
        p, out = self.p, self.out
        self.x_ring = self._ring(lambda cc, j, r: out.at[j, cc, p.z, r], p.x, p.XR, p.XL, 0)
        self.z_ring = self._ring(lambda cc, j, r: out.at[p.x, cc, j, r], p.z, p.ZR, p.ZL, 32)
        self._pass_on(lambda cc: out.at[p.x, cc, p.z])

    def second(self):
        p, out = self.p, self.out
        self.x_ring = self._ring(lambda cc, j, r: out.at[:, cc, j, r], p.z, p.ZR, p.ZL, 0)
        self.z_ring = self._ring(lambda cc, j, r: out.at[j, cc, :, r], p.x, p.XR, p.XL, 32)

    def middle(self):
        self.later = (self.x_ring[0](), self.z_ring[0]())

    def finish(self):
        self.x_ring[1](self.later[0])
        self.z_ring[1](self.later[1])

    def settle(self):
        for view_of, k in self.to_sibling:
            self.links.arrived(view_of(1 - self.p.c), k, self.p.SIB)


CA, CB = pl.ds(0, WIDTH // 2), pl.ds(WIDTH // 2, WIDTH // 2)
HALF = WIDTH // 2


class Reduce:
    def __init__(self, links, place, part, far, near):
        self.links, self.p, self.part, self.far, self.near = links, place, part, far, near

    def send_first(self):
        p, part, near = self.p, self.part, self.near
        self.k0 = self.links.go(part.at[p.y2, :, CA], self.far.at[0], p.YR)
        self.k3 = self.links.go(part.at[p.yl, :, CA], near.at[1, :, CA], p.YL)

    def send_second(self):
        p, part, near = self.p, self.part, self.near
        self.k1 = self.links.go(part.at[p.y2, :, CB], self.far.at[1], p.YL)
        self.k2 = self.links.go(part.at[p.yr, :, CB], near.at[0, :, CB], p.YR)

    def merge(self):
        p, part, near, far = self.p, self.part, self.near, self.far
        self.links.arrived(far.at[0], self.k0, p.YL)
        far[0] = (far[0].astype(F32) + part[p.yr, :, 0:HALF].astype(F32)).astype(BF16)
        self.k4 = self.links.go(far.at[0], near.at[0, :, CA], p.YR)
        self.links.arrived(far.at[1], self.k1, p.YR)
        far[1] = (far[1].astype(F32) + part[p.yl, :, HALF:WIDTH].astype(F32)).astype(BF16)
        self.k5 = self.links.go(far.at[1], near.at[1, :, CB], p.YL)

    def settle(self):
        p, near = self.p, self.near
        self.links.arrived(near.at[0, :, CB], self.k2, p.YL)
        self.links.arrived(near.at[1, :, CA], self.k3, p.YR)
        self.links.arrived(near.at[0, :, CA], self.k4, p.YL)
        self.links.arrived(near.at[1, :, CB], self.k5, p.YR)


class Spread:
    def __init__(self, links, place, out):
        self.links, self.p, self.out = links, place, out

    def start(self):
        go, out, y, p = self.links.go, self.out, self.p.y, self.p
        self.k0 = go(out.at[y, :, CA], out.at[y, :, CA], p.YR)
        self.k1 = go(out.at[y, :, CB], out.at[y, :, CB], p.YL)
        self.k2 = go(out.at[y, :, CB], out.at[y, :, CB], p.YR)
        self.k3 = go(out.at[y, :, CA], out.at[y, :, CA], p.YL)

    def forward(self):
        go, out, p, arrived = self.links.go, self.out, self.p, self.links.arrived
        arrived(out.at[p.yl, :, CA], self.k0, p.YL)
        self.k4 = go(out.at[p.yl, :, CA], out.at[p.yl, :, CA], p.YR)
        arrived(out.at[p.yr, :, CB], self.k1, p.YR)
        self.k5 = go(out.at[p.yr, :, CB], out.at[p.yr, :, CB], p.YL)

    def near(self):
        out, p, arrived = self.out, self.p, self.links.arrived
        arrived(out.at[p.yl, :, CB], self.k2, p.YL)
        arrived(out.at[p.yr, :, CA], self.k3, p.YR)

    def far(self):
        out, p, arrived = self.out, self.p, self.links.arrived
        arrived(out.at[p.y2, :, CA], self.k4, p.YL)
        arrived(out.at[p.y2, :, CB], self.k5, p.YR)


def dot(a, b):
    return jnp.dot(a, b, preferred_element_type=F32)


def dot_nt(a, b):
    return lax.dot_general(a, b, (((1,), (1,)), ((), ())), preferred_element_type=F32)


def dot_tn(a, b):
    return lax.dot_general(a, b, (((0,), (0,)), ((), ())), preferred_element_type=F32)


GELU_C = 0.7978845608028654
GELU_A = 0.044715


def gelu(v):
    return 0.5 * v * (1.0 + jnp.tanh(GELU_C * (v + GELU_A * v * v * v)))


def gelu_pair(v):
    t = jnp.tanh(GELU_C * (v + GELU_A * v * v * v))
    value = 0.5 * v * (1.0 + t)
    slope = 0.5 * (1.0 + t) + 0.5 * v * (1.0 - t * t) * (GELU_C * (1.0 + 3.0 * GELU_A * v * v))
    return value, slope


def tile_scan(a, b, reverse):
    row = lax.broadcasted_iota(jnp.int32, a.shape, 1)
    for step in (1, 2, 4):
        if reverse:
            shift, valid = 8 - step, row < 8 - step
        else:
            shift, valid = step, row >= step
        a_near, b_near = pltpu.roll(a, shift, 1), pltpu.roll(b, shift, 1)
        b = jnp.where(valid, a * b_near + b, b)
        a = jnp.where(valid, a * a_near, a)
    return a, b


def row_scan(a, b, reverse):
    tiles = SPAN // 8
    a, b = tile_scan(a.reshape(tiles, 8, LANES), b.reshape(tiles, 8, LANES), reverse)
    edge = 0 if reverse else 7
    order = range(tiles - 1, -1, -1) if reverse else range(tiles)
    out_a, out_b = [None] * tiles, [None] * tiles
    carry_a = carry_b = None
    for k in order:
        ak, bk = a[k], b[k]
        if carry_a is not None:
            bk = ak * carry_b + bk
            ak = ak * carry_a
        out_a[k], out_b[k] = ak, bk
        carry_a, carry_b = ak[edge : edge + 1], bk[edge : edge + 1]
    return jnp.concatenate(out_a, axis=0), jnp.concatenate(out_b, axis=0), carry_a, carry_b


def put_pair(ref, at, r, first, second):
    row = lax.broadcasted_iota(jnp.int32, (8, LANES), 0)
    ref[:, at] = jnp.where(row == r, first, jnp.where(row == ROWS + r, second, ref[:, at]))


def take_row(ref, at, r):
    row = lax.broadcasted_iota(jnp.int32, (8, LANES), 0)
    return jnp.sum(jnp.where(row == r, ref[:, at], 0.0), axis=0, keepdims=True)


def assemble_vectors(vectors, raw):
    value = raw[...].astype(F32)
    row = lax.broadcasted_iota(jnp.int32, value.shape, 0)
    vectors[...] = jnp.where(row == 7, -rate_scale * jnp.log1p(jnp.exp(jnp.where(row == 7, value, 0.0))), value)


def mix_forward_kernel(
    tokens,
    mix_in,
    mix_out,
    mlp_in,
    mlp_out,
    init_state,
    conv_state,
    fresh_rows,
    doc_start,
    gain_rows,
    raw_vectors,
    gate_w,
    mix_full_out,
    mlp_full,
    states_out,
    pre_out,
    ext_out,
    decay_out,
    input_out,
    conv_out,
    mixed_out,
    normed_in_out,
    entering_out,
    vectors_out,
    normed_mid,
    after_own,
    mlp_own,
    gains,
    vectors,
    mix_full,
    normed_in,
    pre,
    ext,
    decay_g,
    input_g,
    conv_low,
    cum_a,
    loc_b,
    states,
    mixed,
    rim_send,
    rim_recv,
    totals,
    totals_in,
    entering,
    part,
    far,
    near,
    local,
    send,
    recv,
):
    p = Place()
    links = Links(send, recv)
    mine = mix_full.at[p.x, p.c, p.z]
    for j in range(2):
        mine[:, j * CHAN : (j + 1) * CHAN] = mix_in[j]
    mine[:, 2 * CHAN :] = mix_out[...]
    greet([p.seq_at(d) for d in range(1, 8)] + [p.ZR, p.ZL, p.YR, p.YL])
    in_gather = Gather(links, p, mix_full.at[:, :, :, :, pl.ds(0, 2 * CHAN)])
    out_gather = Gather(links, p, mix_full.at[:, :, :, :, pl.ds(2 * CHAN, CHAN)])
    mlp_gather = Gather(links, p, mlp_full)
    in_gather.first()
    for f in range(CHUNKS):
        lo, to = f * CHUNK, 3 * f * CHUNK
        mlp_own[:, to : to + CHUNK] = mlp_in[0, :, lo : lo + CHUNK]
        mlp_own[:, to + CHUNK : to + 2 * CHUNK] = mlp_in[1, :, lo : lo + CHUNK]
        mlp_own[:, to + 2 * CHUNK : to + 3 * CHUNK] = mlp_out[:, lo : lo + CHUNK]
    own_mlp = pltpu.make_async_copy(mlp_own, mlp_full.at[p.x, p.c, p.z], local.at[0])
    own_mlp.start()
    gains[...] = gain_rows[...].astype(F32)
    assemble_vectors(vectors, raw_vectors)

    def norm_rows(first, last):
        def one(k, carry):
            at = pl.ds(pl.multiple_of(k * 32, 32), 32)
            stream = tokens[at, :].astype(F32)
            scale = lax.rsqrt(jnp.mean(stream * stream, axis=-1, keepdims=True) + epsilon)
            normed_in[at, :] = (stream * scale * gains[0:1, :]).astype(BF16)
            return carry

        lax.fori_loop(first, last, one, 0)

    norm_rows(0, 8)
    in_gather.middle()
    in_gather.finish()
    in_gather.second()
    own_mlp.wait()
    norm_rows(8, 16)
    in_gather.middle()
    out_gather.first()
    mlp_gather.first()
    in_gather.finish()
    out_gather.middle()
    out_gather.finish()
    out_gather.second()
    mlp_gather.middle()
    mlp_gather.finish()
    mlp_gather.second()
    in_gather.settle()
    saves = []

    def save(src, dst):
        copy = pltpu.make_async_copy(src, dst, local.at[2 + len(saves)])
        copy.start()
        saves.append(copy)

    save(normed_in, normed_in_out)
    save(vectors, vectors_out)

    def project(n, carry):
        at = pl.ds(pl.multiple_of(n * 256, 256), 256)
        pre[:, at] = dot(normed_in[...], mix_full[:, :, :, :, at].reshape(WIDTH, 256))
        return carry

    lax.fori_loop(2, 5, project, 0)
    for r in range(ROWS):
        ext[r, PAD:, :] = pre[r * SPAN : (r + 1) * SPAN, CHAN : 2 * CHAN].astype(BF16).astype(F32)
        rim_send[r] = ext[r, SPAN : SPAN + PAD, :]
    k_rim = links.go(rim_send, rim_recv, p.seq_at(1))
    lax.fori_loop(0, 2, project, 0)
    save(pre.at[:, pl.ds(0, CHAN)], pre_out)
    links.arrived(rim_recv, k_rim, p.seq_at(-1))
    at_start = p.s == 0
    for r in range(ROWS):
        keep = (1 - fresh_rows[r]).astype(F32)
        ext[r, 0:PAD, :] = jnp.where(at_start, 0.0, rim_recv[r])
        for j in range(CONV - 1):
            at = slice(PAD - 3 + j, PAD - 2 + j)
            first_rim = conv_state[j, r : r + 1, :].astype(F32) * keep
            ext[r, at, :] = jnp.where(at_start, first_rim, rim_recv[r, at, :])
    offset = p.s * SPAN

    def conv_chunk(i, carry):
        r, g = lax.rem(i, ROWS), lax.div(i, ROWS)
        at = pl.ds(pl.multiple_of(g * LANES, LANES), LANES)
        place = offset + lax.broadcasted_iota(jnp.int32, (SPAN, LANES), 0)
        begin = doc_start[r]
        here = place >= begin
        total = jnp.zeros((SPAN, LANES), F32) + vectors[4:5, at]
        for k in range(CONV):
            value = ext[r, PAD - 3 + k : PAD - 3 + k + SPAN, at]
            same = (place - (3 - k) >= begin) == here
            total = total + vectors[k : k + 1, at] * jnp.where(same, value, 0.0)
        rows = pl.ds(pl.multiple_of(r * SPAN, SPAN), SPAN)
        conv_low[rows, at] = total.astype(BF16)
        return carry

    lax.fori_loop(0, ROWS * GROUPS, conv_chunk, 0)
    save(ext, ext_out)
    save(conv_low, conv_out)

    for j, target in ((0, decay_g), (1, input_g)):
        held = None
        for g in range(GROUPS):
            total = held
            if g < HEADS:
                product = dot(conv_low[:, g * LANES : g * LANES + 256], gate_w[j, g])
                total = product[:, :LANES] if held is None else held + product[:, :LANES]
                held = product[:, LANES:]
            target[:, g * LANES : (g + 1) * LANES] = total

    def gate_chunk(i, carry):
        r, g = lax.rem(i, ROWS), lax.div(i, ROWS)
        at = pl.ds(pl.multiple_of(g * LANES, LANES), LANES)
        rows = pl.ds(pl.multiple_of(r * SPAN, SPAN), SPAN)
        gate_d = jax.nn.sigmoid(decay_g[rows, at] + vectors[5:6, at])
        gate_i = jax.nn.sigmoid(input_g[rows, at] + vectors[6:7, at])
        decay_g[rows, at] = gate_d
        input_g[rows, at] = gate_i
        decay_now = jnp.exp(gate_d * vectors[7:8, at])
        root = jnp.sqrt(jnp.maximum(1.0 - decay_now * decay_now, root_floor))
        fed = root * gate_i * conv_low[rows, at].astype(F32)
        place = offset + lax.broadcasted_iota(jnp.int32, (SPAN, LANES), 0)
        carried = jnp.where(place == doc_start[r], 0.0, decay_now)
        a, b, last_a, last_b = row_scan(carried, fed, False)
        cum_a[rows, at] = a
        loc_b[rows, at] = b
        put_pair(totals, at, r, last_a, last_b)
        return carry

    totals[...] = jnp.zeros_like(totals)
    lax.fori_loop(0, ROWS * GROUPS, gate_chunk, 0)
    keys = [links.go(totals, totals_in.at[p.s], p.seq_at(d)) for d in range(1, 8)]
    save(decay_g, decay_out)
    save(input_g, input_out)
    out_gather.middle()
    out_gather.finish()
    row = lax.broadcasted_iota(jnp.int32, (ROWS, CHAN), 0)
    kept = jnp.zeros((ROWS, CHAN), F32)
    for r in range(ROWS):
        kept = jnp.where(row == r, (1 - fresh_rows[r]).astype(F32), kept)
    state = init_state[...] * kept
    for d in range(1, 8):
        links.arrived(totals_in.at[p.seq_at(-d)["seq"]], keys[d - 1], p.seq_at(-d))
    totals_in[p.s] = totals[...]
    for source in range(7):
        both = totals_in[source]
        state = jnp.where(source < p.s, both[0:ROWS] * state + both[ROWS:], state)
    entering[0:ROWS, :] = state
    entering[ROWS:, :] = jnp.zeros((8 - ROWS, CHAN), F32)

    def state_chunk(i, carry):
        r, g = lax.rem(i, ROWS), lax.div(i, ROWS)
        at = pl.ds(pl.multiple_of(g * LANES, LANES), LANES)
        rows = pl.ds(pl.multiple_of(r * SPAN, SPAN), SPAN)
        value = loc_b[rows, at] + cum_a[rows, at] * take_row(entering, at, r)
        states[rows, at] = value
        mixed[rows, at] = (value * gelu(pre[rows, at])).astype(BF16)
        return carry

    lax.fori_loop(0, ROWS * GROUPS, state_chunk, 0)
    save(states, states_out)
    save(mixed, mixed_out)
    save(entering, entering_out)

    out_gather.settle()
    save(mix_full, mix_full_out)

    def partial(n, carry):
        weights = mix_full[lax.div(n, 2), lax.rem(n, 2), :, :, 2 * CHAN :].reshape(256, CHAN)
        product = dot_nt(mixed[...], weights).astype(BF16)
        part[:, :, pl.ds(pl.multiple_of(n * 256, 256), 256)] = product.reshape(ROWS, SPAN, 256)
        return carry

    reduce = Reduce(links, p, part, far, near)
    lax.fori_loop(0, 4, partial, 0)
    reduce.send_first()
    lax.fori_loop(4, 8, partial, 0)
    reduce.send_second()
    mlp_gather.middle()
    reduce.merge()
    reduce.settle()

    def norm_mid(k, carry):
        at = pl.ds(pl.multiple_of(k * 16, 16), 16)
        total = part[p.y, at, :].astype(F32) + near[0, at, :].astype(F32) + near[1, at, :].astype(F32)
        row = pl.ds(pl.multiple_of(p.y * SPAN + k * 16, 16), 16)
        stream = tokens[row, :].astype(F32) + total
        scale = lax.rsqrt(jnp.mean(stream * stream, axis=-1, keepdims=True) + epsilon)
        after_own[at, :] = stream
        normed_mid[p.y, at, :] = (stream * scale * gains[1:2, :]).astype(BF16)
        return carry

    lax.fori_loop(0, SPAN // 16, norm_mid, 0)
    spread = Spread(links, p, normed_mid)
    spread.start()
    mlp_gather.finish()
    spread.forward()
    spread.near()
    spread.far()
    mlp_gather.settle()
    for copy in saves:
        copy.wait()
    links.drain()


def params(collective_id):
    return pltpu.CompilerParams(
        collective_id=collective_id, has_side_effects=True, vmem_limit_bytes=VMEM_BYTES
    )


def vmem():
    return pl.BlockSpec(memory_space=pltpu.VMEM)


def smem():
    return pl.BlockSpec(memory_space=pltpu.SMEM)


def anyspace():
    return pl.BlockSpec(memory_space=pl.ANY)


def mix_forward(*operands):
    shape = jax.ShapeDtypeStruct
    tc = (TOKENS, CHAN)
    ext_shape = (ROWS, PAD + SPAN, CHAN)
    outs = [
        shape((4, 2, 4, 64, MIX_COLS), BF16),
        shape((4, 2, 4, 64, MLP_COLS), BF16),
        shape(tc, F32),
        shape(tc, F32),
        shape(ext_shape, F32),
        shape(tc, F32),
        shape(tc, F32),
        shape(tc, BF16),
        shape(tc, BF16),
        shape((TOKENS, WIDTH), BF16),
        shape((8, CHAN), F32),
        shape((8, CHAN), F32),
        shape((ROWS, SPAN, WIDTH), BF16),
        shape((SPAN, WIDTH), F32),
    ]
    scratch = [
        pltpu.VMEM((64, MLP_COLS), BF16),
        pltpu.VMEM((2, WIDTH), F32),
        pltpu.VMEM((8, CHAN), F32),
        pltpu.VMEM((4, 2, 4, 64, MIX_COLS), BF16),
        pltpu.VMEM((TOKENS, WIDTH), BF16),
        pltpu.VMEM((TOKENS, 2 * CHAN), F32),
        pltpu.VMEM(ext_shape, F32),
        pltpu.VMEM(tc, F32),
        pltpu.VMEM(tc, F32),
        pltpu.VMEM(tc, BF16),
        pltpu.VMEM(tc, F32),
        pltpu.VMEM(tc, F32),
        pltpu.VMEM(tc, F32),
        pltpu.VMEM(tc, BF16),
        pltpu.VMEM((ROWS, PAD, CHAN), F32),
        pltpu.VMEM((ROWS, PAD, CHAN), F32),
        pltpu.VMEM((8, CHAN), F32),
        pltpu.VMEM((8, 8, CHAN), F32),
        pltpu.VMEM((8, CHAN), F32),
        pltpu.VMEM((ROWS, SPAN, WIDTH), BF16),
        pltpu.VMEM((2, SPAN, HALF), BF16),
        pltpu.VMEM((2, SPAN, WIDTH), BF16),
        pltpu.SemaphoreType.DMA((16,)),
        pltpu.SemaphoreType.DMA((184,)),
        pltpu.SemaphoreType.DMA((184,)),
    ]
    return pl.pallas_call(
        mix_forward_kernel,
        out_shape=outs,
        in_specs=[vmem()] * 7 + [smem()] * 2 + [vmem()] * 3,
        out_specs=[anyspace()] * 12 + [vmem()] * 2,
        scratch_shapes=scratch,
        compiler_params=params(0),
        name="mix_forward",
    )(*operands)


def norm_back_rows(d_row, stream, gain_row):
    scale = lax.rsqrt(jnp.mean(stream * stream, axis=-1, keepdims=True) + epsilon)
    unit = stream * scale
    e = d_row * gain_row
    inner = jnp.mean(e * unit, axis=-1, keepdims=True)
    return scale * (e - unit * inner), d_row * unit


def own_sum(reduce, at):
    part, near = reduce.part, reduce.near
    return part[reduce.p.y, at, :].astype(F32) + near[0, at, :].astype(F32) + near[1, at, :].astype(F32)


def mlp_kernel(
    normed, upstream, weights, mid_part, hidden_out, grads, normed_t, upstream_t, d_both, mid_sum
):
    step = pl.program_id(0)

    @pl.when(step == 0)
    def _():
        def turn(n, carry):
            at = pl.ds(pl.multiple_of(n * 256, 256), 256)
            normed_t[at, :] = normed[:, at].T
            upstream_t[at, :] = upstream[:, at].T
            return carry

        lax.fori_loop(0, WIDTH // 256, turn, 0)
        mid_sum[...] = jnp.zeros_like(mid_sum)

    gate = dot(normed[...], weights[:, 0:CHUNK])
    up = dot(normed[...], weights[:, CHUNK : 2 * CHUNK])
    d_hidden = dot(upstream[...], weights[:, 2 * CHUNK :])
    act, slope = gelu_pair(gate)
    hidden = (act * up).astype(BF16)
    d_both[:, 0:CHUNK] = (d_hidden * up * slope).astype(BF16)
    d_both[:, CHUNK : 2 * CHUNK] = (d_hidden * act).astype(BF16)
    d_both[:, 2 * CHUNK :] = hidden
    hidden_out[...] = hidden

    def tile(n, carry):
        at = pl.ds(pl.multiple_of(n * 256, 256), 256)
        grads[at, 0 : 2 * CHUNK] = dot(normed_t[at, :], d_both[:, 0 : 2 * CHUNK]).astype(BF16)
        grads[at, 2 * CHUNK :] = dot(upstream_t[at, :], d_both[:, 2 * CHUNK :]).astype(BF16)
        mid_sum[:, at] += dot_nt(d_both[:, 0 : 2 * CHUNK], weights[at, 0 : 2 * CHUNK])
        return carry

    lax.fori_loop(0, WIDTH // 256, tile, 0, unroll=2)

    @pl.when(step == CHUNKS - 1)
    def _():
        mid_part[...] = mid_sum[...].astype(BF16)


def mlp_all(normed, upstream, weights):
    shape = jax.ShapeDtypeStruct
    whole = pl.BlockSpec((TOKENS, WIDTH), lambda f: (0, 0))
    block = pl.BlockSpec((WIDTH, 3 * CHUNK), lambda f: (0, f))
    return pl.pallas_call(
        mlp_kernel,
        grid=(CHUNKS,),
        out_shape=[
            shape((TOKENS, WIDTH), BF16),
            shape((TOKENS, MLP), BF16),
            shape((WIDTH, MLP_COLS), BF16),
        ],
        in_specs=[whole, whole, block],
        out_specs=[whole, pl.BlockSpec((TOKENS, CHUNK), lambda f: (0, f)), block],
        scratch_shapes=[
            pltpu.VMEM((WIDTH, TOKENS), BF16),
            pltpu.VMEM((WIDTH, TOKENS), BF16),
            pltpu.VMEM((TOKENS, 3 * CHUNK), BF16),
            pltpu.VMEM((TOKENS, WIDTH), F32),
        ],
        compiler_params=pltpu.CompilerParams(vmem_limit_bytes=VMEM_BYTES),
        cost_estimate=pl.CostEstimate(
            flops=16 * TOKENS * WIDTH * MLP, bytes_accessed=4 * WIDTH * MLP_COLS, transcendentals=TOKENS * MLP
        ),
        name="mlp_all",
    )(normed, upstream, weights)


class Scatter:
    def __init__(self, links, place, grads, sib, far, near, half_a, half_b, far_2, near_2):
        self.links, self.p = links, place
        self.grads, self.sib = grads, sib
        self.far, self.near, self.far_2, self.near_2 = far, near, far_2, near_2
        self.half_a, self.half_b = half_a, half_b
        self.sib_keys = {}

    def give(self, xx):
        p = self.p
        self.sib_keys[xx] = self.links.go(self.grads.at[xx, 1 - p.c], self.sib.at[xx], p.SIB)

    def take(self, xx):
        p, sib, grads = self.p, self.sib, self.grads
        self.links.arrived(sib.at[xx], self.sib_keys[xx], p.SIB)

        def one(j, carry):
            sib[xx, j] = (sib[xx, j].astype(F32) + grads[xx, p.c, j].astype(F32)).astype(BF16)
            return carry

        lax.fori_loop(0, 4, one, 0)

    def _ring(self, view, i, right, left, far, near, base):
        links = self.links
        ir, il, i2 = lax.rem(i + 1, 4), lax.rem(i + 3, 4), lax.rem(i + 2, 4)
        a, b = pl.ds(base, 16), pl.ds(base + 16, 16)
        na, nb = pl.ds(0, 16), pl.ds(16, 16)
        k0 = links.go(view(i2, a), far.at[0], right)
        k1 = links.go(view(i2, b), far.at[1], left)
        k2 = links.go(view(ir, b), near.at[0, :, nb], right)
        k3 = links.go(view(il, a), near.at[1, :, na], left)
        keys = []

        def merge():
            for way, k, row, at, source, target, to in (
                (0, k0, ir, a, left, right, na),
                (1, k1, il, b, right, left, nb),
            ):
                links.arrived(far.at[way], k, source)
                mine = view(row, at)

                def one(j, carry):
                    far[way, j] = (far[way, j].astype(F32) + mine[j].astype(F32)).astype(BF16)
                    return carry

                lax.fori_loop(0, far.shape[1], one, 0)
                keys.append(links.go(far.at[way], near.at[way, :, to], target))

        def settle():
            links.arrived(near.at[0, :, nb], k2, left)
            links.arrived(near.at[1, :, na], k3, right)
            links.arrived(near.at[0, :, na], keys[0], left)
            links.arrived(near.at[1, :, nb], keys[1], right)

        return merge, settle

    def first(self):
        p, sib = self.p, self.sib
        self.x_ring = self._ring(lambda j, r: sib.at[j, :, r], p.x, p.XR, p.XL, self.far.at[0], self.near.at[0], 0)
        self.z_ring = self._ring(lambda j, r: sib.at[:, j, r], p.z, p.ZR, p.ZL, self.far.at[1], self.near.at[1], 32)

    def merge(self):
        self.x_ring[0]()
        self.z_ring[0]()

    def turn(self):
        p, sib, near = self.p, self.sib, self.near
        self.x_ring[1]()

        def one_a(j, carry):
            total = sib[p.x, j, 0:32].astype(F32) + near[0, 0, j].astype(F32) + near[0, 1, j].astype(F32)
            self.half_a[j, 0] = total.astype(BF16)
            return carry

        lax.fori_loop(0, 4, one_a, 0)
        half_a, half_b = self.half_a, self.half_b
        self.ring_a = self._ring(
            lambda j, r: half_a.at[j, :, r], p.z, p.ZR, p.ZL, self.far_2.at[0], self.near_2.at[0], 0
        )
        self.z_ring[1]()

        def one_b(j, carry):
            total = sib[j, p.z, 32:64].astype(F32) + near[1, 0, j].astype(F32) + near[1, 1, j].astype(F32)
            self.half_b[j, 0] = total.astype(BF16)
            return carry

        lax.fori_loop(0, 4, one_b, 0)
        self.ring_b = self._ring(
            lambda j, r: half_b.at[j, :, r], p.x, p.XR, p.XL, self.far_2.at[1], self.near_2.at[1], 0
        )

    def merge_2(self):
        self.ring_a[0]()
        self.ring_b[0]()

    def finish(self, store):
        p, near = self.p, self.near_2
        self.ring_a[1]()
        store(0, self.half_a[p.z, 0].astype(F32) + near[0, 0, 0].astype(F32) + near[0, 1, 0].astype(F32))
        self.ring_b[1]()
        store(32, self.half_b[p.x, 0].astype(F32) + near[1, 0, 0].astype(F32) + near[1, 1, 0].astype(F32))

    @staticmethod
    def scratch(columns):
        return [
            pltpu.VMEM((4, 4, 64, columns), BF16),
            pltpu.VMEM((2, 2, 4, 16, columns), BF16),
            pltpu.VMEM((2, 2, 4, 32, columns), BF16),
            pltpu.VMEM((4, 1, 32, columns), BF16),
            pltpu.VMEM((4, 1, 32, columns), BF16),
            pltpu.VMEM((2, 2, 1, 16, columns), BF16),
            pltpu.VMEM((2, 2, 1, 32, columns), BF16),
        ]


def back_kernel(
    mid_part,
    hidden,
    mlp_full,
    mix_full,
    states,
    pre,
    ext,
    decay_g,
    input_g,
    conv_low,
    entering,
    mixed,
    normed_in,
    tokens,
    upstream,
    after_own,
    gain_rows,
    vectors,
    gate_w,
    doc_start,
    grad_tokens,
    block_out,
    grad_mix,
    small_sums,
    block_sums,
    gain_sums,
    work,
    small_work,
    own_tokens,
    own_upstream,
    out_part,
    d_after_low,
    d_after_own,
    gain_mid,
    d_mixed,
    tail_a,
    d_gates,
    d_both,
    d_first,
    small,
    rim_send,
    rim_recv,
    totals,
    totals_in,
    after,
    far_a,
    near_a,
    far_b,
    near_b,
    far_c,
    near_c,
    *rest,
):
    n_scatter = 7
    mix_scratch, rest = rest[:n_scatter], rest[n_scatter:]
    small_scratch, rest = rest[:n_scatter], rest[n_scatter:]
    back_steps(
        mid_part, hidden, mlp_full, mix_full, states, pre, ext, decay_g, input_g, conv_low, entering, mixed,
        normed_in, tokens, upstream, after_own, gain_rows, vectors, gate_w, doc_start,
        grad_tokens, block_out, grad_mix, small_sums, block_sums, gain_sums,
        work, small_work, own_tokens, own_upstream, out_part, d_after_low, d_after_own, gain_mid,
        d_mixed, tail_a, d_gates, d_both, d_first, small, rim_send, rim_recv, totals, totals_in, after,
        far_a, near_a, far_b, near_b, far_c, near_c, mix_scratch, small_scratch, *rest,
    )


def back_steps(
    mid_part, hidden, mlp_full, mix_full, states, pre, ext, decay_g, input_g, conv_low, entering, mixed,
    normed_in, tokens, upstream, after_own, gain_rows, vectors, gate_w, doc_start,
    grad_tokens, block_out, grad_mix, small_sums, block_sums, gain_sums,
    work, small_work, own_tokens, own_upstream, out_part, d_after_low, d_after_own, gain_mid,
    d_mixed, tail_a, d_gates, d_both, d_first, small, rim_send, rim_recv, totals, totals_in, after,
    far_a, near_a, far_b, near_b, far_c, near_c, mix_scratch, small_scratch,
    small_all,
    gain_in,
    gain_y,
    gain_s,
    gain_z,
    local,
    send,
    recv,
):
    p = Place()
    links = Links(send, recv)
    loads = []
    for f in range(CHUNKS):
        lo = 3 * f * CHUNK + 2 * CHUNK
        source = mlp_full.at[:, :, :, :, pl.ds(lo, CHUNK)]
        copy = pltpu.make_async_copy(source, work.at[:, :, :, :, pl.ds(f * CHUNK, CHUNK)], local.at[f])
        copy.start()
        loads.append(copy)
    load_tokens = pltpu.make_async_copy(tokens.at[p.y], own_tokens, local.at[CHUNKS])
    load_tokens.start()
    load_upstream = pltpu.make_async_copy(upstream.at[p.y], own_upstream, local.at[CHUNKS + 1])
    load_upstream.start()
    others_y = [{"tensor": lax.rem(p.y + d, 4)} for d in (1, 2, 3)]
    others_z = [{"dp": lax.rem(p.z + d, 4)} for d in (1, 2, 3)]
    greet([p.seq_at(d) for d in range(1, 8)] + others_y + others_z)
    middle = Reduce(links, p, mid_part, far_c, near_c)
    middle.send_first()
    middle.send_second()
    for copy in loads:
        copy.wait()

    def out_product(n, carry):
        weights = work[lax.div(n, 2), lax.rem(n, 2), :, :, 0:MLP].reshape(256, MLP)
        product = dot_nt(hidden[...], weights).astype(BF16)
        out_part[:, :, pl.ds(pl.multiple_of(n * 256, 256), 256)] = product.reshape(ROWS, SPAN, 256)
        return carry

    lax.fori_loop(0, 8, out_product, 0)
    load = pltpu.make_async_copy(mix_full, work, local.at[CHUNKS + 2])
    load.start()
    middle.merge()
    gain_mid[...] = jnp.zeros_like(gain_mid)
    gain_1 = gain_rows[1:2, :].astype(F32)
    load_upstream.wait()
    middle.settle()

    def middle_rows(k, carry):
        at = pl.ds(pl.multiple_of(k * 16, 16), 16)
        through, share = norm_back_rows(own_sum(middle, at), after_own[at, :], gain_1)
        gain_mid[...] += share[0:8] + share[8:16]
        total = own_upstream[at, :].astype(F32) + through
        d_after_own[at, :] = total
        d_after_low[p.y, at, :] = total.astype(BF16)
        return carry

    lax.fori_loop(0, SPAN // 16, middle_rows, 0)
    spread_c = Spread(links, p, d_after_low)
    spread_c.start()
    load.wait()
    rows_low = d_after_low.reshape(TOKENS, WIDTH)

    def mixed_row(row):
        rows = pl.ds(pl.multiple_of(row * SPAN, SPAN), SPAN)
        for start, size in ((0, 256), (256, 256), (512, 128)):
            weights = work[:, :, :, :, 2 * CHAN + start : 2 * CHAN + start + size].reshape(WIDTH, size)
            d_mixed[rows, start : start + size] = dot(d_after_low[row], weights)

    mixed_row(p.y)
    spread_c.forward()
    spread_c.near()
    mixed_row(p.yl)
    mixed_row(p.yr)
    spread_c.far()
    ahead = Reduce(links, p, out_part, far_b, near_b)
    ahead.send_first()
    ahead.send_second()
    mixed_row(p.y2)
    small[...] = jnp.zeros_like(small)
    totals[...] = jnp.zeros_like(totals)
    gain_in[...] = jnp.zeros_like(gain_in)
    offset = p.s * SPAN

    def chunk(i):
        r, g = lax.rem(i, ROWS), lax.div(i, ROWS)
        at = pl.ds(pl.multiple_of(g * LANES, LANES), LANES)
        rows = pl.ds(pl.multiple_of(r * SPAN, SPAN), SPAN)
        row = lax.broadcasted_iota(jnp.int32, (SPAN, LANES), 0)
        return r, g, at, rows, row

    def states_back(i, carry):
        r, g, at, rows, row = chunk(i)
        d_chunk = d_mixed[rows, at]
        value, slope = gelu_pair(pre[rows, at])
        d_both[rows, at] = (d_chunk * states[rows, at] * slope).astype(BF16)
        decay_now = jnp.exp(decay_g[rows, at] * vectors[7:8, at])
        carried = jnp.where(offset + row == doc_start[r], 0.0, decay_now)
        following = jnp.where(row == SPAN - 1, 1.0, pltpu.roll(carried, SPAN - 1, 0))
        a, b, first_a, first_b = row_scan(following, d_chunk * value, True)
        tail_a[rows, at] = a
        d_mixed[rows, at] = b
        put_pair(totals, at, r, carried[0:1] * first_a, carried[0:1] * first_b)
        return carry

    lax.fori_loop(0, ROWS * GROUPS, states_back, 0)
    keys = [links.go(totals, totals_in.at[p.s], p.seq_at(d)) for d in range(1, 8)]
    ahead.merge()
    state = jnp.zeros((ROWS, CHAN), F32)
    for d in range(1, 8):
        links.arrived(totals_in.at[p.seq_at(-d)["seq"]], keys[d - 1], p.seq_at(-d))
    totals_in[p.s] = totals[...]
    for source in range(7, 0, -1):
        both = totals_in[source]
        state = jnp.where(source > p.s, both[0:ROWS] * state + both[ROWS:], state)
    after[0:ROWS, :] = state
    after[ROWS:, :] = jnp.zeros((8 - ROWS, CHAN), F32)

    def gates_back(i, carry):
        r, g, at, rows, row = chunk(i)
        grads = d_mixed[rows, at] + tail_a[rows, at] * take_row(after, at, r)
        held = states[rows, at]
        previous = jnp.where(row == 0, take_row(entering, at, r), pltpu.roll(held, 1, 0))
        gate_d, gate_i = decay_g[rows, at], input_g[rows, at]
        rate = vectors[7:8, at]
        decay_now = jnp.exp(gate_d * rate)
        headroom = 1.0 - decay_now * decay_now
        root = jnp.sqrt(jnp.maximum(headroom, root_floor))
        conv = conv_low[rows, at].astype(F32)
        d_decay = jnp.where(offset + row == doc_start[r], 0.0, grads * previous) - jnp.where(
            headroom > root_floor, grads * gate_i * conv * decay_now / root, 0.0
        )
        d_log = d_decay * decay_now
        d_zero = d_log * rate * gate_d * (1.0 - gate_d)
        fed = grads * root
        d_one = fed * conv * gate_i * (1.0 - gate_i)
        d_gates[rows, pl.ds(pl.multiple_of(g * LANES, LANES), LANES)] = d_zero.astype(BF16)
        d_gates[rows, pl.ds(pl.multiple_of(CHAN + g * LANES, LANES), LANES)] = d_one.astype(BF16)
        tail_a[rows, at] = fed * gate_i
        small[5:6, at] += jnp.sum(d_zero, axis=0, keepdims=True)
        small[6:7, at] += jnp.sum(d_one, axis=0, keepdims=True)
        small[7:8, at] += jnp.sum(d_log * (-rate_scale * gate_d), axis=0, keepdims=True)
        return carry

    lax.fori_loop(0, ROWS * GROUPS, gates_back, 0)
    ahead.settle()

    def ahead_rows(k, carry):
        at = pl.ds(pl.multiple_of(k * 16, 16), 16)
        block_out[p.y, at, :] = (after_own[at, :] + own_sum(ahead, at)).astype(BF16)
        return carry

    lax.fori_loop(0, SPAN // 16, ahead_rows, 0)
    spread_b = Spread(links, p, block_out)
    spread_b.start()

    d_conv = tail_a
    held = None
    for g in range(GROUPS):
        total = d_conv[:, g * LANES : (g + 1) * LANES]
        if held is not None:
            total = total + held
        if g < HEADS:
            lo = g * LANES
            product = dot_nt(d_gates[:, lo : lo + 256], gate_w[0, g]) + dot_nt(
                d_gates[:, CHAN + lo : CHAN + lo + 256], gate_w[1, g]
            )
            total = total + product[:, :LANES]
            held = product[:, LANES:]
        d_conv[:, g * LANES : (g + 1) * LANES] = total

    body = d_mixed

    def conv_back(i, carry):
        r, g, at, rows, row = chunk(i)
        d_chunk = d_conv[rows, at]
        begin = doc_start[r]
        place = offset + row
        here = place >= begin
        head = jnp.zeros((8, LANES), F32)
        total = jnp.zeros((SPAN, LANES), F32)
        for k in range(CONV):
            before = CONV - 1 - k
            same = (place - before >= begin) == here
            kept = jnp.where(same, d_chunk, 0.0)
            value = ext[r, PAD - before : PAD - before + SPAN, at]
            small[k : k + 1, at] += jnp.sum(kept * value, axis=0, keepdims=True)
            term = kept * vectors[k : k + 1, at]
            if before:
                total = total + jnp.where(row < SPAN - before, pltpu.roll(term, SPAN - before, 0), 0.0)
                head = head + jnp.where(
                    row[0:8] >= 8 - before, pltpu.roll(term[0:8], 8 - before, 0), 0.0
                )
            else:
                total = total + term
        small[4:5, at] += jnp.sum(d_chunk, axis=0, keepdims=True)
        body[rows, at] = total
        rim_send[r, :, at] = head
        return carry

    lax.fori_loop(0, ROWS * GROUPS, conv_back, 0)
    k_rim = links.go(rim_send, rim_recv, p.seq_at(-1))

    def blocks(j, h):
        lo = h * LANES
        product = dot_tn(conv_low[:, lo : lo + 256], d_gates[:, j * CHAN + lo : j * CHAN + lo + 256])
        for q in range(BLK // 32):
            row = (j * HEADS + h) * BLK + 32 * q
            n, inner = row // 64, row % 64
            piece = product[32 * (h + q) : 32 * (h + q + 1), :].astype(BF16)
            small_work[n // 8, (n // 4) % 2, n % 4, inner : inner + 32, :] = piece

    for j in range(2):
        for h in range(HEADS):
            blocks(j, h)
    for n in range(20, 32):
        small_work[n // 8, (n // 4) % 2, n % 4] = jnp.zeros((64, SMALL), BF16)
    for k, n in enumerate((20, 21, 22)):
        width = min(256, CHAN - 256 * k)
        both = jnp.concatenate([small[:, 256 * k : 256 * k + width], jnp.zeros((8, width), F32)], axis=0)
        small_work[n // 8, (n // 4) % 2, n % 4, 0:16, 0:width] = both.astype(BF16)
    small_scatter = Scatter(links, p, small_work, *small_scratch)
    for xx in range(4):
        small_scatter.give(xx)
    spread_b.forward()
    links.arrived(rim_recv, k_rim, p.seq_at(1))
    for r in range(ROWS):
        last = r * SPAN + SPAN - 8
        body[last : last + 8, :] += jnp.where(p.s == 7, 0.0, rim_recv[r])
    for r in range(ROWS):
        d_both[r * SPAN : (r + 1) * SPAN, CHAN:] = body[r * SPAN : (r + 1) * SPAN, :].astype(BF16)

    def first_part(n, carry):
        weights = work[lax.div(n, 2), lax.rem(n, 2), :, :, 0 : 2 * CHAN].reshape(256, 2 * CHAN)
        product = dot_nt(d_both[...], weights).astype(BF16)
        d_first[:, :, pl.ds(pl.multiple_of(n * 256, 256), 256)] = product.reshape(ROWS, SPAN, 256)
        return carry

    back = Reduce(links, p, d_first, far_a, near_a)
    lax.fori_loop(0, 4, first_part, 0)
    back.send_first()
    lax.fori_loop(4, 8, first_part, 0)
    back.send_second()
    for xx in range(4):
        small_scatter.take(xx)
    small_scatter.first()

    def weight_grads(n):
        at = pl.ds(pl.multiple_of(n * 256, 256), 256)
        to = work.at[lax.div(n, 2), lax.rem(n, 2)]
        both = dot_tn(normed_in[:, at], d_both[...])
        to[:, :, 0 : 2 * CHAN] = both.astype(BF16).reshape(4, 64, 2 * CHAN)
        out = dot_tn(rows_low[:, at], mixed[...])
        to[:, :, 2 * CHAN : MIX_COLS] = out.astype(BF16).reshape(4, 64, CHAN)

    scatter = Scatter(links, p, work, *mix_scratch)

    def give(xx, carry):
        weight_grads(xx * 2 + 1 - p.c)
        return carry

    def keep(xx, carry):
        weight_grads(xx * 2 + p.c)
        return carry

    lax.fori_loop(0, 4, give, 0)
    for xx in range(4):
        scatter.give(xx)
    small_scatter.merge()
    back.merge()
    lax.fori_loop(0, 4, keep, 0)
    small_scatter.turn()
    for xx in range(4):
        scatter.take(xx)
    scatter.first()
    small_scatter.merge_2()
    back.settle()
    load_tokens.wait()
    gain = gain_rows[0:1, :].astype(F32)

    def back_rows(k, carry):
        at = pl.ds(pl.multiple_of(k * 16, 16), 16)
        through, share = norm_back_rows(own_sum(back, at), own_tokens[at, :].astype(F32), gain)
        gain_in[...] += share[0:8] + share[8:16]
        grad_tokens[p.y, at, :] = (d_after_own[at, :] + through).astype(BF16)
        return carry

    lax.fori_loop(0, SPAN // 16, back_rows, 0)
    spread_a = Spread(links, p, grad_tokens)
    spread_a.start()
    gain_y[p.y] = jnp.concatenate(
        [jnp.sum(gain_in[...], axis=0, keepdims=True), jnp.sum(gain_mid[...], axis=0, keepdims=True)], axis=0
    )
    y_keys = [links.go(gain_y.at[p.y], gain_y.at[p.y], device) for device in others_y]

    def store_small(base, value):
        small_all[p.x, p.c, p.z, base : base + 32, :] = value.astype(BF16)

    small_scatter.finish(store_small)
    small_gather = Gather(links, p, small_all)
    small_gather.first()
    scatter.merge()
    for d in (1, 2, 3):
        links.arrived(gain_y.at[lax.rem(p.y + 4 - d, 4)], y_keys[d - 1], others_y[0])
    gain_z[p.z] = gain_y[0] + gain_y[1] + gain_y[2] + gain_y[3]
    z_keys = [links.go(gain_z.at[p.z], gain_z.at[p.z], device) for device in others_z]
    small_gather.middle()
    small_gather.finish()
    small_gather.second()
    spread_a.forward()
    scatter.turn()
    for d in (1, 2, 3):
        links.arrived(gain_z.at[lax.rem(p.z + 4 - d, 4)], z_keys[d - 1], others_z[0])
    gain_s[p.s] = gain_z[0] + gain_z[1] + gain_z[2] + gain_z[3]
    s_keys = [links.go(gain_s.at[p.s], gain_s.at[p.s], p.seq_at(d)) for d in range(1, 8)]
    small_gather.middle()
    small_gather.finish()
    scatter.merge_2()
    for d in range(1, 8):
        links.arrived(gain_s.at[p.seq_at(-d)["seq"]], s_keys[d - 1], p.seq_at(-d))
    total = gain_s[0]
    for s in range(1, 8):
        total = total + gain_s[s]
    gain_sums[...] = total
    spread_b.near()
    spread_b.far()
    small_gather.settle()
    for k, n in enumerate((20, 21, 22)):
        width = min(256, CHAN - 256 * k)
        value = small_all[n // 8, (n // 4) % 2, n % 4, 0:16, 0:width].astype(F32)
        small_sums[:, 256 * k : 256 * k + width] = value[0:8]
    for n in range(20):
        value = small_all[n // 8, (n // 4) % 2, n % 4].astype(F32)
        block_sums[64 * n : 64 * (n + 1), :] = value

    def store(base, value):
        grad_mix[base : base + 32, :] = value

    scatter.finish(store)
    spread_a.near()
    spread_a.far()
    links.drain()


def back_all(*operands):
    shape = jax.ShapeDtypeStruct
    tc = (TOKENS, CHAN)
    pair = [pltpu.VMEM((2, SPAN, HALF), BF16), pltpu.VMEM((2, SPAN, WIDTH), BF16)]
    return pl.pallas_call(
        back_kernel,
        out_shape=[
            shape((ROWS, SPAN, WIDTH), BF16),
            shape((ROWS, SPAN, WIDTH), BF16),
            shape((64, MIX_COLS), F32),
            shape((8, CHAN), F32),
            shape((2 * HEADS * BLK, 256), F32),
            shape((2, WIDTH), F32),
        ],
        in_specs=[vmem()] * 2 + [anyspace()] * 2 + [vmem()] * 9 + [anyspace()] * 2 + [vmem()] * 4 + [smem()],
        out_specs=[vmem()] * 6,
        scratch_shapes=[
            pltpu.VMEM((4, 2, 4, 64, MIX_COLS), BF16),
            pltpu.VMEM((4, 2, 4, 64, SMALL), BF16),
            pltpu.VMEM((SPAN, WIDTH), BF16),
            pltpu.VMEM((SPAN, WIDTH), BF16),
            pltpu.VMEM((ROWS, SPAN, WIDTH), BF16),
            pltpu.VMEM((ROWS, SPAN, WIDTH), BF16),
            pltpu.VMEM((SPAN, WIDTH), F32),
            pltpu.VMEM((8, WIDTH), F32),
            pltpu.VMEM(tc, F32),
            pltpu.VMEM(tc, F32),
            pltpu.VMEM((TOKENS, 2 * CHAN), BF16),
            pltpu.VMEM((TOKENS, 2 * CHAN), BF16),
            pltpu.VMEM((ROWS, SPAN, WIDTH), BF16),
            pltpu.VMEM((8, CHAN), F32),
            pltpu.VMEM((ROWS, PAD, CHAN), F32),
            pltpu.VMEM((ROWS, PAD, CHAN), F32),
            pltpu.VMEM((8, CHAN), F32),
            pltpu.VMEM((8, 8, CHAN), F32),
            pltpu.VMEM((8, CHAN), F32),
        ]
        + pair * 3
        + Scatter.scratch(MIX_COLS)
        + Scatter.scratch(SMALL)
        + [
            pltpu.VMEM((4, 2, 4, 64, SMALL), BF16),
            pltpu.VMEM((8, WIDTH), F32),
            pltpu.VMEM((4, 2, WIDTH), F32),
            pltpu.VMEM((8, 2, WIDTH), F32),
            pltpu.VMEM((4, 2, WIDTH), F32),
            pltpu.SemaphoreType.DMA((CHUNKS + 3,)),
            pltpu.SemaphoreType.DMA((184,)),
            pltpu.SemaphoreType.DMA((184,)),
        ],
        compiler_params=params(2),
        name="back_all",
    )(*operands)


def finish_kernel(
    block_in,
    tokens_in,
    states_in,
    mix_sum,
    small,
    blocks_in,
    gains_in,
    mlp_sum,
    block_out,
    states,
    grad_tokens,
    grad_gains,
    grad_mix_in,
    grad_mix_out,
    grad_conv,
    grad_blocks,
    grad_bias,
    grad_mlp_in,
    grad_mlp_out,
):
    step = pl.program_id(0)
    block_out[...] = block_in[...]
    grad_tokens[...] = tokens_in[...]
    states[...] = states_in[...]
    for h in range(HEADS):

        @pl.when(step == h)
        def _():
            for j in range(2):
                grad_blocks[j, 0] = blocks_in[j, 0, :, 32 * h : 32 * h + BLK]

    @pl.when(step == 0)
    def _():
        grad_gains[...] = gains_in[...]
        for j in range(2):
            grad_mix_in[j] = mix_sum[:, j * CHAN : (j + 1) * CHAN]
        grad_mix_out[...] = mix_sum[:, 2 * CHAN :]
        grad_conv[...] = small[0:CONV, :]
        grad_bias[...] = small[CONV + 1 : CONV + 3, :]
        for f in range(CHUNKS):
            lo, at = 3 * f * CHUNK, pl.ds(f * CHUNK, CHUNK)
            for j in range(2):
                grad_mlp_in[j, :, at] = mlp_sum[:, lo + j * CHUNK : lo + (j + 1) * CHUNK].astype(F32)
            grad_mlp_out[:, at] = mlp_sum[:, lo + 2 * CHUNK : lo + 3 * CHUNK].astype(F32)


def finish(*operands):
    shape = jax.ShapeDtypeStruct
    row = lambda width: pl.BlockSpec((1, SPAN, width), lambda i: (i, 0, 0))
    whole = lambda *dims: pl.BlockSpec(dims, lambda i: (0,) * len(dims))
    head = lambda width: pl.BlockSpec((2, 1, BLK, width), lambda i: (0, i, 0, 0))
    return pl.pallas_call(
        finish_kernel,
        grid=(ROWS,),
        out_shape=[
            shape((ROWS, SPAN, WIDTH), BF16),
            shape((ROWS, SPAN, CHAN), F32),
            shape((ROWS, SPAN, WIDTH), BF16),
            shape((2, WIDTH), F32),
            shape((2, 64, CHAN), F32),
            shape((64, CHAN), F32),
            shape((CONV, CHAN), F32),
            shape((2, HEADS, BLK, BLK), F32),
            shape((2, CHAN), F32),
            shape((2, 64, MLP), F32),
            shape((64, MLP), F32),
        ],
        in_specs=[
            row(WIDTH),
            row(WIDTH),
            row(CHAN),
            whole(64, MIX_COLS),
            whole(8, CHAN),
            head(256),
            whole(2, WIDTH),
            whole(64, MLP_COLS),
        ],
        out_specs=[
            row(WIDTH),
            row(CHAN),
            row(WIDTH),
            whole(2, WIDTH),
            whole(2, 64, CHAN),
            whole(64, CHAN),
            whole(CONV, CHAN),
            head(BLK),
            whole(2, CHAN),
            whole(2, 64, MLP),
            whole(64, MLP),
        ],
        compiler_params=pltpu.CompilerParams(vmem_limit_bytes=VMEM_BYTES),
        name="finish",
    )(*operands)


def per_device(
    tokens,
    init_state,
    conv_state,
    fresh_rows,
    doc_start,
    norm_gains,
    mix_in,
    mix_out,
    conv_weight,
    conv_bias,
    gate_blocks,
    gate_bias,
    decay_param,
    mlp_in,
    mlp_out,
    cotangent,
):
    gate_w = jnp.stack(
        [
            jnp.pad(gate_blocks[:, h], ((0, 0), (32 * h, 96 - 32 * h), (32 * h, 96 - 32 * h)))
            for h in range(HEADS)
        ],
        axis=1,
    )
    raw_vectors = jnp.concatenate([conv_weight, conv_bias[None], gate_bias, decay_param[None]], axis=0)
    (
        mix_full,
        mlp_full,
        states,
        pre,
        ext,
        decay_g,
        input_g,
        conv_low,
        mixed,
        normed_in,
        entering,
        vectors,
        normed_mid,
        after_own,
    ) = mix_forward(
        tokens.reshape(TOKENS, WIDTH),
        mix_in,
        mix_out.T,
        mlp_in,
        mlp_out.T,
        init_state,
        conv_state.transpose(1, 0, 2),
        fresh_rows,
        doc_start,
        norm_gains,
        raw_vectors,
        gate_w,
    )
    mid_part, hidden, grad_mlp = mlp_all(
        normed_mid.reshape(TOKENS, WIDTH),
        cotangent.reshape(TOKENS, WIDTH),
        mlp_full.reshape(WIDTH, MLP_COLS),
    )
    grad_mlp = lax.psum_scatter(grad_mlp, ("seq", "dp"), scatter_dimension=0, tiled=True)
    grad_tokens, block_out, grad_mix, small, blocks, grad_gains = back_all(
        mid_part.reshape(ROWS, SPAN, WIDTH),
        hidden,
        mlp_full,
        mix_full,
        states,
        pre,
        ext,
        decay_g,
        input_g,
        conv_low,
        entering,
        mixed,
        normed_in,
        tokens,
        cotangent,
        after_own,
        norm_gains,
        vectors,
        gate_w,
        doc_start,
    )
    (
        block_out,
        states,
        grad_tokens,
        grad_gains,
        grad_mix_in,
        grad_mix_out,
        grad_conv,
        grad_blocks,
        grad_bias,
        grad_mlp_in,
        grad_mlp_out,
    ) = finish(
        block_out,
        grad_tokens,
        states.reshape(ROWS, SPAN, CHAN),
        grad_mix,
        small,
        blocks.reshape(2, HEADS, BLK, 256),
        grad_gains,
        grad_mlp,
    )
    return (
        block_out,
        states,
        grad_tokens,
        grad_gains,
        grad_mix_in,
        grad_mix_out.T,
        grad_conv,
        small[CONV],
        grad_blocks,
        grad_bias,
        small[CONV + 3] * jax.nn.sigmoid(decay_param.astype(F32)),
        grad_mlp_in,
        grad_mlp_out.T,
    )


def solution(mesh):
    in_specs = (
        P("dp", "seq", None),
        P("dp", "tensor"),
        P("dp", None, "tensor"),
        P("dp"),
        P("dp"),
        P(),
        P(None, ("seq", "dp"), "tensor"),
        P("tensor", ("seq", "dp")),
        P(None, "tensor"),
        P("tensor"),
        P(None, "tensor", None, None),
        P(None, "tensor"),
        P("tensor"),
        P(None, ("seq", "dp"), "tensor"),
        P("tensor", ("seq", "dp")),
        P("dp", "seq", None),
    )
    out_specs = (
        P("dp", "seq", None),
        P("dp", "seq", "tensor"),
        P("dp", "seq", None),
        P(),
        P(None, ("seq", "dp"), "tensor"),
        P("tensor", ("seq", "dp")),
        P(None, "tensor"),
        P("tensor"),
        P(None, "tensor", None, None),
        P(None, "tensor"),
        P("tensor"),
        P(None, ("seq", "dp"), "tensor"),
        P("tensor", ("seq", "dp")),
    )
    return jax.shard_map(
        per_device, mesh=mesh, in_specs=in_specs, out_specs=out_specs, check_vma=False
    )
```

```python
import functools

import jax
import jax.numpy as jnp
from jax import lax
from jax.experimental import pallas as pl
from jax.experimental.pallas import tpu as pltpu
from jax.sharding import PartitionSpec as P

MESH = pl.DeviceIdType.MESH
F32 = jnp.float32
BF16 = jnp.bfloat16
VMEM_BYTES = 60 * 2**20

CONV = 4
ROWS = 4
SPAN = 128
TOKENS = ROWS * SPAN
WIDTH = 2048
CHAN = 640
HEADS = 4
BLK = 160
MLP = 1536
MIX_COLS = 3 * CHAN
MLP_COLS = 3 * MLP
MLP_CUT = 2304
CHUNK = 256
CHUNKS = MLP // CHUNK
SMALL = 256
LANES = 128
GROUPS = CHAN // LANES
PAD = 8

epsilon = 1e-06
root_floor = 0.001
rate_scale = 8.0


class Place:
    def __init__(self):
        self.s = lax.axis_index("seq")
        self.z = lax.axis_index("dp")
        self.y = lax.axis_index("tensor")
        self.x, self.c = lax.div(self.s, 2), lax.rem(self.s, 2)
        x, c, z, y = self.x, self.c, self.z, self.y
        self.xr, self.xl = lax.rem(x + 1, 4), lax.rem(x + 3, 4)
        self.zr, self.zl = lax.rem(z + 1, 4), lax.rem(z + 3, 4)
        self.yr, self.yl, self.y2 = lax.rem(y + 1, 4), lax.rem(y + 3, 4), lax.rem(y + 2, 4)
        self.XR, self.XL = {"seq": self.xr * 2 + c}, {"seq": self.xl * 2 + c}
        self.ZR, self.ZL = {"dp": self.zr}, {"dp": self.zl}
        self.YR, self.YL = {"tensor": self.yr}, {"tensor": self.yl}
        self.SIB = {"seq": x * 2 + 1 - c}

    def seq_at(self, distance):
        return {"seq": lax.rem(self.s + distance + 8, 8)}


def greet(devices):
    barrier = pltpu.get_barrier_semaphore()
    for device in devices:
        pl.semaphore_signal(barrier, inc=1, device_id=device, device_id_type=MESH)
    pl.semaphore_wait(barrier, len(devices))


class Links:
    def __init__(self, send, recv):
        self.send, self.recv = send, recv
        self.count = 0
        self.keyed = {}

    def go(self, src, dst, device):
        k = self.count
        self.count += 1
        copy = pltpu.make_async_remote_copy(
            src_ref=src,
            dst_ref=dst,
            send_sem=self.send.at[k],
            recv_sem=self.recv.at[k],
            device_id=device,
            device_id_type=MESH,
        )
        copy.start()
        self.keyed[k] = copy
        return k

    def arrived(self, view, k, device):
        pltpu.make_async_remote_copy(
            src_ref=view,
            dst_ref=view,
            send_sem=self.send.at[k],
            recv_sem=self.recv.at[k],
            device_id=device,
            device_id_type=MESH,
        ).wait_recv()

    def drain(self):
        for copy in self.keyed.values():
            copy.wait_send()
        self.keyed = {}

    def sent(self, keys):
        for k in keys:
            self.keyed.pop(k).wait_send()


class Gather:
    def __init__(self, links, place, out, cut):
        self.links, self.p = links, place
        self.out_a = out.at[:, :, :, :, pl.ds(0, cut)]
        self.out_b = out.at[:, :, :, :, pl.ds(cut, out.shape[-1] - cut)]
        self.to_sibling = []

    def _pass_on(self, view_of):
        k = self.links.go(view_of(self.p.c), view_of(self.p.c), self.p.SIB)
        self.to_sibling.append((view_of, k))

    def _ring(self, blk, i, right, left):
        links, p = self.links, self.p
        c = p.c
        ir, il, i2 = lax.rem(i + 1, 4), lax.rem(i + 3, 4), lax.rem(i + 2, 4)
        a, b = pl.ds(0, 32), pl.ds(32, 32)
        k0 = links.go(blk(c, i, a), blk(c, i, a), right)
        k1 = links.go(blk(c, i, b), blk(c, i, b), left)
        k2 = links.go(blk(c, i, b), blk(c, i, b), right)
        k3 = links.go(blk(c, i, a), blk(c, i, a), left)
        later = []

        def middle():
            links.arrived(blk(c, il, a), k0, left)
            later.append(links.go(blk(c, il, a), blk(c, il, a), right))
            links.arrived(blk(c, ir, b), k1, right)
            later.append(links.go(blk(c, ir, b), blk(c, ir, b), left))
            self._pass_on(lambda cc: blk(cc, il, a))
            self._pass_on(lambda cc: blk(cc, ir, b))

        def finish():
            for view, k, source in (
                (lambda cc: blk(cc, il, b), k2, left),
                (lambda cc: blk(cc, ir, a), k3, right),
                (lambda cc: blk(cc, i2, a), later[0], left),
                (lambda cc: blk(cc, i2, b), later[1], right),
            ):
                links.arrived(view(c), k, source)
                self._pass_on(view)

        return middle, finish

    def first(self):
        p, a, b = self.p, self.out_a, self.out_b
        self.ring_a = self._ring(lambda cc, j, r: a.at[j, cc, p.z, r], p.x, p.XR, p.XL)
        self.ring_b = self._ring(lambda cc, j, r: b.at[p.x, cc, j, r], p.z, p.ZR, p.ZL)
        self._pass_on(lambda cc: a.at[p.x, cc, p.z])
        self._pass_on(lambda cc: b.at[p.x, cc, p.z])

    def second_z(self):
        p, a = self.p, self.out_a
        self.ring_a = self._ring(lambda cc, j, r: a.at[:, cc, j, r], p.z, p.ZR, p.ZL)

    def second_x(self):
        p, b = self.p, self.out_b
        self.ring_b = self._ring(lambda cc, j, r: b.at[j, cc, :, r], p.x, p.XR, p.XL)

    def second(self):
        self.second_z()
        self.second_x()

    def middle(self):
        self.ring_a[0]()
        self.ring_b[0]()

    def finish(self):
        self.ring_a[1]()
        self.ring_b[1]()

    def settle(self):
        for view_of, k in self.to_sibling:
            self.links.arrived(view_of(1 - self.p.c), k, self.p.SIB)


CA, CB = pl.ds(0, WIDTH // 2), pl.ds(WIDTH // 2, WIDTH // 2)
HALF = WIDTH // 2


class Reduce:
    def __init__(self, links, place, part, far, near):
        self.links, self.p, self.part, self.far, self.near = links, place, part, far, near

    def send_first(self):
        p, part, near = self.p, self.part, self.near
        self.k0 = self.links.go(part.at[p.y2, :, CA], self.far.at[0], p.YR)
        self.k3 = self.links.go(part.at[p.yl, :, CA], near.at[1, :, CA], p.YL)

    def send_second(self):
        p, part, near = self.p, self.part, self.near
        self.k1 = self.links.go(part.at[p.y2, :, CB], self.far.at[1], p.YL)
        self.k2 = self.links.go(part.at[p.yr, :, CB], near.at[0, :, CB], p.YR)

    def merge(self):
        p, part, near, far = self.p, self.part, self.near, self.far
        self.links.arrived(far.at[0], self.k0, p.YL)
        far[0] = (far[0].astype(F32) + part[p.yr, :, 0:HALF].astype(F32)).astype(BF16)
        self.k4 = self.links.go(far.at[0], near.at[0, :, CA], p.YR)
        self.links.arrived(far.at[1], self.k1, p.YR)
        far[1] = (far[1].astype(F32) + part[p.yl, :, HALF:WIDTH].astype(F32)).astype(BF16)
        self.k5 = self.links.go(far.at[1], near.at[1, :, CB], p.YL)

    def settle(self):
        p, near = self.p, self.near
        self.links.arrived(near.at[0, :, CB], self.k2, p.YL)
        self.links.arrived(near.at[1, :, CA], self.k3, p.YR)
        self.links.arrived(near.at[0, :, CA], self.k4, p.YL)
        self.links.arrived(near.at[1, :, CB], self.k5, p.YR)


class Spread:
    def __init__(self, links, place, out):
        self.links, self.p, self.out = links, place, out

    def start(self):
        self.start_first()
        self.start_second()

    def start_first(self):
        go, out, y, p = self.links.go, self.out, self.p.y, self.p
        self.k0 = go(out.at[y, :, CA], out.at[y, :, CA], p.YR)
        self.k1 = go(out.at[y, :, CB], out.at[y, :, CB], p.YL)

    def start_second(self):
        go, out, y, p = self.links.go, self.out, self.p.y, self.p
        self.k2 = go(out.at[y, :, CB], out.at[y, :, CB], p.YR)
        self.k3 = go(out.at[y, :, CA], out.at[y, :, CA], p.YL)

    def forward(self):
        go, out, p, arrived = self.links.go, self.out, self.p, self.links.arrived
        arrived(out.at[p.yl, :, CA], self.k0, p.YL)
        self.k4 = go(out.at[p.yl, :, CA], out.at[p.yl, :, CA], p.YR)
        arrived(out.at[p.yr, :, CB], self.k1, p.YR)
        self.k5 = go(out.at[p.yr, :, CB], out.at[p.yr, :, CB], p.YL)

    def near(self):
        out, p, arrived = self.out, self.p, self.links.arrived
        arrived(out.at[p.yl, :, CB], self.k2, p.YL)
        arrived(out.at[p.yr, :, CA], self.k3, p.YR)

    def far(self):
        out, p, arrived = self.out, self.p, self.links.arrived
        arrived(out.at[p.y2, :, CA], self.k4, p.YL)
        arrived(out.at[p.y2, :, CB], self.k5, p.YR)


def dot(a, b):
    return jnp.dot(a, b, preferred_element_type=F32)


def dot_nt(a, b):
    return lax.dot_general(a, b, (((1,), (1,)), ((), ())), preferred_element_type=F32)


def dot_tn(a, b):
    return lax.dot_general(a, b, (((0,), (0,)), ((), ())), preferred_element_type=F32)


GELU_C = 0.7978845608028654
GELU_A = 0.044715


def gelu(v):
    return 0.5 * v * (1.0 + jnp.tanh(GELU_C * (v + GELU_A * v * v * v)))


def gelu_pair(v):
    t = jnp.tanh(GELU_C * (v + GELU_A * v * v * v))
    value = 0.5 * v * (1.0 + t)
    slope = 0.5 * (1.0 + t) + 0.5 * v * (1.0 - t * t) * (GELU_C * (1.0 + 3.0 * GELU_A * v * v))
    return value, slope


def tile_scan(a, b, reverse):
    row = lax.broadcasted_iota(jnp.int32, a.shape, 1)
    for step in (1, 2, 4):
        if reverse:
            shift, valid = 8 - step, row < 8 - step
        else:
            shift, valid = step, row >= step
        a_near, b_near = pltpu.roll(a, shift, 1), pltpu.roll(b, shift, 1)
        b = jnp.where(valid, a * b_near + b, b)
        a = jnp.where(valid, a * a_near, a)
    return a, b


def row_scan(a, b, reverse):
    tiles = SPAN // 8
    a, b = tile_scan(a.reshape(tiles, 8, LANES), b.reshape(tiles, 8, LANES), reverse)
    edge = 0 if reverse else 7
    order = range(tiles - 1, -1, -1) if reverse else range(tiles)
    out_a, out_b = [None] * tiles, [None] * tiles
    carry_a = carry_b = None
    for k in order:
        ak, bk = a[k], b[k]
        if carry_a is not None:
            bk = ak * carry_b + bk
            ak = ak * carry_a
        out_a[k], out_b[k] = ak, bk
        carry_a, carry_b = ak[edge : edge + 1], bk[edge : edge + 1]
    return jnp.concatenate(out_a, axis=0), jnp.concatenate(out_b, axis=0), carry_a, carry_b


def put_pair(ref, at, r, first, second):
    row = lax.broadcasted_iota(jnp.int32, (8, LANES), 0)
    ref[:, at] = jnp.where(row == r, first, jnp.where(row == ROWS + r, second, ref[:, at]))


def take_row(ref, at, r):
    row = lax.broadcasted_iota(jnp.int32, (8, LANES), 0)
    return jnp.sum(jnp.where(row == r, ref[:, at], 0.0), axis=0, keepdims=True)


def assemble_vectors(vectors, raw):
    value = raw[...].astype(F32)
    row = lax.broadcasted_iota(jnp.int32, value.shape, 0)
    vectors[...] = jnp.where(row == 7, -rate_scale * jnp.log1p(jnp.exp(jnp.where(row == 7, value, 0.0))), value)


def mix_forward_kernel(
    tokens,
    mix_in,
    mix_out,
    mlp_in,
    mlp_out,
    init_state,
    conv_state,
    fresh_rows,
    doc_start,
    gain_rows,
    raw_vectors,
    gate_w,
    mix_full_out,
    mlp_full,
    states_out,
    pre_out,
    ext_out,
    decay_out,
    input_out,
    conv_out,
    mixed_out,
    normed_in_out,
    entering_out,
    vectors_out,
    normed_mid,
    after_own,
    mlp_own,
    gains,
    vectors,
    mix_full,
    normed_in,
    pre,
    ext,
    decay_g,
    input_g,
    conv_low,
    cum_a,
    loc_b,
    states,
    mixed,
    rim_send,
    rim_recv,
    totals,
    totals_in,
    entering,
    part,
    far,
    near,
    local,
    send,
    recv,
):
    p = Place()
    links = Links(send, recv)
    mine = mix_full.at[p.x, p.c, p.z]
    for j in range(2):
        mine[:, j * CHAN : (j + 1) * CHAN] = mix_in[j]
    mine[:, 2 * CHAN :] = mix_out[...]
    greet([p.seq_at(d) for d in range(1, 8)] + [p.ZR, p.ZL, p.YR, p.YL])
    in_gather = Gather(links, p, mix_full.at[:, :, :, :, pl.ds(0, 2 * CHAN)], CHAN)
    out_gather = Gather(links, p, mix_full.at[:, :, :, :, pl.ds(2 * CHAN, CHAN)], 384)
    mlp_gather = Gather(links, p, mlp_full, MLP_CUT)
    in_gather.first()
    for j in range(2):
        mlp_own[:, j * MLP : (j + 1) * MLP] = mlp_in[j]
    mlp_own[:, 2 * MLP :] = mlp_out[...]
    own_mlp = pltpu.make_async_copy(mlp_own, mlp_full.at[p.x, p.c, p.z], local.at[0])
    own_mlp.start()
    gains[...] = gain_rows[...].astype(F32)
    assemble_vectors(vectors, raw_vectors)

    def norm_rows(first, last):
        def one(k, carry):
            at = pl.ds(pl.multiple_of(k * 32, 32), 32)
            stream = tokens[at, :].astype(F32)
            scale = lax.rsqrt(jnp.mean(stream * stream, axis=-1, keepdims=True) + epsilon)
            normed_in[at, :] = (stream * scale * gains[0:1, :]).astype(BF16)
            return carry

        lax.fori_loop(first, last, one, 0)

    norm_rows(0, 8)
    in_gather.middle()
    in_gather.finish()
    in_gather.second()
    own_mlp.wait()
    norm_rows(8, 16)
    in_gather.middle()
    out_gather.first()
    mlp_gather.first()
    in_gather.finish()
    out_gather.middle()
    out_gather.finish()
    out_gather.second()
    in_gather.settle()
    saves = []

    def save(src, dst):
        copy = pltpu.make_async_copy(src, dst, local.at[2 + len(saves)])
        copy.start()
        saves.append(copy)

    save(normed_in, normed_in_out)
    save(vectors, vectors_out)

    def project(n, carry):
        at = pl.ds(pl.multiple_of(n * 256, 256), 256)
        pre[:, at] = dot(normed_in[...], mix_full[:, :, :, :, at].reshape(WIDTH, 256))
        return carry

    lax.fori_loop(2, 5, project, 0)
    for r in range(ROWS):
        ext[r, PAD:, :] = pre[r * SPAN : (r + 1) * SPAN, CHAN : 2 * CHAN].astype(BF16).astype(F32)
        rim_send[r] = ext[r, SPAN : SPAN + PAD, :]
    k_rim = links.go(rim_send, rim_recv, p.seq_at(1))
    lax.fori_loop(0, 2, project, 0)
    save(pre.at[:, pl.ds(0, CHAN)], pre_out)
    links.arrived(rim_recv, k_rim, p.seq_at(-1))
    at_start = p.s == 0
    for r in range(ROWS):
        keep = (1 - fresh_rows[r]).astype(F32)
        ext[r, 0:PAD, :] = jnp.where(at_start, 0.0, rim_recv[r])
        for j in range(CONV - 1):
            at = slice(PAD - 3 + j, PAD - 2 + j)
            first_rim = conv_state[j, r : r + 1, :].astype(F32) * keep
            ext[r, at, :] = jnp.where(at_start, first_rim, rim_recv[r, at, :])
    offset = p.s * SPAN

    def conv_chunk(i, carry):
        r, g = lax.rem(i, ROWS), lax.div(i, ROWS)
        at = pl.ds(pl.multiple_of(g * LANES, LANES), LANES)
        place = offset + lax.broadcasted_iota(jnp.int32, (SPAN, LANES), 0)
        begin = doc_start[r]
        here = place >= begin
        total = jnp.zeros((SPAN, LANES), F32) + vectors[4:5, at]
        for k in range(CONV):
            value = ext[r, PAD - 3 + k : PAD - 3 + k + SPAN, at]
            same = (place - (3 - k) >= begin) == here
            total = total + vectors[k : k + 1, at] * jnp.where(same, value, 0.0)
        rows = pl.ds(pl.multiple_of(r * SPAN, SPAN), SPAN)
        conv_low[rows, at] = total.astype(BF16)
        return carry

    lax.fori_loop(0, ROWS * GROUPS, conv_chunk, 0)
    save(ext, ext_out)
    save(conv_low, conv_out)

    for j, target in ((0, decay_g), (1, input_g)):
        held = None
        for g in range(GROUPS):
            total = held
            if g < HEADS:
                product = dot(conv_low[:, g * LANES : g * LANES + 256], gate_w[j, g])
                total = product[:, :LANES] if held is None else held + product[:, :LANES]
                held = product[:, LANES:]
            target[:, g * LANES : (g + 1) * LANES] = total

    def gate_chunk(i, carry):
        r, g = lax.rem(i, ROWS), lax.div(i, ROWS)
        at = pl.ds(pl.multiple_of(g * LANES, LANES), LANES)
        rows = pl.ds(pl.multiple_of(r * SPAN, SPAN), SPAN)
        gate_d = jax.nn.sigmoid(decay_g[rows, at] + vectors[5:6, at])
        gate_i = jax.nn.sigmoid(input_g[rows, at] + vectors[6:7, at])
        decay_g[rows, at] = gate_d
        input_g[rows, at] = gate_i
        decay_now = jnp.exp(gate_d * vectors[7:8, at])
        root = jnp.sqrt(jnp.maximum(1.0 - decay_now * decay_now, root_floor))
        fed = root * gate_i * conv_low[rows, at].astype(F32)
        place = offset + lax.broadcasted_iota(jnp.int32, (SPAN, LANES), 0)
        carried = jnp.where(place == doc_start[r], 0.0, decay_now)
        a, b, last_a, last_b = row_scan(carried, fed, False)
        cum_a[rows, at] = a
        loc_b[rows, at] = b
        put_pair(totals, at, r, last_a, last_b)
        return carry

    totals[...] = jnp.zeros_like(totals)
    lax.fori_loop(0, ROWS * GROUPS, gate_chunk, 0)
    keys = [links.go(totals, totals_in.at[p.s], p.seq_at(d)) for d in range(1, 8)]
    save(decay_g, decay_out)
    save(input_g, input_out)
    out_gather.middle()
    out_gather.finish()
    row = lax.broadcasted_iota(jnp.int32, (ROWS, CHAN), 0)
    kept = jnp.zeros((ROWS, CHAN), F32)
    for r in range(ROWS):
        kept = jnp.where(row == r, (1 - fresh_rows[r]).astype(F32), kept)
    state = init_state[...] * kept
    for d in range(1, 8):
        links.arrived(totals_in.at[p.seq_at(-d)["seq"]], keys[d - 1], p.seq_at(-d))
    mlp_gather.middle()
    mlp_gather.finish()
    mlp_gather.second()
    totals_in[p.s] = totals[...]
    for source in range(7):
        both = totals_in[source]
        state = jnp.where(source < p.s, both[0:ROWS] * state + both[ROWS:], state)
    entering[0:ROWS, :] = state
    entering[ROWS:, :] = jnp.zeros((8 - ROWS, CHAN), F32)

    def state_chunk(i, carry):
        r, g = lax.rem(i, ROWS), lax.div(i, ROWS)
        at = pl.ds(pl.multiple_of(g * LANES, LANES), LANES)
        rows = pl.ds(pl.multiple_of(r * SPAN, SPAN), SPAN)
        value = loc_b[rows, at] + cum_a[rows, at] * take_row(entering, at, r)
        states[rows, at] = value
        mixed[rows, at] = (value * gelu(pre[rows, at])).astype(BF16)
        return carry

    lax.fori_loop(0, ROWS * GROUPS, state_chunk, 0)
    save(states, states_out)
    save(mixed, mixed_out)
    save(entering, entering_out)

    out_gather.settle()
    save(mix_full, mix_full_out)

    def partial(n, carry):
        weights = mix_full[lax.div(n, 2), lax.rem(n, 2), :, :, 2 * CHAN :].reshape(256, CHAN)
        product = dot_nt(mixed[...], weights).astype(BF16)
        part[:, :, pl.ds(pl.multiple_of(n * 256, 256), 256)] = product.reshape(ROWS, SPAN, 256)
        return carry

    reduce = Reduce(links, p, part, far, near)
    lax.fori_loop(0, 4, partial, 0)
    reduce.send_first()
    lax.fori_loop(4, 8, partial, 0)
    reduce.send_second()
    mlp_gather.middle()
    reduce.merge()
    reduce.settle()

    def norm_mid(k, carry):
        at = pl.ds(pl.multiple_of(k * 16, 16), 16)
        total = part[p.y, at, :].astype(F32) + near[0, at, :].astype(F32) + near[1, at, :].astype(F32)
        row = pl.ds(pl.multiple_of(p.y * SPAN + k * 16, 16), 16)
        stream = tokens[row, :].astype(F32) + total
        scale = lax.rsqrt(jnp.mean(stream * stream, axis=-1, keepdims=True) + epsilon)
        after_own[at, :] = stream
        normed_mid[p.y, at, :] = (stream * scale * gains[1:2, :]).astype(BF16)
        return carry

    lax.fori_loop(0, SPAN // 16, norm_mid, 0)
    spread = Spread(links, p, normed_mid)
    spread.start()
    mlp_gather.finish()
    spread.forward()
    spread.near()
    spread.far()
    mlp_gather.settle()
    for copy in saves:
        copy.wait()
    links.drain()


def params(collective_id):
    return pltpu.CompilerParams(
        collective_id=collective_id, has_side_effects=True, vmem_limit_bytes=VMEM_BYTES
    )


def vmem():
    return pl.BlockSpec(memory_space=pltpu.VMEM)


def smem():
    return pl.BlockSpec(memory_space=pltpu.SMEM)


def anyspace():
    return pl.BlockSpec(memory_space=pl.ANY)


def mix_forward(*operands):
    shape = jax.ShapeDtypeStruct
    tc = (TOKENS, CHAN)
    ext_shape = (ROWS, PAD + SPAN, CHAN)
    outs = [
        shape((4, 2, 4, 64, MIX_COLS), BF16),
        shape((4, 2, 4, 64, MLP_COLS), BF16),
        shape(tc, F32),
        shape(tc, F32),
        shape(ext_shape, F32),
        shape(tc, F32),
        shape(tc, F32),
        shape(tc, BF16),
        shape(tc, BF16),
        shape((TOKENS, WIDTH), BF16),
        shape((8, CHAN), F32),
        shape((8, CHAN), F32),
        shape((ROWS, SPAN, WIDTH), BF16),
        shape((SPAN, WIDTH), F32),
    ]
    scratch = [
        pltpu.VMEM((64, MLP_COLS), BF16),
        pltpu.VMEM((2, WIDTH), F32),
        pltpu.VMEM((8, CHAN), F32),
        pltpu.VMEM((4, 2, 4, 64, MIX_COLS), BF16),
        pltpu.VMEM((TOKENS, WIDTH), BF16),
        pltpu.VMEM((TOKENS, 2 * CHAN), F32),
        pltpu.VMEM(ext_shape, F32),
        pltpu.VMEM(tc, F32),
        pltpu.VMEM(tc, F32),
        pltpu.VMEM(tc, BF16),
        pltpu.VMEM(tc, F32),
        pltpu.VMEM(tc, F32),
        pltpu.VMEM(tc, F32),
        pltpu.VMEM(tc, BF16),
        pltpu.VMEM((ROWS, PAD, CHAN), F32),
        pltpu.VMEM((ROWS, PAD, CHAN), F32),
        pltpu.VMEM((8, CHAN), F32),
        pltpu.VMEM((8, 8, CHAN), F32),
        pltpu.VMEM((8, CHAN), F32),
        pltpu.VMEM((ROWS, SPAN, WIDTH), BF16),
        pltpu.VMEM((2, SPAN, HALF), BF16),
        pltpu.VMEM((2, SPAN, WIDTH), BF16),
        pltpu.SemaphoreType.DMA((16,)),
        pltpu.SemaphoreType.DMA((184,)),
        pltpu.SemaphoreType.DMA((184,)),
    ]
    return pl.pallas_call(
        mix_forward_kernel,
        out_shape=outs,
        in_specs=[vmem()] * 7 + [smem()] * 2 + [vmem()] * 3,
        out_specs=[anyspace()] * 12 + [vmem()] * 2,
        scratch_shapes=scratch,
        compiler_params=params(0),
        name="mix_forward",
    )(*operands)


def norm_back_rows(d_row, stream, gain_row):
    scale = lax.rsqrt(jnp.mean(stream * stream, axis=-1, keepdims=True) + epsilon)
    unit = stream * scale
    e = d_row * gain_row
    inner = jnp.mean(e * unit, axis=-1, keepdims=True)
    return scale * (e - unit * inner), d_row * unit


def own_sum(reduce, at):
    part, near = reduce.part, reduce.near
    return part[reduce.p.y, at, :].astype(F32) + near[0, at, :].astype(F32) + near[1, at, :].astype(F32)


def mlp_kernel(
    normed,
    upstream,
    gate_weights,
    up_weights,
    down_weights,
    states_in,
    d_gate_out,
    d_up_out,
    hidden_out,
    grads,
    states_out,
    normed_t,
    upstream_t,
    d_both,
):
    states_out[...] = states_in[...]

    @pl.when(pl.program_id(0) == 0)
    def _():
        def turn(n, carry):
            at = pl.ds(pl.multiple_of(n * 256, 256), 256)
            normed_t[at, :] = normed[:, at].T
            upstream_t[at, :] = upstream[:, at].T
            return carry

        lax.fori_loop(0, WIDTH // 256, turn, 0)

    gate = dot(normed[...], gate_weights[...])
    up = dot(normed[...], up_weights[...])
    d_hidden = dot(upstream[...], down_weights[...])
    act, slope = gelu_pair(gate)
    hidden = (act * up).astype(BF16)
    d_gate = (d_hidden * up * slope).astype(BF16)
    d_up = (d_hidden * act).astype(BF16)
    d_both[:, 0:CHUNK] = d_gate
    d_both[:, CHUNK : 2 * CHUNK] = d_up
    d_both[:, 2 * CHUNK :] = hidden
    d_gate_out[...] = d_gate
    d_up_out[...] = d_up
    hidden_out[...] = hidden

    def tile(n, carry):
        at = pl.ds(pl.multiple_of(n * 256, 256), 256)
        grads[at, 0 : 2 * CHUNK] = dot(normed_t[at, :], d_both[:, 0 : 2 * CHUNK]).astype(BF16)
        grads[at, 2 * CHUNK :] = dot(upstream_t[at, :], d_both[:, 2 * CHUNK :]).astype(BF16)
        return carry

    lax.fori_loop(0, WIDTH // 256, tile, 0, unroll=2)


def mlp_all(normed, upstream, weights, states):
    shape = jax.ShapeDtypeStruct
    whole = pl.BlockSpec((TOKENS, WIDTH), lambda f: (0, 0))
    part = lambda j: pl.BlockSpec((WIDTH, CHUNK), lambda f: (0, j * CHUNKS + f))
    block = pl.BlockSpec((WIDTH, 3 * CHUNK), lambda f: (0, f))
    column = pl.BlockSpec((TOKENS, CHUNK), lambda f: (0, f))
    row = pl.BlockSpec((1, SPAN, CHAN), lambda f: (jnp.minimum(f, ROWS - 1), 0, 0))
    return pl.pallas_call(
        mlp_kernel,
        grid=(CHUNKS,),
        out_shape=[shape((TOKENS, MLP), BF16)] * 3
        + [shape((WIDTH, MLP_COLS), BF16), shape((ROWS, SPAN, CHAN), F32)],
        in_specs=[whole, whole, part(0), part(1), part(2), row],
        out_specs=[column] * 3 + [block, row],
        scratch_shapes=[
            pltpu.VMEM((WIDTH, TOKENS), BF16),
            pltpu.VMEM((WIDTH, TOKENS), BF16),
            pltpu.VMEM((TOKENS, 3 * CHUNK), BF16),
        ],
        compiler_params=pltpu.CompilerParams(vmem_limit_bytes=VMEM_BYTES),
        cost_estimate=pl.CostEstimate(
            flops=12 * TOKENS * WIDTH * MLP, bytes_accessed=4 * WIDTH * MLP_COLS, transcendentals=TOKENS * MLP
        ),
        name="mlp_all",
    )(normed, upstream, weights, weights, weights, states)


class Scatter:
    def __init__(self, links, place, grads, sib, far, near, half_a, half_b, far_2, near_2):
        self.links, self.p = links, place
        self.grads, self.sib = grads, sib
        self.far, self.near, self.far_2, self.near_2 = far, near, far_2, near_2
        self.half_a, self.half_b = half_a, half_b
        self.sib_keys = {}

    def give(self, xx):
        p = self.p
        self.sib_keys[xx] = self.links.go(self.grads.at[xx, 1 - p.c], self.sib.at[xx], p.SIB)

    def take(self, xx):
        p, sib, grads = self.p, self.sib, self.grads
        self.links.arrived(sib.at[xx], self.sib_keys[xx], p.SIB)

        def one(j, carry):
            sib[xx, j] = (sib[xx, j].astype(F32) + grads[xx, p.c, j].astype(F32)).astype(BF16)
            return carry

        lax.fori_loop(0, 4, one, 0)

    def _ring(self, view, i, right, left, far, near, base):
        links = self.links
        ir, il, i2 = lax.rem(i + 1, 4), lax.rem(i + 3, 4), lax.rem(i + 2, 4)
        a, b = pl.ds(base, 16), pl.ds(base + 16, 16)
        na, nb = pl.ds(0, 16), pl.ds(16, 16)
        k0 = links.go(view(i2, a), far.at[0], right)
        k1 = links.go(view(i2, b), far.at[1], left)
        k2 = links.go(view(ir, b), near.at[0, :, nb], right)
        k3 = links.go(view(il, a), near.at[1, :, na], left)
        keys = []

        def merge():
            for way, k, row, at, source, target, to in (
                (0, k0, ir, a, left, right, na),
                (1, k1, il, b, right, left, nb),
            ):
                links.arrived(far.at[way], k, source)
                mine = view(row, at)

                def one(j, carry):
                    far[way, j] = (far[way, j].astype(F32) + mine[j].astype(F32)).astype(BF16)
                    return carry

                lax.fori_loop(0, far.shape[1], one, 0)
                keys.append(links.go(far.at[way], near.at[way, :, to], target))

        def settle():
            links.arrived(near.at[0, :, nb], k2, left)
            links.arrived(near.at[1, :, na], k3, right)
            links.arrived(near.at[0, :, na], keys[0], left)
            links.arrived(near.at[1, :, nb], keys[1], right)

        return merge, settle

    def first(self):
        p, sib = self.p, self.sib
        self.x_ring = self._ring(lambda j, r: sib.at[j, :, r], p.x, p.XR, p.XL, self.far.at[0], self.near.at[0], 0)
        self.z_ring = self._ring(lambda j, r: sib.at[:, j, r], p.z, p.ZR, p.ZL, self.far.at[1], self.near.at[1], 32)

    def merge(self):
        self.x_ring[0]()
        self.z_ring[0]()

    def turn(self):
        p, sib, near = self.p, self.sib, self.near
        self.x_ring[1]()

        def one_a(j, carry):
            total = sib[p.x, j, 0:32].astype(F32) + near[0, 0, j].astype(F32) + near[0, 1, j].astype(F32)
            self.half_a[j, 0] = total.astype(BF16)
            return carry

        lax.fori_loop(0, 4, one_a, 0)
        half_a, half_b = self.half_a, self.half_b
        self.ring_a = self._ring(
            lambda j, r: half_a.at[j, :, r], p.z, p.ZR, p.ZL, self.far_2.at[0], self.near_2.at[0], 0
        )
        self.z_ring[1]()

        def one_b(j, carry):
            total = sib[j, p.z, 32:64].astype(F32) + near[1, 0, j].astype(F32) + near[1, 1, j].astype(F32)
            self.half_b[j, 0] = total.astype(BF16)
            return carry

        lax.fori_loop(0, 4, one_b, 0)
        self.ring_b = self._ring(
            lambda j, r: half_b.at[j, :, r], p.x, p.XR, p.XL, self.far_2.at[1], self.near_2.at[1], 0
        )

    def merge_2(self):
        self.ring_a[0]()
        self.ring_b[0]()

    def finish(self, store):
        p, near = self.p, self.near_2
        self.ring_a[1]()
        store(0, self.half_a[p.z, 0].astype(F32) + near[0, 0, 0].astype(F32) + near[0, 1, 0].astype(F32))
        self.ring_b[1]()
        store(32, self.half_b[p.x, 0].astype(F32) + near[1, 0, 0].astype(F32) + near[1, 1, 0].astype(F32))

    @staticmethod
    def scratch(columns):
        return [
            pltpu.VMEM((4, 4, 64, columns), BF16),
            pltpu.VMEM((2, 2, 4, 16, columns), BF16),
            pltpu.VMEM((2, 2, 4, 32, columns), BF16),
            pltpu.VMEM((4, 1, 32, columns), BF16),
            pltpu.VMEM((4, 1, 32, columns), BF16),
            pltpu.VMEM((2, 2, 1, 16, columns), BF16),
            pltpu.VMEM((2, 2, 1, 32, columns), BF16),
        ]


def back_kernel(
    hbm_d_gate,
    hbm_d_up,
    hbm_hidden,
    mlp_full,
    mix_full,
    hbm_saved_0,
    hbm_saved_1,
    hbm_saved_2,
    hbm_saved_3,
    hbm_saved_4,
    hbm_saved_5,
    hbm_saved_6,
    hbm_saved_7,
    hbm_saved_8,
    entering,
    tokens,
    upstream,
    gain_rows,
    vectors,
    gate_w,
    doc_start,
    grad_tokens,
    block_out,
    grad_mix,
    small_sums,
    block_sums,
    gain_sums,
    hidden,
    states,
    pre,
    ext,
    decay_g,
    input_g,
    conv_low,
    mixed,
    normed_in,
    after_own,
    work,
    small_work,
    own_tokens,
    own_upstream,
    mid_part,
    out_part,
    d_after_low,
    d_after_own,
    gain_mid,
    d_mixed,
    tail_a,
    d_gates,
    d_both,
    small,
    rim_send,
    rim_recv,
    totals,
    totals_in,
    after,
    far_a,
    near_a,
    far_b,
    near_b,
    *rest,
):
    n_scatter = 7
    mix_scratch, rest = rest[:n_scatter], rest[n_scatter:]
    small_scratch, rest = rest[:n_scatter], rest[n_scatter:]
    saved = (
        (hbm_saved_0, states),
        (hbm_saved_1, pre),
        (hbm_saved_2, ext),
        (hbm_saved_3, decay_g),
        (hbm_saved_4, input_g),
        (hbm_saved_5, conv_low),
        (hbm_saved_6, mixed),
        (hbm_saved_7, normed_in),
        (hbm_saved_8, after_own),
    )
    back_steps(
        (hbm_d_gate, hbm_d_up, hbm_hidden), saved, mlp_full, mix_full, hidden, states, pre, ext, decay_g, input_g,
        conv_low, entering, mixed, normed_in, tokens, upstream, after_own, gain_rows, vectors, gate_w, doc_start,
        grad_tokens, block_out, grad_mix, small_sums, block_sums, gain_sums,
        work, small_work, own_tokens, own_upstream, mid_part, out_part, d_after_low, d_after_own, gain_mid,
        d_mixed, tail_a, d_gates, d_both, small, rim_send, rim_recv, totals, totals_in, after,
        far_a, near_a, far_b, near_b, mix_scratch, small_scratch, *rest,
    )


def back_steps(
    mlp_saved, saved, mlp_full, mix_full, hidden, states, pre, ext, decay_g, input_g,
    conv_low, entering, mixed, normed_in, tokens, upstream, after_own, gain_rows, vectors, gate_w, doc_start,
    grad_tokens, block_out, grad_mix, small_sums, block_sums, gain_sums,
    work, small_work, own_tokens, own_upstream, mid_part, out_part, d_after_low, d_after_own, gain_mid,
    d_mixed, tail_a, d_gates, d_both, small, rim_send, rim_recv, totals, totals_in, after,
    far_a, near_a, far_b, near_b, mix_scratch, small_scratch,
    small_all,
    gain_in,
    gain_y,
    gain_s,
    gain_z,
    local,
    tiles,
    send,
    recv,
):
    p = Place()
    links = Links(send, recv)
    sib = mix_scratch[0]
    early = (
        pltpu.make_async_copy(mlp_saved[0], sib.at[pl.ds(0, 2), :, :, pl.ds(0, MLP)], local.at[0]),
        pltpu.make_async_copy(mlp_saved[1], sib.at[pl.ds(2, 2), :, :, pl.ds(0, MLP)], local.at[1]),
    )
    for copy in early:
        copy.start()

    def weight_tile(n, j, slot):
        source = mlp_full.at[n // 2, n % 2, :, :, pl.ds(j * MLP, MLP)]
        return pltpu.make_async_copy(source, work.at[slot // 2, slot % 2, :, :, pl.ds(0, MLP)], tiles.at[slot])

    fetched = {}

    def fetch(n):
        for j in range(2):
            fetched[n, j] = weight_tile(n, j, (2 * n + j) % 8)
            fetched[n, j].start()

    for n in range(3):
        fetch(n)
    hidden_load = pltpu.make_async_copy(mlp_saved[2], hidden, local.at[2])
    hidden_load.start()
    saved_loads = [
        pltpu.make_async_copy(source, target, local.at[3 + k]) for k, (source, target) in enumerate(saved)
    ]
    load_tokens = pltpu.make_async_copy(tokens.at[p.y], own_tokens, local.at[12])
    load_tokens.start()
    load_upstream = pltpu.make_async_copy(upstream.at[p.y], own_upstream, local.at[13])
    load_upstream.start()
    others_y = [{"tensor": lax.rem(p.y + d, 4)} for d in (1, 2, 3)]
    others_z = [{"dp": lax.rem(p.z + d, 4)} for d in (1, 2, 3)]
    greet([p.seq_at(d) for d in range(1, 8)] + others_y + others_z)
    middle = Reduce(links, p, mid_part, far_a, near_a)
    for copy in early:
        copy.wait()

    def tile_of(slot):
        return work[slot // 2, slot % 2, :, :, 0:MLP].reshape(256, MLP)

    for n in range(8):
        if n + 3 < 8:
            fetch(n + 3)
        if n == 4:
            middle.send_first()
        for j in range(2):
            fetched[n, j].wait()
        at = slice(n * 256, (n + 1) * 256)
        product = dot_nt(sib[0:2, :, :, 0:MLP].reshape(TOKENS, MLP), tile_of(2 * n % 8)) + dot_nt(
            sib[2:4, :, :, 0:MLP].reshape(TOKENS, MLP), tile_of((2 * n + 1) % 8)
        )
        mid_part[:, :, at] = product.astype(BF16).reshape(ROWS, SPAN, 256)
    middle.send_second()
    downs = [weight_tile(n, 2, n) for n in range(8)]
    for copy in downs + saved_loads:
        copy.start()
    hidden_load.wait()
    for copy in downs:
        copy.wait()

    def out_product(n, carry):
        weights = work[lax.div(n, 2), lax.rem(n, 2), :, :, 0:MLP].reshape(256, MLP)
        product = dot_nt(hidden[...], weights).astype(BF16)
        out_part[:, :, pl.ds(pl.multiple_of(n * 256, 256), 256)] = product.reshape(ROWS, SPAN, 256)
        return carry

    lax.fori_loop(0, 4, out_product, 0)
    middle.merge()
    lax.fori_loop(4, 8, out_product, 0)
    load = pltpu.make_async_copy(mix_full, work, local.at[14])
    load.start()
    for copy in saved_loads:
        copy.wait()
    gain_mid[...] = jnp.zeros_like(gain_mid)
    gain_1 = gain_rows[1:2, :].astype(F32)
    load_upstream.wait()
    middle.settle()

    def middle_rows(k, carry):
        at = pl.ds(pl.multiple_of(k * 16, 16), 16)
        through, share = norm_back_rows(own_sum(middle, at), after_own[at, :], gain_1)
        gain_mid[...] += share[0:8] + share[8:16]
        total = own_upstream[at, :].astype(F32) + through
        d_after_own[at, :] = total
        d_after_low[p.y, at, :] = total.astype(BF16)
        return carry

    lax.fori_loop(0, SPAN // 16, middle_rows, 0)
    links.sent([middle.k0, middle.k1, middle.k2, middle.k3, middle.k4, middle.k5])
    spread_c = Spread(links, p, d_after_low)
    spread_c.start()
    load.wait()
    rows_low = d_after_low.reshape(TOKENS, WIDTH)

    def mixed_row(row):
        rows = pl.ds(pl.multiple_of(row * SPAN, SPAN), SPAN)
        for start, size in ((0, 256), (256, 256), (512, 128)):
            weights = work[:, :, :, :, 2 * CHAN + start : 2 * CHAN + start + size].reshape(WIDTH, size)
            d_mixed[rows, start : start + size] = dot(d_after_low[row], weights)

    mixed_row(p.y)
    spread_c.forward()
    spread_c.near()
    mixed_row(p.yl)
    mixed_row(p.yr)
    spread_c.far()
    ahead = Reduce(links, p, out_part, far_b, near_b)
    ahead.send_first()
    ahead.send_second()
    mixed_row(p.y2)
    small[...] = jnp.zeros_like(small)
    totals[...] = jnp.zeros_like(totals)
    gain_in[...] = jnp.zeros_like(gain_in)
    offset = p.s * SPAN

    def chunk(i):
        r, g = lax.rem(i, ROWS), lax.div(i, ROWS)
        at = pl.ds(pl.multiple_of(g * LANES, LANES), LANES)
        rows = pl.ds(pl.multiple_of(r * SPAN, SPAN), SPAN)
        row = lax.broadcasted_iota(jnp.int32, (SPAN, LANES), 0)
        return r, g, at, rows, row

    def states_back(i, carry):
        r, g, at, rows, row = chunk(i)
        d_chunk = d_mixed[rows, at]
        value, slope = gelu_pair(pre[rows, at])
        d_both[rows, at] = (d_chunk * states[rows, at] * slope).astype(BF16)
        decay_now = jnp.exp(decay_g[rows, at] * vectors[7:8, at])
        carried = jnp.where(offset + row == doc_start[r], 0.0, decay_now)
        following = jnp.where(row == SPAN - 1, 1.0, pltpu.roll(carried, SPAN - 1, 0))
        a, b, first_a, first_b = row_scan(following, d_chunk * value, True)
        tail_a[rows, at] = a
        d_mixed[rows, at] = b
        put_pair(totals, at, r, carried[0:1] * first_a, carried[0:1] * first_b)
        return carry

    lax.fori_loop(0, ROWS * GROUPS, states_back, 0)
    keys = [links.go(totals, totals_in.at[p.s], p.seq_at(d)) for d in range(1, 8)]
    ahead.merge()
    state = jnp.zeros((ROWS, CHAN), F32)
    for d in range(1, 8):
        links.arrived(totals_in.at[p.seq_at(-d)["seq"]], keys[d - 1], p.seq_at(-d))
    totals_in[p.s] = totals[...]
    for source in range(7, 0, -1):
        both = totals_in[source]
        state = jnp.where(source > p.s, both[0:ROWS] * state + both[ROWS:], state)
    after[0:ROWS, :] = state
    after[ROWS:, :] = jnp.zeros((8 - ROWS, CHAN), F32)

    def gates_back(i, carry):
        r, g, at, rows, row = chunk(i)
        grads = d_mixed[rows, at] + tail_a[rows, at] * take_row(after, at, r)
        held = states[rows, at]
        previous = jnp.where(row == 0, take_row(entering, at, r), pltpu.roll(held, 1, 0))
        gate_d, gate_i = decay_g[rows, at], input_g[rows, at]
        rate = vectors[7:8, at]
        decay_now = jnp.exp(gate_d * rate)
        headroom = 1.0 - decay_now * decay_now
        root = jnp.sqrt(jnp.maximum(headroom, root_floor))
        conv = conv_low[rows, at].astype(F32)
        d_decay = jnp.where(offset + row == doc_start[r], 0.0, grads * previous) - jnp.where(
            headroom > root_floor, grads * gate_i * conv * decay_now / root, 0.0
        )
        d_log = d_decay * decay_now
        d_zero = d_log * rate * gate_d * (1.0 - gate_d)
        fed = grads * root
        d_one = fed * conv * gate_i * (1.0 - gate_i)
        d_gates[rows, pl.ds(pl.multiple_of(g * LANES, LANES), LANES)] = d_zero.astype(BF16)
        d_gates[rows, pl.ds(pl.multiple_of(CHAN + g * LANES, LANES), LANES)] = d_one.astype(BF16)
        tail_a[rows, at] = fed * gate_i
        small[5:6, at] += jnp.sum(d_zero, axis=0, keepdims=True)
        small[6:7, at] += jnp.sum(d_one, axis=0, keepdims=True)
        small[7:8, at] += jnp.sum(d_log * (-rate_scale * gate_d), axis=0, keepdims=True)
        return carry

    lax.fori_loop(0, ROWS * GROUPS, gates_back, 0)

    def ahead_rows(k, carry):
        at = pl.ds(pl.multiple_of(k * 16, 16), 16)
        block_out[p.y, at, :] = (after_own[at, :] + own_sum(ahead, at)).astype(BF16)
        return carry

    spread_b = Spread(links, p, block_out)

    d_conv = tail_a
    held = None
    for g in range(GROUPS):
        total = d_conv[:, g * LANES : (g + 1) * LANES]
        if held is not None:
            total = total + held
        if g < HEADS:
            lo = g * LANES
            product = dot_nt(d_gates[:, lo : lo + 256], gate_w[0, g]) + dot_nt(
                d_gates[:, CHAN + lo : CHAN + lo + 256], gate_w[1, g]
            )
            total = total + product[:, :LANES]
            held = product[:, LANES:]
        d_conv[:, g * LANES : (g + 1) * LANES] = total

    body = d_mixed

    def conv_back(i, carry):
        r, g, at, rows, row = chunk(i)
        d_chunk = d_conv[rows, at]
        begin = doc_start[r]
        place = offset + row
        here = place >= begin
        head = jnp.zeros((8, LANES), F32)
        total = jnp.zeros((SPAN, LANES), F32)
        for k in range(CONV):
            before = CONV - 1 - k
            same = (place - before >= begin) == here
            kept = jnp.where(same, d_chunk, 0.0)
            value = ext[r, PAD - before : PAD - before + SPAN, at]
            small[k : k + 1, at] += jnp.sum(kept * value, axis=0, keepdims=True)
            term = kept * vectors[k : k + 1, at]
            if before:
                total = total + jnp.where(row < SPAN - before, pltpu.roll(term, SPAN - before, 0), 0.0)
                head = head + jnp.where(
                    row[0:8] >= 8 - before, pltpu.roll(term[0:8], 8 - before, 0), 0.0
                )
            else:
                total = total + term
        small[4:5, at] += jnp.sum(d_chunk, axis=0, keepdims=True)
        body[rows, at] = total
        rim_send[r, :, at] = head
        return carry

    lax.fori_loop(0, ROWS * GROUPS, conv_back, 0)
    k_rim = links.go(rim_send, rim_recv, p.seq_at(-1))

    def blocks(j, h):
        lo = h * LANES
        product = dot_tn(conv_low[:, lo : lo + 256], d_gates[:, j * CHAN + lo : j * CHAN + lo + 256])
        for q in range(BLK // 32):
            row = (j * HEADS + h) * BLK + 32 * q
            n, inner = row // 64, row % 64
            piece = product[32 * (h + q) : 32 * (h + q + 1), :].astype(BF16)
            small_work[n // 8, (n // 4) % 2, n % 4, inner : inner + 32, :] = piece

    for j in range(2):
        for h in range(HEADS):
            blocks(j, h)
    for n in range(20, 32):
        small_work[n // 8, (n // 4) % 2, n % 4] = jnp.zeros((64, SMALL), BF16)
    for k, n in enumerate((20, 21, 22)):
        width = min(256, CHAN - 256 * k)
        both = jnp.concatenate([small[:, 256 * k : 256 * k + width], jnp.zeros((8, width), F32)], axis=0)
        small_work[n // 8, (n // 4) % 2, n % 4, 0:16, 0:width] = both.astype(BF16)
    small_scatter = Scatter(links, p, small_work, *small_scratch)
    for xx in range(4):
        small_scatter.give(xx)
    links.arrived(rim_recv, k_rim, p.seq_at(1))
    for r in range(ROWS):
        last = r * SPAN + SPAN - 8
        body[last : last + 8, :] += jnp.where(p.s == 7, 0.0, rim_recv[r])
    for r in range(ROWS):
        d_both[r * SPAN : (r + 1) * SPAN, CHAN:] = body[r * SPAN : (r + 1) * SPAN, :].astype(BF16)

    def first_part(n, carry):
        weights = work[lax.div(n, 2), lax.rem(n, 2), :, :, 0 : 2 * CHAN].reshape(256, 2 * CHAN)
        product = dot_nt(d_both[...], weights).astype(BF16)
        d_first[:, :, pl.ds(pl.multiple_of(n * 256, 256), 256)] = product.reshape(ROWS, SPAN, 256)
        return carry

    d_first = mid_part
    back = Reduce(links, p, d_first, far_a, near_a)
    ahead.settle()
    lax.fori_loop(0, SPAN // 16, ahead_rows, 0)
    spread_b.start_first()
    lax.fori_loop(0, 4, first_part, 0)
    back.send_first()
    lax.fori_loop(4, 8, first_part, 0)
    back.send_second()
    for xx in range(4):
        small_scatter.take(xx)
    small_scatter.first()

    def weight_grads(n):
        at = pl.ds(pl.multiple_of(n * 256, 256), 256)
        to = work.at[lax.div(n, 2), lax.rem(n, 2)]
        both = dot_tn(normed_in[:, at], d_both[...])
        to[:, :, 0 : 2 * CHAN] = both.astype(BF16).reshape(4, 64, 2 * CHAN)
        out = dot_tn(rows_low[:, at], mixed[...])
        to[:, :, 2 * CHAN : MIX_COLS] = out.astype(BF16).reshape(4, 64, CHAN)

    scatter = Scatter(links, p, work, *mix_scratch)

    def give(xx, carry):
        weight_grads(xx * 2 + 1 - p.c)
        return carry

    def keep(xx, carry):
        weight_grads(xx * 2 + p.c)
        return carry

    lax.fori_loop(0, 4, give, 0)
    for xx in range(4):
        scatter.give(xx)
    small_scatter.merge()
    back.merge()
    spread_b.start_second()
    lax.fori_loop(0, 4, keep, 0)
    small_scatter.turn()
    for xx in range(4):
        scatter.take(xx)
    scatter.first()
    small_scatter.merge_2()
    back.settle()
    load_tokens.wait()
    gain = gain_rows[0:1, :].astype(F32)

    def back_rows(k, carry):
        at = pl.ds(pl.multiple_of(k * 16, 16), 16)
        through, share = norm_back_rows(own_sum(back, at), own_tokens[at, :].astype(F32), gain)
        gain_in[...] += share[0:8] + share[8:16]
        grad_tokens[p.y, at, :] = (d_after_own[at, :] + through).astype(BF16)
        return carry

    lax.fori_loop(0, SPAN // 16, back_rows, 0)
    spread_a = Spread(links, p, grad_tokens)
    spread_a.start()
    spread_b.forward()
    gain_y[p.y] = jnp.concatenate(
        [jnp.sum(gain_in[...], axis=0, keepdims=True), jnp.sum(gain_mid[...], axis=0, keepdims=True)], axis=0
    )
    y_keys = [links.go(gain_y.at[p.y], gain_y.at[p.y], device) for device in others_y]

    def store_small(base, value):
        small_all[p.x, p.c, p.z, base : base + 32, :] = value.astype(BF16)

    small_scatter.finish(store_small)
    small_gather = Gather(links, p, small_all, 128)
    small_gather.first()
    scatter.merge()
    for d in (1, 2, 3):
        links.arrived(gain_y.at[lax.rem(p.y + 4 - d, 4)], y_keys[d - 1], others_y[0])
    gain_z[p.z] = gain_y[0] + gain_y[1] + gain_y[2] + gain_y[3]
    z_keys = [links.go(gain_z.at[p.z], gain_z.at[p.z], device) for device in others_z]
    small_gather.middle()
    small_gather.finish()
    small_gather.second()
    spread_a.forward()
    scatter.turn()
    for d in (1, 2, 3):
        links.arrived(gain_z.at[lax.rem(p.z + 4 - d, 4)], z_keys[d - 1], others_z[0])
    gain_s[p.s] = gain_z[0] + gain_z[1] + gain_z[2] + gain_z[3]
    s_keys = [links.go(gain_s.at[p.s], gain_s.at[p.s], p.seq_at(d)) for d in range(1, 8)]
    small_gather.middle()
    small_gather.finish()
    scatter.merge_2()
    for d in range(1, 8):
        links.arrived(gain_s.at[p.seq_at(-d)["seq"]], s_keys[d - 1], p.seq_at(-d))
    total = gain_s[0]
    for s in range(1, 8):
        total = total + gain_s[s]
    gain_sums[...] = total
    spread_b.near()
    spread_b.far()
    small_gather.settle()
    for k, n in enumerate((20, 21, 22)):
        width = min(256, CHAN - 256 * k)
        value = small_all[n // 8, (n // 4) % 2, n % 4, 0:16, 0:width].astype(F32)
        small_sums[:, 256 * k : 256 * k + width] = value[0:8]
    for n in range(20):
        value = small_all[n // 8, (n // 4) % 2, n % 4].astype(F32)
        block_sums[64 * n : 64 * (n + 1), :] = value

    def store(base, value):
        grad_mix[base : base + 32, :] = value

    scatter.finish(store)
    spread_a.near()
    spread_a.far()
    links.drain()


def back_all(*operands):
    shape = jax.ShapeDtypeStruct
    tc = (TOKENS, CHAN)
    pair = [pltpu.VMEM((2, SPAN, HALF), BF16), pltpu.VMEM((2, SPAN, WIDTH), BF16)]
    return pl.pallas_call(
        back_kernel,
        out_shape=[
            shape((ROWS, SPAN, WIDTH), BF16),
            shape((ROWS, SPAN, WIDTH), BF16),
            shape((64, MIX_COLS), F32),
            shape((8, CHAN), F32),
            shape((2 * HEADS * BLK, 256), F32),
            shape((2, WIDTH), F32),
        ],
        in_specs=[anyspace()] * 14 + [vmem()] + [anyspace()] * 2 + [vmem()] * 3 + [smem()],
        out_specs=[vmem()] * 6,
        scratch_shapes=[
            pltpu.VMEM((TOKENS, MLP), BF16),
            pltpu.VMEM(tc, F32),
            pltpu.VMEM(tc, F32),
            pltpu.VMEM((ROWS, PAD + SPAN, CHAN), F32),
            pltpu.VMEM(tc, F32),
            pltpu.VMEM(tc, F32),
            pltpu.VMEM(tc, BF16),
            pltpu.VMEM(tc, BF16),
            pltpu.VMEM((TOKENS, WIDTH), BF16),
            pltpu.VMEM((SPAN, WIDTH), F32),
            pltpu.VMEM((4, 2, 4, 64, MIX_COLS), BF16),
            pltpu.VMEM((4, 2, 4, 64, SMALL), BF16),
            pltpu.VMEM((SPAN, WIDTH), BF16),
            pltpu.VMEM((SPAN, WIDTH), BF16),
            pltpu.VMEM((ROWS, SPAN, WIDTH), BF16),
            pltpu.VMEM((ROWS, SPAN, WIDTH), BF16),
            pltpu.VMEM((ROWS, SPAN, WIDTH), BF16),
            pltpu.VMEM((SPAN, WIDTH), F32),
            pltpu.VMEM((8, WIDTH), F32),
            pltpu.VMEM(tc, F32),
            pltpu.VMEM(tc, F32),
            pltpu.VMEM((TOKENS, 2 * CHAN), BF16),
            pltpu.VMEM((TOKENS, 2 * CHAN), BF16),
            pltpu.VMEM((8, CHAN), F32),
            pltpu.VMEM((ROWS, PAD, CHAN), F32),
            pltpu.VMEM((ROWS, PAD, CHAN), F32),
            pltpu.VMEM((8, CHAN), F32),
            pltpu.VMEM((8, 8, CHAN), F32),
            pltpu.VMEM((8, CHAN), F32),
        ]
        + pair * 2
        + Scatter.scratch(MIX_COLS)
        + Scatter.scratch(SMALL)
        + [
            pltpu.VMEM((4, 2, 4, 64, SMALL), BF16),
            pltpu.VMEM((8, WIDTH), F32),
            pltpu.VMEM((4, 2, WIDTH), F32),
            pltpu.VMEM((8, 2, WIDTH), F32),
            pltpu.VMEM((4, 2, WIDTH), F32),
            pltpu.SemaphoreType.DMA((15,)),
            pltpu.SemaphoreType.DMA((8,)),
            pltpu.SemaphoreType.DMA((184,)),
            pltpu.SemaphoreType.DMA((184,)),
        ],
        compiler_params=params(2),
        name="back_all",
    )(*operands)


def finish_kernel(
    block_in,
    tokens_in,
    mix_sum,
    small,
    blocks_in,
    gains_in,
    mlp_sum,
    block_out,
    grad_tokens,
    grad_gains,
    grad_mix_in,
    grad_mix_out,
    grad_conv,
    grad_blocks,
    grad_bias,
    grad_mlp_in,
    grad_mlp_out,
):
    step = pl.program_id(0)
    block_out[...] = block_in[...]
    grad_tokens[...] = tokens_in[...]
    for h in range(HEADS):

        @pl.when(step == h)
        def _():
            for j in range(2):
                grad_blocks[j, 0] = blocks_in[j, 0, :, 32 * h : 32 * h + BLK]

    @pl.when(step == 0)
    def _():
        grad_gains[...] = gains_in[...]
        for j in range(2):
            grad_mix_in[j] = mix_sum[:, j * CHAN : (j + 1) * CHAN]
        grad_mix_out[...] = mix_sum[:, 2 * CHAN :]
        grad_conv[...] = small[0:CONV, :]
        grad_bias[...] = small[CONV + 1 : CONV + 3, :]
        for f in range(CHUNKS):
            lo, at = 3 * f * CHUNK, pl.ds(f * CHUNK, CHUNK)
            for j in range(2):
                grad_mlp_in[j, :, at] = mlp_sum[:, lo + j * CHUNK : lo + (j + 1) * CHUNK].astype(F32)
            grad_mlp_out[:, at] = mlp_sum[:, lo + 2 * CHUNK : lo + 3 * CHUNK].astype(F32)


def finish(*operands):
    shape = jax.ShapeDtypeStruct
    row = lambda width: pl.BlockSpec((1, SPAN, width), lambda i: (i, 0, 0))
    whole = lambda *dims: pl.BlockSpec(dims, lambda i: (0,) * len(dims))
    head = lambda width: pl.BlockSpec((2, 1, BLK, width), lambda i: (0, i, 0, 0))
    return pl.pallas_call(
        finish_kernel,
        grid=(ROWS,),
        out_shape=[
            shape((ROWS, SPAN, WIDTH), BF16),
            shape((ROWS, SPAN, WIDTH), BF16),
            shape((2, WIDTH), F32),
            shape((2, 64, CHAN), F32),
            shape((64, CHAN), F32),
            shape((CONV, CHAN), F32),
            shape((2, HEADS, BLK, BLK), F32),
            shape((2, CHAN), F32),
            shape((2, 64, MLP), F32),
            shape((64, MLP), F32),
        ],
        in_specs=[
            row(WIDTH),
            row(WIDTH),
            whole(64, MIX_COLS),
            whole(8, CHAN),
            head(256),
            whole(2, WIDTH),
            whole(64, MLP_COLS),
        ],
        out_specs=[
            row(WIDTH),
            row(WIDTH),
            whole(2, WIDTH),
            whole(2, 64, CHAN),
            whole(64, CHAN),
            whole(CONV, CHAN),
            head(BLK),
            whole(2, CHAN),
            whole(2, 64, MLP),
            whole(64, MLP),
        ],
        compiler_params=pltpu.CompilerParams(vmem_limit_bytes=VMEM_BYTES),
        name="finish",
    )(*operands)


def per_device(
    tokens,
    init_state,
    conv_state,
    fresh_rows,
    doc_start,
    norm_gains,
    mix_in,
    mix_out,
    conv_weight,
    conv_bias,
    gate_blocks,
    gate_bias,
    decay_param,
    mlp_in,
    mlp_out,
    cotangent,
):
    gate_w = jnp.stack(
        [
            jnp.pad(gate_blocks[:, h], ((0, 0), (32 * h, 96 - 32 * h), (32 * h, 96 - 32 * h)))
            for h in range(HEADS)
        ],
        axis=1,
    )
    raw_vectors = jnp.concatenate([conv_weight, conv_bias[None], gate_bias, decay_param[None]], axis=0)
    (
        mix_full,
        mlp_full,
        states,
        pre,
        ext,
        decay_g,
        input_g,
        conv_low,
        mixed,
        normed_in,
        entering,
        vectors,
        normed_mid,
        after_own,
    ) = mix_forward(
        tokens.reshape(TOKENS, WIDTH),
        mix_in,
        mix_out.T,
        mlp_in,
        mlp_out.T,
        init_state,
        conv_state.transpose(1, 0, 2),
        fresh_rows,
        doc_start,
        norm_gains,
        raw_vectors,
        gate_w,
    )
    d_gate, d_up, hidden, grad_mlp, states_out = mlp_all(
        normed_mid.reshape(TOKENS, WIDTH),
        cotangent.reshape(TOKENS, WIDTH),
        mlp_full.reshape(WIDTH, MLP_COLS),
        states.reshape(ROWS, SPAN, CHAN),
    )
    grad_mlp = lax.psum_scatter(grad_mlp, ("seq", "dp"), scatter_dimension=0, tiled=True)
    grad_tokens, block_out, grad_mix, small, blocks, grad_gains = back_all(
        d_gate.reshape(2, 4, 64, MLP),
        d_up.reshape(2, 4, 64, MLP),
        hidden,
        mlp_full,
        mix_full,
        states,
        pre,
        ext,
        decay_g,
        input_g,
        conv_low,
        mixed,
        normed_in,
        after_own,
        entering,
        tokens,
        cotangent,
        norm_gains,
        vectors,
        gate_w,
        doc_start,
    )
    (
        block_out,
        grad_tokens,
        grad_gains,
        grad_mix_in,
        grad_mix_out,
        grad_conv,
        grad_blocks,
        grad_bias,
        grad_mlp_in,
        grad_mlp_out,
    ) = finish(
        block_out,
        grad_tokens,
        grad_mix,
        small,
        blocks.reshape(2, HEADS, BLK, 256),
        grad_gains,
        grad_mlp,
    )
    return (
        block_out,
        states_out,
        grad_tokens,
        grad_gains,
        grad_mix_in,
        grad_mix_out.T,
        grad_conv,
        small[CONV],
        grad_blocks,
        grad_bias,
        small[CONV + 3] * jax.nn.sigmoid(decay_param.astype(F32)),
        grad_mlp_in,
        grad_mlp_out.T,
    )


def solution(mesh):
    in_specs = (
        P("dp", "seq", None),
        P("dp", "tensor"),
        P("dp", None, "tensor"),
        P("dp"),
        P("dp"),
        P(),
        P(None, ("seq", "dp"), "tensor"),
        P("tensor", ("seq", "dp")),
        P(None, "tensor"),
        P("tensor"),
        P(None, "tensor", None, None),
        P(None, "tensor"),
        P("tensor"),
        P(None, ("seq", "dp"), "tensor"),
        P("tensor", ("seq", "dp")),
        P("dp", "seq", None),
    )
    out_specs = (
        P("dp", "seq", None),
        P("dp", "seq", "tensor"),
        P("dp", "seq", None),
        P(),
        P(None, ("seq", "dp"), "tensor"),
        P("tensor", ("seq", "dp")),
        P(None, "tensor"),
        P("tensor"),
        P(None, "tensor", None, None),
        P(None, "tensor"),
        P("tensor"),
        P(None, ("seq", "dp"), "tensor"),
        P("tensor", ("seq", "dp")),
    )
    return jax.shard_map(
        per_device, mesh=mesh, in_specs=in_specs, out_specs=out_specs, check_vma=False
    )
```

```python
import functools

import jax
import jax.numpy as jnp
from jax import lax
from jax.experimental import pallas as pl
from jax.experimental.pallas import tpu as pltpu
from jax.sharding import PartitionSpec as P

MESH = pl.DeviceIdType.MESH
F32 = jnp.float32
BF16 = jnp.bfloat16
VMEM_BYTES = 60 * 2**20

CONV = 4
ROWS = 4
SPAN = 128
TOKENS = ROWS * SPAN
WIDTH = 2048
CHAN = 640
HEADS = 4
BLK = 160
MLP = 1536
MIX_COLS = 3 * CHAN
MLP_COLS = 3 * MLP
MLP_CUT = 2304
CHUNK = 256
CHUNKS = MLP // CHUNK
SMALL = 256
LANES = 128
GROUPS = CHAN // LANES
PAD = 8

epsilon = 1e-06
root_floor = 0.001
rate_scale = 8.0


class Place:
    def __init__(self):
        self.s = lax.axis_index("seq")
        self.z = lax.axis_index("dp")
        self.y = lax.axis_index("tensor")
        self.x, self.c = lax.div(self.s, 2), lax.rem(self.s, 2)
        x, c, z, y = self.x, self.c, self.z, self.y
        self.xr, self.xl = lax.rem(x + 1, 4), lax.rem(x + 3, 4)
        self.zr, self.zl = lax.rem(z + 1, 4), lax.rem(z + 3, 4)
        self.yr, self.yl, self.y2 = lax.rem(y + 1, 4), lax.rem(y + 3, 4), lax.rem(y + 2, 4)
        self.XR, self.XL = {"seq": self.xr * 2 + c}, {"seq": self.xl * 2 + c}
        self.ZR, self.ZL = {"dp": self.zr}, {"dp": self.zl}
        self.YR, self.YL = {"tensor": self.yr}, {"tensor": self.yl}
        self.SIB = {"seq": x * 2 + 1 - c}

    def seq_at(self, distance):
        return {"seq": lax.rem(self.s + distance + 8, 8)}


def greet(devices):
    barrier = pltpu.get_barrier_semaphore()
    for device in devices:
        pl.semaphore_signal(barrier, inc=1, device_id=device, device_id_type=MESH)
    pl.semaphore_wait(barrier, len(devices))


class Links:
    def __init__(self, send, recv):
        self.send, self.recv = send, recv
        self.count = 0
        self.keyed = {}

    def go(self, src, dst, device):
        k = self.count
        self.count += 1
        copy = pltpu.make_async_remote_copy(
            src_ref=src,
            dst_ref=dst,
            send_sem=self.send.at[k],
            recv_sem=self.recv.at[k],
            device_id=device,
            device_id_type=MESH,
        )
        copy.start()
        self.keyed[k] = copy
        return k

    def arrived(self, view, k, device):
        pltpu.make_async_remote_copy(
            src_ref=view,
            dst_ref=view,
            send_sem=self.send.at[k],
            recv_sem=self.recv.at[k],
            device_id=device,
            device_id_type=MESH,
        ).wait_recv()

    def drain(self):
        for copy in self.keyed.values():
            copy.wait_send()
        self.keyed = {}

    def sent(self, keys):
        for k in keys:
            self.keyed.pop(k).wait_send()


class Gather:
    def __init__(self, links, place, out, cut):
        self.links, self.p = links, place
        self.out_a = out.at[:, :, :, :, pl.ds(0, cut)]
        self.out_b = out.at[:, :, :, :, pl.ds(cut, out.shape[-1] - cut)]
        self.to_sibling = []

    def _pass_on(self, view_of):
        k = self.links.go(view_of(self.p.c), view_of(self.p.c), self.p.SIB)
        self.to_sibling.append((view_of, k))

    def _ring(self, blk, i, right, left):
        links, p = self.links, self.p
        c = p.c
        ir, il, i2 = lax.rem(i + 1, 4), lax.rem(i + 3, 4), lax.rem(i + 2, 4)
        a, b = pl.ds(0, 32), pl.ds(32, 32)
        k0 = links.go(blk(c, i, a), blk(c, i, a), right)
        k1 = links.go(blk(c, i, b), blk(c, i, b), left)
        k2 = links.go(blk(c, i, b), blk(c, i, b), right)
        k3 = links.go(blk(c, i, a), blk(c, i, a), left)
        later = []

        def middle():
            links.arrived(blk(c, il, a), k0, left)
            later.append(links.go(blk(c, il, a), blk(c, il, a), right))
            links.arrived(blk(c, ir, b), k1, right)
            later.append(links.go(blk(c, ir, b), blk(c, ir, b), left))
            self._pass_on(lambda cc: blk(cc, il, a))
            self._pass_on(lambda cc: blk(cc, ir, b))

        def finish():
            for view, k, source in (
                (lambda cc: blk(cc, il, b), k2, left),
                (lambda cc: blk(cc, ir, a), k3, right),
                (lambda cc: blk(cc, i2, a), later[0], left),
                (lambda cc: blk(cc, i2, b), later[1], right),
            ):
                links.arrived(view(c), k, source)
                self._pass_on(view)

        return middle, finish

    def first(self):
        p, a, b = self.p, self.out_a, self.out_b
        self.ring_a = self._ring(lambda cc, j, r: a.at[j, cc, p.z, r], p.x, p.XR, p.XL)
        self.ring_b = self._ring(lambda cc, j, r: b.at[p.x, cc, j, r], p.z, p.ZR, p.ZL)
        self._pass_on(lambda cc: a.at[p.x, cc, p.z])
        self._pass_on(lambda cc: b.at[p.x, cc, p.z])

    def second_z(self):
        p, a = self.p, self.out_a
        self.ring_a = self._ring(lambda cc, j, r: a.at[:, cc, j, r], p.z, p.ZR, p.ZL)

    def second_x(self):
        p, b = self.p, self.out_b
        self.ring_b = self._ring(lambda cc, j, r: b.at[j, cc, :, r], p.x, p.XR, p.XL)

    def second(self):
        self.second_z()
        self.second_x()

    def middle(self):
        self.ring_a[0]()
        self.ring_b[0]()

    def finish(self):
        self.ring_a[1]()
        self.ring_b[1]()

    def settle(self):
        for view_of, k in self.to_sibling:
            self.links.arrived(view_of(1 - self.p.c), k, self.p.SIB)


CA, CB = pl.ds(0, WIDTH // 2), pl.ds(WIDTH // 2, WIDTH // 2)
HALF = WIDTH // 2


class Reduce:
    def __init__(self, links, place, part, far, near):
        self.links, self.p, self.part, self.far, self.near = links, place, part, far, near

    def send_first(self):
        p, part, near = self.p, self.part, self.near
        self.k0 = self.links.go(part.at[p.y2, :, CA], self.far.at[0], p.YR)
        self.k3 = self.links.go(part.at[p.yl, :, CA], near.at[1, :, CA], p.YL)

    def send_second(self):
        p, part, near = self.p, self.part, self.near
        self.k1 = self.links.go(part.at[p.y2, :, CB], self.far.at[1], p.YL)
        self.k2 = self.links.go(part.at[p.yr, :, CB], near.at[0, :, CB], p.YR)

    def send_far(self):
        p, part = self.p, self.part
        self.k0 = self.links.go(part.at[p.y2, :, CA], self.far.at[0], p.YR)
        self.k1 = self.links.go(part.at[p.y2, :, CB], self.far.at[1], p.YL)

    def send_near(self):
        p, part, near = self.p, self.part, self.near
        self.k2 = self.links.go(part.at[p.yr, :, CB], near.at[0, :, CB], p.YR)
        self.k3 = self.links.go(part.at[p.yl, :, CA], near.at[1, :, CA], p.YL)

    def merge(self):
        p, part, near, far = self.p, self.part, self.near, self.far
        self.links.arrived(far.at[0], self.k0, p.YL)
        far[0] = (far[0].astype(F32) + part[p.yr, :, 0:HALF].astype(F32)).astype(BF16)
        self.k4 = self.links.go(far.at[0], near.at[0, :, CA], p.YR)
        self.links.arrived(far.at[1], self.k1, p.YR)
        far[1] = (far[1].astype(F32) + part[p.yl, :, HALF:WIDTH].astype(F32)).astype(BF16)
        self.k5 = self.links.go(far.at[1], near.at[1, :, CB], p.YL)

    def settle(self):
        p, near = self.p, self.near
        self.links.arrived(near.at[0, :, CB], self.k2, p.YL)
        self.links.arrived(near.at[1, :, CA], self.k3, p.YR)
        self.links.arrived(near.at[0, :, CA], self.k4, p.YL)
        self.links.arrived(near.at[1, :, CB], self.k5, p.YR)


class Spread:
    def __init__(self, links, place, out):
        self.links, self.p, self.out = links, place, out

    def start(self):
        self.start_first()
        self.start_second()

    def start_first(self):
        go, out, y, p = self.links.go, self.out, self.p.y, self.p
        self.k0 = go(out.at[y, :, CA], out.at[y, :, CA], p.YR)
        self.k1 = go(out.at[y, :, CB], out.at[y, :, CB], p.YL)

    def start_second(self):
        go, out, y, p = self.links.go, self.out, self.p.y, self.p
        self.k2 = go(out.at[y, :, CB], out.at[y, :, CB], p.YR)
        self.k3 = go(out.at[y, :, CA], out.at[y, :, CA], p.YL)

    def forward(self):
        go, out, p, arrived = self.links.go, self.out, self.p, self.links.arrived
        arrived(out.at[p.yl, :, CA], self.k0, p.YL)
        self.k4 = go(out.at[p.yl, :, CA], out.at[p.yl, :, CA], p.YR)
        arrived(out.at[p.yr, :, CB], self.k1, p.YR)
        self.k5 = go(out.at[p.yr, :, CB], out.at[p.yr, :, CB], p.YL)

    def near(self):
        out, p, arrived = self.out, self.p, self.links.arrived
        arrived(out.at[p.yl, :, CB], self.k2, p.YL)
        arrived(out.at[p.yr, :, CA], self.k3, p.YR)

    def far(self):
        out, p, arrived = self.out, self.p, self.links.arrived
        arrived(out.at[p.y2, :, CA], self.k4, p.YL)
        arrived(out.at[p.y2, :, CB], self.k5, p.YR)


def dot(a, b):
    return jnp.dot(a, b, preferred_element_type=F32)


def dot_nt(a, b):
    return lax.dot_general(a, b, (((1,), (1,)), ((), ())), preferred_element_type=F32)


def dot_tn(a, b):
    return lax.dot_general(a, b, (((0,), (0,)), ((), ())), preferred_element_type=F32)


GELU_C = 0.7978845608028654
GELU_A = 0.044715


def gelu(v):
    return 0.5 * v * (1.0 + jnp.tanh(GELU_C * (v + GELU_A * v * v * v)))


def gelu_pair(v):
    t = jnp.tanh(GELU_C * (v + GELU_A * v * v * v))
    value = 0.5 * v * (1.0 + t)
    slope = 0.5 * (1.0 + t) + 0.5 * v * (1.0 - t * t) * (GELU_C * (1.0 + 3.0 * GELU_A * v * v))
    return value, slope


def tile_scan(a, b, reverse):
    row = lax.broadcasted_iota(jnp.int32, a.shape, 1)
    for step in (1, 2, 4):
        if reverse:
            shift, valid = 8 - step, row < 8 - step
        else:
            shift, valid = step, row >= step
        a_near, b_near = pltpu.roll(a, shift, 1), pltpu.roll(b, shift, 1)
        b = jnp.where(valid, a * b_near + b, b)
        a = jnp.where(valid, a * a_near, a)
    return a, b


def row_scan(a, b, reverse):
    tiles = SPAN // 8
    a, b = tile_scan(a.reshape(tiles, 8, LANES), b.reshape(tiles, 8, LANES), reverse)
    edge = 0 if reverse else 7
    order = range(tiles - 1, -1, -1) if reverse else range(tiles)
    out_a, out_b = [None] * tiles, [None] * tiles
    carry_a = carry_b = None
    for k in order:
        ak, bk = a[k], b[k]
        if carry_a is not None:
            bk = ak * carry_b + bk
            ak = ak * carry_a
        out_a[k], out_b[k] = ak, bk
        carry_a, carry_b = ak[edge : edge + 1], bk[edge : edge + 1]
    return jnp.concatenate(out_a, axis=0), jnp.concatenate(out_b, axis=0), carry_a, carry_b


def put_pair(ref, at, r, first, second):
    row = lax.broadcasted_iota(jnp.int32, (8, LANES), 0)
    ref[:, at] = jnp.where(row == r, first, jnp.where(row == ROWS + r, second, ref[:, at]))


def take_row(ref, at, r):
    row = lax.broadcasted_iota(jnp.int32, (8, LANES), 0)
    return jnp.sum(jnp.where(row == r, ref[:, at], 0.0), axis=0, keepdims=True)


def assemble_vectors(vectors, conv_weight, conv_bias, gate_bias, decay_param):
    vectors[0:4, :] = conv_weight[...].astype(F32)
    vectors[4:5, :] = conv_bias[...].astype(F32).reshape(1, CHAN)
    vectors[5:7, :] = gate_bias[...].astype(F32)
    decay = decay_param[...].astype(F32).reshape(1, CHAN)
    vectors[7:8, :] = -rate_scale * jnp.log1p(jnp.exp(decay))


def assemble_gates(gate_w, gate_blocks):
    for j in range(2):
        for h in range(HEADS):
            before, behind = 32 * h, 96 - 32 * h
            block = gate_blocks[j, h].astype(F32)
            parts = [jnp.zeros((BLK, before), F32)] if before else []
            parts += [block] + ([jnp.zeros((BLK, behind), F32)] if behind else [])
            wide = jnp.concatenate(parts, axis=1)
            tall = [jnp.zeros((before, 256), F32)] if before else []
            tall += [wide] + ([jnp.zeros((behind, 256), F32)] if behind else [])
            gate_w[j, h] = jnp.concatenate(tall, axis=0).astype(BF16)


def mix_forward_kernel(
    tokens,
    mix_in,
    mix_out,
    mlp_in,
    mlp_out,
    init_state,
    conv_state,
    fresh_rows,
    doc_start,
    gain_rows,
    conv_weight,
    conv_bias,
    gate_bias,
    decay_param,
    gate_blocks,
    mix_full_out,
    mlp_full,
    states_out,
    pre_out,
    ext_out,
    decay_out,
    input_out,
    conv_out,
    mixed_out,
    normed_in_out,
    entering_out,
    vectors_out,
    gate_w_out,
    normed_mid,
    after_own,
    mlp_own,
    gains,
    vectors,
    gate_w,
    mix_full,
    normed_in,
    pre,
    ext,
    decay_g,
    input_g,
    conv_low,
    cum_a,
    loc_b,
    states,
    mixed,
    rim_send,
    rim_recv,
    totals,
    totals_in,
    entering,
    part,
    far,
    near,
    local,
    send,
    recv,
):
    p = Place()
    links = Links(send, recv)
    mine = mix_full.at[p.x, p.c, p.z]
    for j in range(2):
        mine[:, j * CHAN : (j + 1) * CHAN] = mix_in[j]
    mine[:, 2 * CHAN :] = mix_out[...]
    greet([p.seq_at(d) for d in range(1, 8)] + [p.ZR, p.ZL, p.YR, p.YL])
    in_gather = Gather(links, p, mix_full.at[:, :, :, :, pl.ds(0, 2 * CHAN)], CHAN)
    out_gather = Gather(links, p, mix_full.at[:, :, :, :, pl.ds(2 * CHAN, CHAN)], 384)
    mlp_gather = Gather(links, p, mlp_full, MLP_CUT)
    in_gather.first()
    for j in range(2):
        mlp_own[:, j * MLP : (j + 1) * MLP] = mlp_in[j]
    mlp_own[:, 2 * MLP :] = mlp_out[...]
    own_mlp = pltpu.make_async_copy(mlp_own, mlp_full.at[p.x, p.c, p.z], local.at[0])
    own_mlp.start()
    gains[...] = gain_rows[...].astype(F32)
    assemble_vectors(vectors, conv_weight, conv_bias, gate_bias, decay_param)
    assemble_gates(gate_w, gate_blocks)

    def norm_rows(first, last):
        def one(k, carry):
            at = pl.ds(pl.multiple_of(k * 32, 32), 32)
            stream = tokens[at, :].astype(F32)
            scale = lax.rsqrt(jnp.mean(stream * stream, axis=-1, keepdims=True) + epsilon)
            normed_in[at, :] = (stream * scale * gains[0:1, :]).astype(BF16)
            return carry

        lax.fori_loop(first, last, one, 0)

    norm_rows(0, 8)
    in_gather.middle()
    in_gather.finish()
    in_gather.second()
    own_mlp.wait()
    norm_rows(8, 16)
    in_gather.middle()
    out_gather.first()
    mlp_gather.first()
    in_gather.finish()
    out_gather.middle()
    out_gather.finish()
    out_gather.second()
    in_gather.settle()
    saves = []

    def save(src, dst):
        copy = pltpu.make_async_copy(src, dst, local.at[2 + len(saves)])
        copy.start()
        saves.append(copy)

    save(normed_in, normed_in_out)
    save(vectors, vectors_out)
    save(gate_w, gate_w_out)

    def project(n, carry):
        at = pl.ds(pl.multiple_of(n * 256, 256), 256)
        pre[:, at] = dot(normed_in[...], mix_full[:, :, :, :, at].reshape(WIDTH, 256))
        return carry

    lax.fori_loop(2, 5, project, 0)
    for r in range(ROWS):
        ext[r, PAD:, :] = pre[r * SPAN : (r + 1) * SPAN, CHAN : 2 * CHAN].astype(BF16).astype(F32)
        rim_send[r] = ext[r, SPAN : SPAN + PAD, :]
    k_rim = links.go(rim_send, rim_recv, p.seq_at(1))
    lax.fori_loop(0, 2, project, 0)
    save(pre.at[:, pl.ds(0, CHAN)], pre_out)
    links.arrived(rim_recv, k_rim, p.seq_at(-1))
    at_start = p.s == 0
    for r in range(ROWS):
        keep = (1 - fresh_rows[r]).astype(F32)
        ext[r, 0:PAD, :] = jnp.where(at_start, 0.0, rim_recv[r])
        for j in range(CONV - 1):
            at = slice(PAD - 3 + j, PAD - 2 + j)
            first_rim = conv_state[j, r : r + 1, :].astype(F32) * keep
            ext[r, at, :] = jnp.where(at_start, first_rim, rim_recv[r, at, :])
    offset = p.s * SPAN

    def conv_chunk(i, carry):
        r, g = lax.rem(i, ROWS), lax.div(i, ROWS)
        at = pl.ds(pl.multiple_of(g * LANES, LANES), LANES)
        place = offset + lax.broadcasted_iota(jnp.int32, (SPAN, LANES), 0)
        begin = doc_start[r]
        here = place >= begin
        total = jnp.zeros((SPAN, LANES), F32) + vectors[4:5, at]
        for k in range(CONV):
            value = ext[r, PAD - 3 + k : PAD - 3 + k + SPAN, at]
            same = (place - (3 - k) >= begin) == here
            total = total + vectors[k : k + 1, at] * jnp.where(same, value, 0.0)
        rows = pl.ds(pl.multiple_of(r * SPAN, SPAN), SPAN)
        conv_low[rows, at] = total.astype(BF16)
        return carry

    lax.fori_loop(0, ROWS * GROUPS, conv_chunk, 0)
    save(ext, ext_out)
    save(conv_low, conv_out)

    for j, target in ((0, decay_g), (1, input_g)):
        held = None
        for g in range(GROUPS):
            total = held
            if g < HEADS:
                product = dot(conv_low[:, g * LANES : g * LANES + 256], gate_w[j, g])
                total = product[:, :LANES] if held is None else held + product[:, :LANES]
                held = product[:, LANES:]
            target[:, g * LANES : (g + 1) * LANES] = total

    def gate_chunk(i, carry):
        r, g = lax.rem(i, ROWS), lax.div(i, ROWS)
        at = pl.ds(pl.multiple_of(g * LANES, LANES), LANES)
        rows = pl.ds(pl.multiple_of(r * SPAN, SPAN), SPAN)
        gate_d = jax.nn.sigmoid(decay_g[rows, at] + vectors[5:6, at])
        gate_i = jax.nn.sigmoid(input_g[rows, at] + vectors[6:7, at])
        decay_g[rows, at] = gate_d
        input_g[rows, at] = gate_i
        decay_now = jnp.exp(gate_d * vectors[7:8, at])
        root = jnp.sqrt(jnp.maximum(1.0 - decay_now * decay_now, root_floor))
        fed = root * gate_i * conv_low[rows, at].astype(F32)
        place = offset + lax.broadcasted_iota(jnp.int32, (SPAN, LANES), 0)
        carried = jnp.where(place == doc_start[r], 0.0, decay_now)
        a, b, last_a, last_b = row_scan(carried, fed, False)
        cum_a[rows, at] = a
        loc_b[rows, at] = b
        put_pair(totals, at, r, last_a, last_b)
        return carry

    totals[...] = jnp.zeros_like(totals)
    lax.fori_loop(0, ROWS * GROUPS, gate_chunk, 0)
    keys = [links.go(totals, totals_in.at[p.s], p.seq_at(d)) for d in range(1, 8)]
    save(decay_g, decay_out)
    save(input_g, input_out)
    out_gather.middle()
    out_gather.finish()
    row = lax.broadcasted_iota(jnp.int32, (ROWS, CHAN), 0)
    kept = jnp.zeros((ROWS, CHAN), F32)
    for r in range(ROWS):
        kept = jnp.where(row == r, (1 - fresh_rows[r]).astype(F32), kept)
    state = init_state[...] * kept
    for d in range(1, 8):
        links.arrived(totals_in.at[p.seq_at(-d)["seq"]], keys[d - 1], p.seq_at(-d))
    mlp_gather.middle()
    mlp_gather.finish()
    mlp_gather.second()
    totals_in[p.s] = totals[...]
    for source in range(7):
        both = totals_in[source]
        state = jnp.where(source < p.s, both[0:ROWS] * state + both[ROWS:], state)
    entering[0:ROWS, :] = state
    entering[ROWS:, :] = jnp.zeros((8 - ROWS, CHAN), F32)

    def state_chunk(i, carry):
        r, g = lax.rem(i, ROWS), lax.div(i, ROWS)
        at = pl.ds(pl.multiple_of(g * LANES, LANES), LANES)
        rows = pl.ds(pl.multiple_of(r * SPAN, SPAN), SPAN)
        value = loc_b[rows, at] + cum_a[rows, at] * take_row(entering, at, r)
        states[rows, at] = value
        mixed[rows, at] = (value * gelu(pre[rows, at])).astype(BF16)
        return carry

    lax.fori_loop(0, ROWS * GROUPS, state_chunk, 0)
    save(states, states_out)
    save(mixed, mixed_out)
    save(entering, entering_out)

    out_gather.settle()
    save(mix_full, mix_full_out)

    def partial(n, carry):
        weights = mix_full[lax.div(n, 2), lax.rem(n, 2), :, :, 2 * CHAN :].reshape(256, CHAN)
        product = dot_nt(mixed[...], weights).astype(BF16)
        part[:, :, pl.ds(pl.multiple_of(n * 256, 256), 256)] = product.reshape(ROWS, SPAN, 256)
        return carry

    reduce = Reduce(links, p, part, far, near)
    lax.fori_loop(0, 4, partial, 0)
    reduce.send_first()
    lax.fori_loop(4, 8, partial, 0)
    reduce.send_second()
    mlp_gather.middle()
    reduce.merge()
    reduce.settle()

    def norm_mid(k, carry):
        at = pl.ds(pl.multiple_of(k * 16, 16), 16)
        total = part[p.y, at, :].astype(F32) + near[0, at, :].astype(F32) + near[1, at, :].astype(F32)
        row = pl.ds(pl.multiple_of(p.y * SPAN + k * 16, 16), 16)
        stream = tokens[row, :].astype(F32) + total
        scale = lax.rsqrt(jnp.mean(stream * stream, axis=-1, keepdims=True) + epsilon)
        after_own[at, :] = stream
        normed_mid[p.y, at, :] = (stream * scale * gains[1:2, :]).astype(BF16)
        return carry

    lax.fori_loop(0, SPAN // 16, norm_mid, 0)
    spread = Spread(links, p, normed_mid)
    spread.start()
    mlp_gather.finish()
    spread.forward()
    spread.near()
    spread.far()
    mlp_gather.settle()
    for copy in saves:
        copy.wait()
    links.drain()


def params(collective_id):
    return pltpu.CompilerParams(
        collective_id=collective_id, has_side_effects=True, vmem_limit_bytes=VMEM_BYTES
    )


def vmem():
    return pl.BlockSpec(memory_space=pltpu.VMEM)


def smem():
    return pl.BlockSpec(memory_space=pltpu.SMEM)


def anyspace():
    return pl.BlockSpec(memory_space=pl.ANY)


def mix_forward(*operands):
    shape = jax.ShapeDtypeStruct
    tc = (TOKENS, CHAN)
    ext_shape = (ROWS, PAD + SPAN, CHAN)
    outs = [
        shape((4, 2, 4, 64, MIX_COLS), BF16),
        shape((4, 2, 4, 64, MLP_COLS), BF16),
        shape(tc, F32),
        shape(tc, F32),
        shape(ext_shape, F32),
        shape(tc, F32),
        shape(tc, F32),
        shape(tc, BF16),
        shape(tc, BF16),
        shape((TOKENS, WIDTH), BF16),
        shape((8, CHAN), F32),
        shape((8, CHAN), F32),
        shape((2, HEADS, 256, 256), BF16),
        shape((ROWS, SPAN, WIDTH), BF16),
        shape((SPAN, WIDTH), F32),
    ]
    scratch = [
        pltpu.VMEM((64, MLP_COLS), BF16),
        pltpu.VMEM((2, WIDTH), F32),
        pltpu.VMEM((8, CHAN), F32),
        pltpu.VMEM((2, HEADS, 256, 256), BF16),
        pltpu.VMEM((4, 2, 4, 64, MIX_COLS), BF16),
        pltpu.VMEM((TOKENS, WIDTH), BF16),
        pltpu.VMEM((TOKENS, 2 * CHAN), F32),
        pltpu.VMEM(ext_shape, F32),
        pltpu.VMEM(tc, F32),
        pltpu.VMEM(tc, F32),
        pltpu.VMEM(tc, BF16),
        pltpu.VMEM(tc, F32),
        pltpu.VMEM(tc, F32),
        pltpu.VMEM(tc, F32),
        pltpu.VMEM(tc, BF16),
        pltpu.VMEM((ROWS, PAD, CHAN), F32),
        pltpu.VMEM((ROWS, PAD, CHAN), F32),
        pltpu.VMEM((8, CHAN), F32),
        pltpu.VMEM((8, 8, CHAN), F32),
        pltpu.VMEM((8, CHAN), F32),
        pltpu.VMEM((ROWS, SPAN, WIDTH), BF16),
        pltpu.VMEM((2, SPAN, HALF), BF16),
        pltpu.VMEM((2, SPAN, WIDTH), BF16),
        pltpu.SemaphoreType.DMA((20,)),
        pltpu.SemaphoreType.DMA((184,)),
        pltpu.SemaphoreType.DMA((184,)),
    ]
    return pl.pallas_call(
        mix_forward_kernel,
        out_shape=outs,
        in_specs=[vmem()] * 7 + [smem()] * 2 + [vmem()] * 6,
        out_specs=[anyspace()] * 13 + [vmem()] * 2,
        scratch_shapes=scratch,
        compiler_params=params(0),
        name="mix_forward",
    )(*operands)


def norm_back_rows(d_row, stream, gain_row):
    scale = lax.rsqrt(jnp.mean(stream * stream, axis=-1, keepdims=True) + epsilon)
    unit = stream * scale
    e = d_row * gain_row
    inner = jnp.mean(e * unit, axis=-1, keepdims=True)
    return scale * (e - unit * inner), d_row * unit


def own_sum(reduce, at):
    part, near = reduce.part, reduce.near
    return part[reduce.p.y, at, :].astype(F32) + near[0, at, :].astype(F32) + near[1, at, :].astype(F32)


def mlp_kernel(
    normed,
    upstream,
    gate_weights,
    up_weights,
    down_weights,
    states_in,
    d_gate_out,
    d_up_out,
    hidden_out,
    grads,
    states_out,
    normed_t,
    upstream_t,
    d_both,
):
    states_out[...] = states_in[...]

    @pl.when(pl.program_id(0) == 0)
    def _():
        def turn(n, carry):
            at = pl.ds(pl.multiple_of(n * 256, 256), 256)
            normed_t[at, :] = normed[:, at].T
            upstream_t[at, :] = upstream[:, at].T
            return carry

        lax.fori_loop(0, WIDTH // 256, turn, 0)

    gate = dot(normed[...], gate_weights[...])
    up = dot(normed[...], up_weights[...])
    d_hidden = dot(upstream[...], down_weights[...])
    act, slope = gelu_pair(gate)
    hidden = (act * up).astype(BF16)
    d_gate = (d_hidden * up * slope).astype(BF16)
    d_up = (d_hidden * act).astype(BF16)
    d_both[:, 0:CHUNK] = d_gate
    d_both[:, CHUNK : 2 * CHUNK] = d_up
    d_both[:, 2 * CHUNK :] = hidden
    d_gate_out[...] = d_gate
    d_up_out[...] = d_up
    hidden_out[...] = hidden

    def tile(n, carry):
        at = pl.ds(pl.multiple_of(n * 256, 256), 256)
        grads[at, 0 : 2 * CHUNK] = dot(normed_t[at, :], d_both[:, 0 : 2 * CHUNK]).astype(BF16)
        grads[at, 2 * CHUNK :] = dot(upstream_t[at, :], d_both[:, 2 * CHUNK :]).astype(BF16)
        return carry

    lax.fori_loop(0, WIDTH // 256, tile, 0, unroll=2)


def mlp_all(normed, upstream, weights, states):
    shape = jax.ShapeDtypeStruct
    whole = pl.BlockSpec((TOKENS, WIDTH), lambda f: (0, 0))
    part = lambda j: pl.BlockSpec((WIDTH, CHUNK), lambda f: (0, j * CHUNKS + f))
    block = pl.BlockSpec((WIDTH, 3 * CHUNK), lambda f: (0, f))
    column = pl.BlockSpec((TOKENS, CHUNK), lambda f: (0, f))
    row = pl.BlockSpec((1, SPAN, CHAN), lambda f: (jnp.minimum(f, ROWS - 1), 0, 0))
    return pl.pallas_call(
        mlp_kernel,
        grid=(CHUNKS,),
        out_shape=[shape((TOKENS, MLP), BF16)] * 3
        + [shape((WIDTH, MLP_COLS), BF16), shape((ROWS, SPAN, CHAN), F32)],
        in_specs=[whole, whole, part(0), part(1), part(2), row],
        out_specs=[column] * 3 + [block, row],
        scratch_shapes=[
            pltpu.VMEM((WIDTH, TOKENS), BF16),
            pltpu.VMEM((WIDTH, TOKENS), BF16),
            pltpu.VMEM((TOKENS, 3 * CHUNK), BF16),
        ],
        compiler_params=pltpu.CompilerParams(vmem_limit_bytes=VMEM_BYTES),
        cost_estimate=pl.CostEstimate(
            flops=12 * TOKENS * WIDTH * MLP, bytes_accessed=4 * WIDTH * MLP_COLS, transcendentals=TOKENS * MLP
        ),
        name="mlp_all",
    )(normed, upstream, weights, weights, weights, states)


class Scatter:
    def __init__(self, links, place, grads, sib, far, near, half_a, half_b, far_2, near_2):
        self.links, self.p = links, place
        self.grads, self.sib = grads, sib
        self.far, self.near, self.far_2, self.near_2 = far, near, far_2, near_2
        self.half_a, self.half_b = half_a, half_b
        self.sib_keys = {}

    def give(self, xx):
        p = self.p
        self.sib_keys[xx] = self.links.go(self.grads.at[xx, 1 - p.c], self.sib.at[xx], p.SIB)

    def take(self, xx):
        p, sib, grads = self.p, self.sib, self.grads
        self.links.arrived(sib.at[xx], self.sib_keys[xx], p.SIB)

        def one(j, carry):
            sib[xx, j] = (sib[xx, j].astype(F32) + grads[xx, p.c, j].astype(F32)).astype(BF16)
            return carry

        lax.fori_loop(0, 4, one, 0)

    def _ring(self, view, i, right, left, far, near, base):
        links = self.links
        ir, il, i2 = lax.rem(i + 1, 4), lax.rem(i + 3, 4), lax.rem(i + 2, 4)
        a, b = pl.ds(base, 16), pl.ds(base + 16, 16)
        na, nb = pl.ds(0, 16), pl.ds(16, 16)
        k0 = links.go(view(i2, a), far.at[0], right)
        k1 = links.go(view(i2, b), far.at[1], left)
        k2 = links.go(view(ir, b), near.at[0, :, nb], right)
        k3 = links.go(view(il, a), near.at[1, :, na], left)
        keys = []

        def merge():
            for way, k, row, at, source, target, to in (
                (0, k0, ir, a, left, right, na),
                (1, k1, il, b, right, left, nb),
            ):
                links.arrived(far.at[way], k, source)
                mine = view(row, at)

                def one(j, carry):
                    far[way, j] = (far[way, j].astype(F32) + mine[j].astype(F32)).astype(BF16)
                    return carry

                lax.fori_loop(0, far.shape[1], one, 0)
                keys.append(links.go(far.at[way], near.at[way, :, to], target))

        def settle():
            links.arrived(near.at[0, :, nb], k2, left)
            links.arrived(near.at[1, :, na], k3, right)
            links.arrived(near.at[0, :, na], keys[0], left)
            links.arrived(near.at[1, :, nb], keys[1], right)

        return merge, settle

    def first(self):
        p, sib = self.p, self.sib
        self.x_ring = self._ring(lambda j, r: sib.at[j, :, r], p.x, p.XR, p.XL, self.far.at[0], self.near.at[0], 0)
        self.z_ring = self._ring(lambda j, r: sib.at[:, j, r], p.z, p.ZR, p.ZL, self.far.at[1], self.near.at[1], 32)

    def merge(self):
        self.x_ring[0]()
        self.z_ring[0]()

    def turn(self):
        p, sib, near = self.p, self.sib, self.near
        self.x_ring[1]()

        def one_a(j, carry):
            total = sib[p.x, j, 0:32].astype(F32) + near[0, 0, j].astype(F32) + near[0, 1, j].astype(F32)
            self.half_a[j, 0] = total.astype(BF16)
            return carry

        lax.fori_loop(0, 4, one_a, 0)
        half_a, half_b = self.half_a, self.half_b
        self.ring_a = self._ring(
            lambda j, r: half_a.at[j, :, r], p.z, p.ZR, p.ZL, self.far_2.at[0], self.near_2.at[0], 0
        )
        self.z_ring[1]()

        def one_b(j, carry):
            total = sib[j, p.z, 32:64].astype(F32) + near[1, 0, j].astype(F32) + near[1, 1, j].astype(F32)
            self.half_b[j, 0] = total.astype(BF16)
            return carry

        lax.fori_loop(0, 4, one_b, 0)
        self.ring_b = self._ring(
            lambda j, r: half_b.at[j, :, r], p.x, p.XR, p.XL, self.far_2.at[1], self.near_2.at[1], 0
        )

    def merge_2(self):
        self.ring_a[0]()
        self.ring_b[0]()

    def finish(self, store):
        p, near = self.p, self.near_2
        self.ring_a[1]()
        store(0, self.half_a[p.z, 0].astype(F32) + near[0, 0, 0].astype(F32) + near[0, 1, 0].astype(F32))
        self.ring_b[1]()
        store(32, self.half_b[p.x, 0].astype(F32) + near[1, 0, 0].astype(F32) + near[1, 1, 0].astype(F32))

    @staticmethod
    def scratch(columns):
        return [
            pltpu.VMEM((4, 4, 64, columns), BF16),
            pltpu.VMEM((2, 2, 4, 16, columns), BF16),
            pltpu.VMEM((2, 2, 4, 32, columns), BF16),
            pltpu.VMEM((4, 1, 32, columns), BF16),
            pltpu.VMEM((4, 1, 32, columns), BF16),
            pltpu.VMEM((2, 2, 1, 16, columns), BF16),
            pltpu.VMEM((2, 2, 1, 32, columns), BF16),
        ]


def back_kernel(
    hbm_d_gate,
    hbm_d_up,
    hbm_hidden,
    mlp_full,
    mix_full,
    hbm_saved_0,
    hbm_saved_1,
    hbm_saved_2,
    hbm_saved_3,
    hbm_saved_4,
    hbm_saved_5,
    hbm_saved_6,
    hbm_saved_7,
    hbm_saved_8,
    entering,
    tokens,
    upstream,
    gain_rows,
    vectors,
    gate_w,
    doc_start,
    grad_tokens,
    block_out,
    grad_mix,
    small_sums,
    block_sums,
    gain_sums,
    hidden,
    states,
    pre,
    ext,
    decay_g,
    input_g,
    conv_low,
    mixed,
    normed_in,
    after_own,
    work,
    small_work,
    own_tokens,
    own_upstream,
    mid_part,
    out_part,
    d_after_low,
    d_after_own,
    gain_mid,
    d_mixed,
    tail_a,
    d_gates,
    d_both,
    small,
    rim_send,
    rim_recv,
    totals,
    totals_in,
    after,
    far_a,
    near_a,
    far_b,
    near_b,
    *rest,
):
    n_scatter = 7
    mix_scratch, rest = rest[:n_scatter], rest[n_scatter:]
    small_scratch, rest = rest[:n_scatter], rest[n_scatter:]
    saved = (
        (hbm_saved_0, states),
        (hbm_saved_1, pre),
        (hbm_saved_2, ext),
        (hbm_saved_3, decay_g),
        (hbm_saved_4, input_g),
        (hbm_saved_5, conv_low),
        (hbm_saved_6, mixed),
        (hbm_saved_7, normed_in),
        (hbm_saved_8, after_own),
    )
    back_steps(
        (hbm_d_gate, hbm_d_up, hbm_hidden), saved, mlp_full, mix_full, hidden, states, pre, ext, decay_g, input_g,
        conv_low, entering, mixed, normed_in, tokens, upstream, after_own, gain_rows, vectors, gate_w, doc_start,
        grad_tokens, block_out, grad_mix, small_sums, block_sums, gain_sums,
        work, small_work, own_tokens, own_upstream, mid_part, out_part, d_after_low, d_after_own, gain_mid,
        d_mixed, tail_a, d_gates, d_both, small, rim_send, rim_recv, totals, totals_in, after,
        far_a, near_a, far_b, near_b, mix_scratch, small_scratch, *rest,
    )


def back_steps(
    mlp_saved, saved, mlp_full, mix_full, hidden, states, pre, ext, decay_g, input_g,
    conv_low, entering, mixed, normed_in, tokens, upstream, after_own, gain_rows, vectors, gate_w, doc_start,
    grad_tokens, block_out, grad_mix, small_sums, block_sums, gain_sums,
    work, small_work, own_tokens, own_upstream, mid_part, out_part, d_after_low, d_after_own, gain_mid,
    d_mixed, tail_a, d_gates, d_both, small, rim_send, rim_recv, totals, totals_in, after,
    far_a, near_a, far_b, near_b, mix_scratch, small_scratch,
    small_all,
    gain_in,
    gain_y,
    gain_s,
    gain_z,
    local,
    tiles,
    send,
    recv,
):
    p = Place()
    links = Links(send, recv)
    sib = mix_scratch[0]
    early = (
        pltpu.make_async_copy(mlp_saved[0], sib.at[pl.ds(0, 2), :, :, pl.ds(0, MLP)], local.at[0]),
        pltpu.make_async_copy(mlp_saved[1], sib.at[pl.ds(2, 2), :, :, pl.ds(0, MLP)], local.at[1]),
    )
    for copy in early:
        copy.start()

    def weight_tile(n, j, slot):
        source = mlp_full.at[n // 2, n % 2, :, :, pl.ds(j * MLP, MLP)]
        return pltpu.make_async_copy(source, work.at[slot // 2, slot % 2, :, :, pl.ds(0, MLP)], tiles.at[slot])

    fetched = {}

    def fetch(n):
        for j in range(2):
            fetched[n, j] = weight_tile(n, j, (2 * n + j) % 8)
            fetched[n, j].start()

    for n in range(3):
        fetch(n)
    hidden_load = pltpu.make_async_copy(mlp_saved[2], hidden, local.at[2])
    hidden_load.start()
    saved_loads = [
        pltpu.make_async_copy(source, target, local.at[3 + k]) for k, (source, target) in enumerate(saved)
    ]
    load_tokens = pltpu.make_async_copy(tokens.at[p.y], own_tokens, local.at[12])
    load_tokens.start()
    load_upstream = pltpu.make_async_copy(upstream.at[p.y], own_upstream, local.at[13])
    load_upstream.start()
    others_y = [{"tensor": lax.rem(p.y + d, 4)} for d in (1, 2, 3)]
    others_z = [{"dp": lax.rem(p.z + d, 4)} for d in (1, 2, 3)]
    greet([p.seq_at(d) for d in range(1, 8)] + others_y + others_z)
    middle = Reduce(links, p, mid_part, far_a, near_a)
    for copy in early:
        copy.wait()

    def tile_of(slot):
        return work[slot // 2, slot % 2, :, :, 0:MLP].reshape(256, MLP)

    for n in range(8):
        if n + 3 < 8:
            fetch(n + 3)
        if n == 4:
            middle.send_first()
        for j in range(2):
            fetched[n, j].wait()
        at = slice(n * 256, (n + 1) * 256)
        product = dot_nt(sib[0:2, :, :, 0:MLP].reshape(TOKENS, MLP), tile_of(2 * n % 8)) + dot_nt(
            sib[2:4, :, :, 0:MLP].reshape(TOKENS, MLP), tile_of((2 * n + 1) % 8)
        )
        mid_part[:, :, at] = product.astype(BF16).reshape(ROWS, SPAN, 256)
    middle.send_second()
    downs = [weight_tile(n, 2, n) for n in range(8)]
    for copy in downs:
        copy.start()
    middle.merge()
    hidden_load.wait()
    for copy in downs:
        copy.wait()
    for copy in saved_loads:
        copy.start()

    def out_product(n, carry):
        weights = work[lax.div(n, 2), lax.rem(n, 2), :, :, 0:MLP].reshape(256, MLP)
        product = dot_nt(hidden[...], weights).astype(BF16)
        out_part[:, :, pl.ds(pl.multiple_of(n * 256, 256), 256)] = product.reshape(ROWS, SPAN, 256)
        return carry

    lax.fori_loop(0, 8, out_product, 0)
    load = pltpu.make_async_copy(mix_full, work, local.at[14])
    load.start()
    for copy in saved_loads:
        copy.wait()
    gain_mid[...] = jnp.zeros_like(gain_mid)
    gain_1 = gain_rows[1:2, :].astype(F32)
    load_upstream.wait()
    middle.settle()

    def middle_rows(k, carry):
        at = pl.ds(pl.multiple_of(k * 16, 16), 16)
        through, share = norm_back_rows(own_sum(middle, at), after_own[at, :], gain_1)
        gain_mid[...] += share[0:8] + share[8:16]
        total = own_upstream[at, :].astype(F32) + through
        d_after_own[at, :] = total
        d_after_low[p.y, at, :] = total.astype(BF16)
        return carry

    lax.fori_loop(0, SPAN // 16, middle_rows, 0)
    links.sent([middle.k0, middle.k1, middle.k2, middle.k3, middle.k4, middle.k5])
    spread_c = Spread(links, p, d_after_low)
    spread_c.start()
    load.wait()
    rows_low = d_after_low.reshape(TOKENS, WIDTH)

    def mixed_row(row):
        rows = pl.ds(pl.multiple_of(row * SPAN, SPAN), SPAN)
        for start, size in ((0, 256), (256, 256), (512, 128)):
            weights = work[:, :, :, :, 2 * CHAN + start : 2 * CHAN + start + size].reshape(WIDTH, size)
            d_mixed[rows, start : start + size] = dot(d_after_low[row], weights)

    mixed_row(p.y)
    spread_c.forward()
    ahead = Reduce(links, p, out_part, far_b, near_b)
    ahead.send_far()
    ahead.send_near()
    spread_c.near()
    mixed_row(p.yl)
    mixed_row(p.yr)
    spread_c.far()
    mixed_row(p.y2)
    small[...] = jnp.zeros_like(small)
    totals[...] = jnp.zeros_like(totals)
    gain_in[...] = jnp.zeros_like(gain_in)
    offset = p.s * SPAN

    def chunk(i):
        r, g = lax.rem(i, ROWS), lax.div(i, ROWS)
        at = pl.ds(pl.multiple_of(g * LANES, LANES), LANES)
        rows = pl.ds(pl.multiple_of(r * SPAN, SPAN), SPAN)
        row = lax.broadcasted_iota(jnp.int32, (SPAN, LANES), 0)
        return r, g, at, rows, row

    def states_back(i, carry):
        r, g, at, rows, row = chunk(i)
        d_chunk = d_mixed[rows, at]
        value, slope = gelu_pair(pre[rows, at])
        d_both[rows, at] = (d_chunk * states[rows, at] * slope).astype(BF16)
        decay_now = jnp.exp(decay_g[rows, at] * vectors[7:8, at])
        carried = jnp.where(offset + row == doc_start[r], 0.0, decay_now)
        following = jnp.where(row == SPAN - 1, 1.0, pltpu.roll(carried, SPAN - 1, 0))
        a, b, first_a, first_b = row_scan(following, d_chunk * value, True)
        tail_a[rows, at] = a
        d_mixed[rows, at] = b
        put_pair(totals, at, r, carried[0:1] * first_a, carried[0:1] * first_b)
        return carry

    lax.fori_loop(0, ROWS * GROUPS, states_back, 0)
    keys = [links.go(totals, totals_in.at[p.s], p.seq_at(d)) for d in range(1, 8)]
    ahead.merge()
    state = jnp.zeros((ROWS, CHAN), F32)
    for d in range(1, 8):
        links.arrived(totals_in.at[p.seq_at(-d)["seq"]], keys[d - 1], p.seq_at(-d))
    totals_in[p.s] = totals[...]
    for source in range(7, 0, -1):
        both = totals_in[source]
        state = jnp.where(source > p.s, both[0:ROWS] * state + both[ROWS:], state)
    after[0:ROWS, :] = state
    after[ROWS:, :] = jnp.zeros((8 - ROWS, CHAN), F32)

    def gates_back(i, carry):
        r, g, at, rows, row = chunk(i)
        grads = d_mixed[rows, at] + tail_a[rows, at] * take_row(after, at, r)
        held = states[rows, at]
        previous = jnp.where(row == 0, take_row(entering, at, r), pltpu.roll(held, 1, 0))
        gate_d, gate_i = decay_g[rows, at], input_g[rows, at]
        rate = vectors[7:8, at]
        decay_now = jnp.exp(gate_d * rate)
        headroom = 1.0 - decay_now * decay_now
        root = jnp.sqrt(jnp.maximum(headroom, root_floor))
        conv = conv_low[rows, at].astype(F32)
        d_decay = jnp.where(offset + row == doc_start[r], 0.0, grads * previous) - jnp.where(
            headroom > root_floor, grads * gate_i * conv * decay_now / root, 0.0
        )
        d_log = d_decay * decay_now
        d_zero = d_log * rate * gate_d * (1.0 - gate_d)
        fed = grads * root
        d_one = fed * conv * gate_i * (1.0 - gate_i)
        d_gates[rows, pl.ds(pl.multiple_of(g * LANES, LANES), LANES)] = d_zero.astype(BF16)
        d_gates[rows, pl.ds(pl.multiple_of(CHAN + g * LANES, LANES), LANES)] = d_one.astype(BF16)
        tail_a[rows, at] = fed * gate_i
        small[5:6, at] += jnp.sum(d_zero, axis=0, keepdims=True)
        small[6:7, at] += jnp.sum(d_one, axis=0, keepdims=True)
        small[7:8, at] += jnp.sum(d_log * (-rate_scale * gate_d), axis=0, keepdims=True)
        return carry

    lax.fori_loop(0, ROWS * GROUPS, gates_back, 0)

    def ahead_rows(k, carry):
        at = pl.ds(pl.multiple_of(k * 16, 16), 16)
        block_out[p.y, at, :] = (after_own[at, :] + own_sum(ahead, at)).astype(BF16)
        return carry

    spread_b = Spread(links, p, block_out)

    d_conv = tail_a
    held = None
    for g in range(GROUPS):
        total = d_conv[:, g * LANES : (g + 1) * LANES]
        if held is not None:
            total = total + held
        if g < HEADS:
            lo = g * LANES
            product = dot_nt(d_gates[:, lo : lo + 256], gate_w[0, g]) + dot_nt(
                d_gates[:, CHAN + lo : CHAN + lo + 256], gate_w[1, g]
            )
            total = total + product[:, :LANES]
            held = product[:, LANES:]
        d_conv[:, g * LANES : (g + 1) * LANES] = total

    body = d_mixed

    def conv_back(i, carry):
        r, g, at, rows, row = chunk(i)
        d_chunk = d_conv[rows, at]
        begin = doc_start[r]
        place = offset + row
        here = place >= begin
        head = jnp.zeros((8, LANES), F32)
        total = jnp.zeros((SPAN, LANES), F32)
        for k in range(CONV):
            before = CONV - 1 - k
            same = (place - before >= begin) == here
            kept = jnp.where(same, d_chunk, 0.0)
            value = ext[r, PAD - before : PAD - before + SPAN, at]
            small[k : k + 1, at] += jnp.sum(kept * value, axis=0, keepdims=True)
            term = kept * vectors[k : k + 1, at]
            if before:
                total = total + jnp.where(row < SPAN - before, pltpu.roll(term, SPAN - before, 0), 0.0)
                head = head + jnp.where(
                    row[0:8] >= 8 - before, pltpu.roll(term[0:8], 8 - before, 0), 0.0
                )
            else:
                total = total + term
        small[4:5, at] += jnp.sum(d_chunk, axis=0, keepdims=True)
        body[rows, at] = total
        rim_send[r, :, at] = head
        return carry

    lax.fori_loop(0, ROWS * GROUPS, conv_back, 0)
    k_rim = links.go(rim_send, rim_recv, p.seq_at(-1))

    def blocks(j, h):
        lo = h * LANES
        product = dot_tn(conv_low[:, lo : lo + 256], d_gates[:, j * CHAN + lo : j * CHAN + lo + 256])
        for q in range(BLK // 32):
            row = (j * HEADS + h) * BLK + 32 * q
            n, inner = row // 64, row % 64
            piece = product[32 * (h + q) : 32 * (h + q + 1), :].astype(BF16)
            small_work[n // 8, (n // 4) % 2, n % 4, inner : inner + 32, :] = piece

    for j in range(2):
        for h in range(HEADS):
            blocks(j, h)
    for n in range(20, 32):
        small_work[n // 8, (n // 4) % 2, n % 4] = jnp.zeros((64, SMALL), BF16)
    for k, n in enumerate((20, 21, 22)):
        width = min(256, CHAN - 256 * k)
        both = jnp.concatenate([small[:, 256 * k : 256 * k + width], jnp.zeros((8, width), F32)], axis=0)
        small_work[n // 8, (n // 4) % 2, n % 4, 0:16, 0:width] = both.astype(BF16)
    small_scatter = Scatter(links, p, small_work, *small_scratch)
    for xx in range(4):
        small_scatter.give(xx)
    links.arrived(rim_recv, k_rim, p.seq_at(1))
    for r in range(ROWS):
        last = r * SPAN + SPAN - 8
        body[last : last + 8, :] += jnp.where(p.s == 7, 0.0, rim_recv[r])
    for r in range(ROWS):
        d_both[r * SPAN : (r + 1) * SPAN, CHAN:] = body[r * SPAN : (r + 1) * SPAN, :].astype(BF16)

    def first_part(n, carry):
        weights = work[lax.div(n, 2), lax.rem(n, 2), :, :, 0 : 2 * CHAN].reshape(256, 2 * CHAN)
        product = dot_nt(d_both[...], weights).astype(BF16)
        d_first[:, :, pl.ds(pl.multiple_of(n * 256, 256), 256)] = product.reshape(ROWS, SPAN, 256)
        return carry

    d_first = mid_part
    back = Reduce(links, p, d_first, far_a, near_a)
    ahead.settle()
    lax.fori_loop(0, SPAN // 16, ahead_rows, 0)
    spread_b.start_first()
    lax.fori_loop(0, 4, first_part, 0)
    back.send_first()
    lax.fori_loop(4, 8, first_part, 0)
    back.send_second()
    for xx in range(4):
        small_scatter.take(xx)
    small_scatter.first()

    def weight_grads(n):
        at = pl.ds(pl.multiple_of(n * 256, 256), 256)
        to = work.at[lax.div(n, 2), lax.rem(n, 2)]
        both = dot_tn(normed_in[:, at], d_both[...])
        to[:, :, 0 : 2 * CHAN] = both.astype(BF16).reshape(4, 64, 2 * CHAN)
        out = dot_tn(rows_low[:, at], mixed[...])
        to[:, :, 2 * CHAN : MIX_COLS] = out.astype(BF16).reshape(4, 64, CHAN)

    scatter = Scatter(links, p, work, *mix_scratch)

    def give(xx, carry):
        weight_grads(xx * 2 + 1 - p.c)
        return carry

    def keep(xx, carry):
        weight_grads(xx * 2 + p.c)
        return carry

    lax.fori_loop(0, 4, give, 0)
    for xx in range(4):
        scatter.give(xx)
    small_scatter.merge()
    back.merge()
    spread_b.start_second()
    lax.fori_loop(0, 4, keep, 0)
    small_scatter.turn()
    for xx in range(4):
        scatter.take(xx)
    scatter.first()
    def store_small(base, value):
        small_all[p.x, p.c, p.z, base : base + 32, :] = value.astype(BF16)

    small_scatter.merge_2()
    back.settle()
    load_tokens.wait()
    gain = gain_rows[0:1, :].astype(F32)

    def back_rows(k, carry):
        at = pl.ds(pl.multiple_of(k * 16, 16), 16)
        through, share = norm_back_rows(own_sum(back, at), own_tokens[at, :].astype(F32), gain)
        gain_in[...] += share[0:8] + share[8:16]
        grad_tokens[p.y, at, :] = (d_after_own[at, :] + through).astype(BF16)
        return carry

    lax.fori_loop(0, SPAN // 16, back_rows, 0)
    spread_a = Spread(links, p, grad_tokens)
    spread_a.start()
    small_scatter.finish(store_small)
    small_gather = Gather(links, p, small_all, 128)
    small_gather.first()
    gain_y[p.y] = jnp.concatenate(
        [jnp.sum(gain_in[...], axis=0, keepdims=True), jnp.sum(gain_mid[...], axis=0, keepdims=True)], axis=0
    )
    y_keys = [links.go(gain_y.at[p.y], gain_y.at[p.y], device) for device in others_y]

    scatter.merge()
    small_gather.middle()
    small_gather.finish()
    small_gather.second()
    spread_a.forward()
    spread_b.forward()
    for d in (1, 2, 3):
        links.arrived(gain_y.at[lax.rem(p.y + 4 - d, 4)], y_keys[d - 1], others_y[0])
    gain_z[p.z] = gain_y[0] + gain_y[1] + gain_y[2] + gain_y[3]
    z_keys = [links.go(gain_z.at[p.z], gain_z.at[p.z], device) for device in others_z]
    scatter.turn()
    for d in (1, 2, 3):
        links.arrived(gain_z.at[lax.rem(p.z + 4 - d, 4)], z_keys[d - 1], others_z[0])
    gain_s[p.s] = gain_z[0] + gain_z[1] + gain_z[2] + gain_z[3]
    s_keys = [links.go(gain_s.at[p.s], gain_s.at[p.s], p.seq_at(d)) for d in range(1, 8)]
    small_gather.middle()
    small_gather.finish()
    scatter.merge_2()
    for d in range(1, 8):
        links.arrived(gain_s.at[p.seq_at(-d)["seq"]], s_keys[d - 1], p.seq_at(-d))
    total = gain_s[0]
    for s in range(1, 8):
        total = total + gain_s[s]
    gain_sums[...] = total
    spread_b.near()
    spread_b.far()
    small_gather.settle()
    for k, n in enumerate((20, 21, 22)):
        width = min(256, CHAN - 256 * k)
        value = small_all[n // 8, (n // 4) % 2, n % 4, 0:16, 0:width].astype(F32)
        small_sums[:, 256 * k : 256 * k + width] = value[0:8]
    for n in range(20):
        value = small_all[n // 8, (n // 4) % 2, n % 4].astype(F32)
        block_sums[64 * n : 64 * (n + 1), :] = value

    def store(base, value):
        grad_mix[base : base + 32, :] = value

    scatter.finish(store)
    spread_a.near()
    spread_a.far()
    links.drain()


def back_all(*operands):
    shape = jax.ShapeDtypeStruct
    tc = (TOKENS, CHAN)
    pair = [pltpu.VMEM((2, SPAN, HALF), BF16), pltpu.VMEM((2, SPAN, WIDTH), BF16)]
    return pl.pallas_call(
        back_kernel,
        out_shape=[
            shape((ROWS, SPAN, WIDTH), BF16),
            shape((ROWS, SPAN, WIDTH), BF16),
            shape((64, MIX_COLS), F32),
            shape((8, CHAN), F32),
            shape((2 * HEADS * BLK, 256), F32),
            shape((2, WIDTH), F32),
        ],
        in_specs=[anyspace()] * 14 + [vmem()] + [anyspace()] * 2 + [vmem()] * 3 + [smem()],
        out_specs=[vmem()] * 6,
        scratch_shapes=[
            pltpu.VMEM((TOKENS, MLP), BF16),
            pltpu.VMEM(tc, F32),
            pltpu.VMEM(tc, F32),
            pltpu.VMEM((ROWS, PAD + SPAN, CHAN), F32),
            pltpu.VMEM(tc, F32),
            pltpu.VMEM(tc, F32),
            pltpu.VMEM(tc, BF16),
            pltpu.VMEM(tc, BF16),
            pltpu.VMEM((TOKENS, WIDTH), BF16),
            pltpu.VMEM((SPAN, WIDTH), F32),
            pltpu.VMEM((4, 2, 4, 64, MIX_COLS), BF16),
            pltpu.VMEM((4, 2, 4, 64, SMALL), BF16),
            pltpu.VMEM((SPAN, WIDTH), BF16),
            pltpu.VMEM((SPAN, WIDTH), BF16),
            pltpu.VMEM((ROWS, SPAN, WIDTH), BF16),
            pltpu.VMEM((ROWS, SPAN, WIDTH), BF16),
            pltpu.VMEM((ROWS, SPAN, WIDTH), BF16),
            pltpu.VMEM((SPAN, WIDTH), F32),
            pltpu.VMEM((8, WIDTH), F32),
            pltpu.VMEM(tc, F32),
            pltpu.VMEM(tc, F32),
            pltpu.VMEM((TOKENS, 2 * CHAN), BF16),
            pltpu.VMEM((TOKENS, 2 * CHAN), BF16),
            pltpu.VMEM((8, CHAN), F32),
            pltpu.VMEM((ROWS, PAD, CHAN), F32),
            pltpu.VMEM((ROWS, PAD, CHAN), F32),
            pltpu.VMEM((8, CHAN), F32),
            pltpu.VMEM((8, 8, CHAN), F32),
            pltpu.VMEM((8, CHAN), F32),
        ]
        + pair * 2
        + Scatter.scratch(MIX_COLS)
        + Scatter.scratch(SMALL)
        + [
            pltpu.VMEM((4, 2, 4, 64, SMALL), BF16),
            pltpu.VMEM((8, WIDTH), F32),
            pltpu.VMEM((4, 2, WIDTH), F32),
            pltpu.VMEM((8, 2, WIDTH), F32),
            pltpu.VMEM((4, 2, WIDTH), F32),
            pltpu.SemaphoreType.DMA((15,)),
            pltpu.SemaphoreType.DMA((8,)),
            pltpu.SemaphoreType.DMA((184,)),
            pltpu.SemaphoreType.DMA((184,)),
        ],
        compiler_params=params(2),
        name="back_all",
    )(*operands)


def finish_kernel(
    block_in,
    tokens_in,
    mix_sum,
    small,
    blocks_in,
    gains_in,
    mlp_sum,
    decay_param,
    block_out,
    grad_tokens,
    grad_gains,
    grad_mix_in,
    grad_mix_out,
    grad_conv,
    grad_conv_bias,
    grad_blocks,
    grad_bias,
    grad_decay,
    grad_mlp_in,
    grad_mlp_out,
):
    step = pl.program_id(0)
    block_out[...] = block_in[...]
    grad_tokens[...] = tokens_in[...]
    for h in range(HEADS):

        @pl.when(step == h)
        def _():
            for j in range(2):
                grad_blocks[j, 0] = blocks_in[j, 0, :, 32 * h : 32 * h + BLK]

    @pl.when(step == 0)
    def _():
        grad_gains[...] = gains_in[...]
        for j in range(2):
            grad_mix_in[j] = mix_sum[:, j * CHAN : (j + 1) * CHAN]
        grad_mix_out[...] = mix_sum[:, 2 * CHAN :]
        grad_conv[...] = small[0:CONV, :]
        grad_bias[...] = small[CONV + 1 : CONV + 3, :]
        grad_conv_bias[...] = small[CONV : CONV + 1, :].reshape(CHAN)
        slope = jax.nn.sigmoid(decay_param[...].astype(F32))
        grad_decay[...] = small[CONV + 3 : CONV + 4, :].reshape(CHAN) * slope
        for f in range(CHUNKS):
            lo, at = 3 * f * CHUNK, pl.ds(f * CHUNK, CHUNK)
            for j in range(2):
                grad_mlp_in[j, :, at] = mlp_sum[:, lo + j * CHUNK : lo + (j + 1) * CHUNK].astype(F32)
            grad_mlp_out[:, at] = mlp_sum[:, lo + 2 * CHUNK : lo + 3 * CHUNK].astype(F32)


def finish(*operands):
    shape = jax.ShapeDtypeStruct
    row = lambda width: pl.BlockSpec((1, SPAN, width), lambda i: (i, 0, 0))
    whole = lambda *dims: pl.BlockSpec(dims, lambda i: (0,) * len(dims))
    head = lambda width: pl.BlockSpec((2, 1, BLK, width), lambda i: (0, i, 0, 0))
    return pl.pallas_call(
        finish_kernel,
        grid=(ROWS,),
        out_shape=[
            shape((ROWS, SPAN, WIDTH), BF16),
            shape((ROWS, SPAN, WIDTH), BF16),
            shape((2, WIDTH), F32),
            shape((2, 64, CHAN), F32),
            shape((64, CHAN), F32),
            shape((CONV, CHAN), F32),
            shape((CHAN,), F32),
            shape((2, HEADS, BLK, BLK), F32),
            shape((2, CHAN), F32),
            shape((CHAN,), F32),
            shape((2, 64, MLP), F32),
            shape((64, MLP), F32),
        ],
        in_specs=[
            row(WIDTH),
            row(WIDTH),
            whole(64, MIX_COLS),
            whole(8, CHAN),
            head(256),
            whole(2, WIDTH),
            whole(64, MLP_COLS),
            whole(CHAN),
        ],
        out_specs=[
            row(WIDTH),
            row(WIDTH),
            whole(2, WIDTH),
            whole(2, 64, CHAN),
            whole(64, CHAN),
            whole(CONV, CHAN),
            whole(CHAN),
            head(BLK),
            whole(2, CHAN),
            whole(CHAN),
            whole(2, 64, MLP),
            whole(64, MLP),
        ],
        compiler_params=pltpu.CompilerParams(vmem_limit_bytes=VMEM_BYTES),
        name="finish",
    )(*operands)


def per_device(
    tokens,
    init_state,
    conv_state,
    fresh_rows,
    doc_start,
    norm_gains,
    mix_in,
    mix_out,
    conv_weight,
    conv_bias,
    gate_blocks,
    gate_bias,
    decay_param,
    mlp_in,
    mlp_out,
    cotangent,
):
    (
        mix_full,
        mlp_full,
        states,
        pre,
        ext,
        decay_g,
        input_g,
        conv_low,
        mixed,
        normed_in,
        entering,
        vectors,
        gate_w,
        normed_mid,
        after_own,
    ) = mix_forward(
        tokens.reshape(TOKENS, WIDTH),
        mix_in,
        mix_out.T,
        mlp_in,
        mlp_out.T,
        init_state,
        conv_state.transpose(1, 0, 2),
        fresh_rows,
        doc_start,
        norm_gains,
        conv_weight,
        conv_bias,
        gate_bias,
        decay_param,
        gate_blocks,
    )
    d_gate, d_up, hidden, grad_mlp, states_out = mlp_all(
        normed_mid.reshape(TOKENS, WIDTH),
        cotangent.reshape(TOKENS, WIDTH),
        mlp_full.reshape(WIDTH, MLP_COLS),
        states.reshape(ROWS, SPAN, CHAN),
    )
    grad_mlp = lax.psum_scatter(grad_mlp, ("seq", "dp"), scatter_dimension=0, tiled=True)
    grad_tokens, block_out, grad_mix, small, blocks, grad_gains = back_all(
        d_gate.reshape(2, 4, 64, MLP),
        d_up.reshape(2, 4, 64, MLP),
        hidden,
        mlp_full,
        mix_full,
        states,
        pre,
        ext,
        decay_g,
        input_g,
        conv_low,
        mixed,
        normed_in,
        after_own,
        entering,
        tokens,
        cotangent,
        norm_gains,
        vectors,
        gate_w,
        doc_start,
    )
    (
        block_out,
        grad_tokens,
        grad_gains,
        grad_mix_in,
        grad_mix_out,
        grad_conv,
        grad_conv_bias,
        grad_blocks,
        grad_bias,
        grad_decay,
        grad_mlp_in,
        grad_mlp_out,
    ) = finish(
        block_out,
        grad_tokens,
        grad_mix,
        small,
        blocks.reshape(2, HEADS, BLK, 256),
        grad_gains,
        grad_mlp,
        decay_param,
    )
    return (
        block_out,
        states_out,
        grad_tokens,
        grad_gains,
        grad_mix_in,
        grad_mix_out.T,
        grad_conv,
        grad_conv_bias,
        grad_blocks,
        grad_bias,
        grad_decay,
        grad_mlp_in,
        grad_mlp_out.T,
    )


def solution(mesh):
    in_specs = (
        P("dp", "seq", None),
        P("dp", "tensor"),
        P("dp", None, "tensor"),
        P("dp"),
        P("dp"),
        P(),
        P(None, ("seq", "dp"), "tensor"),
        P("tensor", ("seq", "dp")),
        P(None, "tensor"),
        P("tensor"),
        P(None, "tensor", None, None),
        P(None, "tensor"),
        P("tensor"),
        P(None, ("seq", "dp"), "tensor"),
        P("tensor", ("seq", "dp")),
        P("dp", "seq", None),
    )
    out_specs = (
        P("dp", "seq", None),
        P("dp", "seq", "tensor"),
        P("dp", "seq", None),
        P(),
        P(None, ("seq", "dp"), "tensor"),
        P("tensor", ("seq", "dp")),
        P(None, "tensor"),
        P("tensor"),
        P(None, "tensor", None, None),
        P(None, "tensor"),
        P("tensor"),
        P(None, ("seq", "dp"), "tensor"),
        P("tensor", ("seq", "dp")),
    )
    return jax.shard_map(
        per_device, mesh=mesh, in_specs=in_specs, out_specs=out_specs, check_vma=False
    )
```

```python
import functools

import jax
import jax.numpy as jnp
from jax import lax
from jax.experimental import pallas as pl
from jax.experimental.pallas import tpu as pltpu
from jax.sharding import PartitionSpec as P

MESH = pl.DeviceIdType.MESH
F32 = jnp.float32
BF16 = jnp.bfloat16
VMEM_BYTES = 60 * 2**20

CONV = 4
ROWS = 4
SPAN = 128
TOKENS = ROWS * SPAN
WIDTH = 2048
CHAN = 640
HEADS = 4
BLK = 160
MLP = 1536
MIX_COLS = 3 * CHAN
MLP_COLS = 3 * MLP
MLP_CUT = 2304
CHUNK = 256
CHUNKS = MLP // CHUNK
SMALL = 256
LANES = 128
GROUPS = CHAN // LANES
PAD = 8

epsilon = 1e-06
root_floor = 0.001
rate_scale = 8.0


class Place:
    def __init__(self):
        self.s = lax.axis_index("seq")
        self.z = lax.axis_index("dp")
        self.y = lax.axis_index("tensor")
        self.x, self.c = lax.div(self.s, 2), lax.rem(self.s, 2)
        x, c, z, y = self.x, self.c, self.z, self.y
        self.xr, self.xl = lax.rem(x + 1, 4), lax.rem(x + 3, 4)
        self.zr, self.zl = lax.rem(z + 1, 4), lax.rem(z + 3, 4)
        self.yr, self.yl, self.y2 = lax.rem(y + 1, 4), lax.rem(y + 3, 4), lax.rem(y + 2, 4)
        self.XR, self.XL = {"seq": self.xr * 2 + c}, {"seq": self.xl * 2 + c}
        self.ZR, self.ZL = {"dp": self.zr}, {"dp": self.zl}
        self.YR, self.YL = {"tensor": self.yr}, {"tensor": self.yl}
        self.SIB = {"seq": x * 2 + 1 - c}

    def seq_at(self, distance):
        return {"seq": lax.rem(self.s + distance + 8, 8)}


def greet(devices):
    barrier = pltpu.get_barrier_semaphore()
    for device in devices:
        pl.semaphore_signal(barrier, inc=1, device_id=device, device_id_type=MESH)
    pl.semaphore_wait(barrier, len(devices))


class Links:
    def __init__(self, send, recv):
        self.send, self.recv = send, recv
        self.count = 0
        self.keyed = {}

    def go(self, src, dst, device):
        k = self.count
        self.count += 1
        copy = pltpu.make_async_remote_copy(
            src_ref=src,
            dst_ref=dst,
            send_sem=self.send.at[k],
            recv_sem=self.recv.at[k],
            device_id=device,
            device_id_type=MESH,
        )
        copy.start()
        self.keyed[k] = copy
        return k

    def arrived(self, view, k, device):
        pltpu.make_async_remote_copy(
            src_ref=view,
            dst_ref=view,
            send_sem=self.send.at[k],
            recv_sem=self.recv.at[k],
            device_id=device,
            device_id_type=MESH,
        ).wait_recv()

    def drain(self):
        for copy in self.keyed.values():
            copy.wait_send()
        self.keyed = {}

    def sent(self, keys):
        for k in keys:
            self.keyed.pop(k).wait_send()


class Gather:
    def __init__(self, links, place, out, cut):
        self.links, self.p = links, place
        self.out_a = out.at[:, :, :, :, pl.ds(0, cut)]
        self.out_b = out.at[:, :, :, :, pl.ds(cut, out.shape[-1] - cut)]
        self.to_sibling = []

    def _pass_on(self, view_of):
        k = self.links.go(view_of(self.p.c), view_of(self.p.c), self.p.SIB)
        self.to_sibling.append((view_of, k))

    def _ring(self, blk, i, right, left):
        links, p = self.links, self.p
        c = p.c
        ir, il, i2 = lax.rem(i + 1, 4), lax.rem(i + 3, 4), lax.rem(i + 2, 4)
        a, b = pl.ds(0, 32), pl.ds(32, 32)
        k0 = links.go(blk(c, i, a), blk(c, i, a), right)
        k1 = links.go(blk(c, i, b), blk(c, i, b), left)
        k2 = links.go(blk(c, i, b), blk(c, i, b), right)
        k3 = links.go(blk(c, i, a), blk(c, i, a), left)
        later = []

        def middle():
            links.arrived(blk(c, il, a), k0, left)
            later.append(links.go(blk(c, il, a), blk(c, il, a), right))
            links.arrived(blk(c, ir, b), k1, right)
            later.append(links.go(blk(c, ir, b), blk(c, ir, b), left))
            self._pass_on(lambda cc: blk(cc, il, a))
            self._pass_on(lambda cc: blk(cc, ir, b))

        def finish():
            for view, k, source in (
                (lambda cc: blk(cc, il, b), k2, left),
                (lambda cc: blk(cc, ir, a), k3, right),
                (lambda cc: blk(cc, i2, a), later[0], left),
                (lambda cc: blk(cc, i2, b), later[1], right),
            ):
                links.arrived(view(c), k, source)
                self._pass_on(view)

        return middle, finish

    def first(self):
        p, a, b = self.p, self.out_a, self.out_b
        self.ring_a = self._ring(lambda cc, j, r: a.at[j, cc, p.z, r], p.x, p.XR, p.XL)
        self.ring_b = self._ring(lambda cc, j, r: b.at[p.x, cc, j, r], p.z, p.ZR, p.ZL)
        self._pass_on(lambda cc: a.at[p.x, cc, p.z])
        self._pass_on(lambda cc: b.at[p.x, cc, p.z])

    def second_z(self):
        p, a = self.p, self.out_a
        self.ring_a = self._ring(lambda cc, j, r: a.at[:, cc, j, r], p.z, p.ZR, p.ZL)

    def second_x(self):
        p, b = self.p, self.out_b
        self.ring_b = self._ring(lambda cc, j, r: b.at[j, cc, :, r], p.x, p.XR, p.XL)

    def second(self):
        self.second_z()
        self.second_x()

    def middle(self):
        self.ring_a[0]()
        self.ring_b[0]()

    def finish(self):
        self.ring_a[1]()
        self.ring_b[1]()

    def settle(self):
        for view_of, k in self.to_sibling:
            self.links.arrived(view_of(1 - self.p.c), k, self.p.SIB)


CA, CB = pl.ds(0, WIDTH // 2), pl.ds(WIDTH // 2, WIDTH // 2)
HALF = WIDTH // 2


class Reduce:
    def __init__(self, links, place, part, far, near, start=0, size=SPAN):
        self.links, self.p, self.part, self.far, self.near = links, place, part, far, near
        self.rows, self.span = pl.ds(start, size), slice(start, start + size)

    def send_first(self):
        p, part, near, rows = self.p, self.part, self.near, self.rows
        self.k0 = self.links.go(part.at[p.y2, rows, CA], self.far.at[0, rows], p.YR)
        self.k3 = self.links.go(part.at[p.yl, rows, CA], near.at[1, rows, CA], p.YL)

    def send_second(self):
        self.send_second_far()
        self.send_second_near()

    def send_second_far(self):
        p, part, rows = self.p, self.part, self.rows
        self.k1 = self.links.go(part.at[p.y2, rows, CB], self.far.at[1, rows], p.YL)

    def send_second_near(self):
        p, part, near, rows = self.p, self.part, self.near, self.rows
        self.k2 = self.links.go(part.at[p.yr, rows, CB], near.at[0, rows, CB], p.YR)

    def merge(self):
        p, part, near, far, rows, span = self.p, self.part, self.near, self.far, self.rows, self.span
        self.links.arrived(far.at[0, rows], self.k0, p.YL)
        far[0, span] = (far[0, span].astype(F32) + part[p.yr, span, 0:HALF].astype(F32)).astype(BF16)
        self.k4 = self.links.go(far.at[0, rows], near.at[0, rows, CA], p.YR)
        self.links.arrived(far.at[1, rows], self.k1, p.YR)
        far[1, span] = (far[1, span].astype(F32) + part[p.yl, span, HALF:WIDTH].astype(F32)).astype(BF16)
        self.k5 = self.links.go(far.at[1, rows], near.at[1, rows, CB], p.YL)

    def settle(self):
        p, near, rows = self.p, self.near, self.rows
        self.links.arrived(near.at[0, rows, CB], self.k2, p.YL)
        self.links.arrived(near.at[1, rows, CA], self.k3, p.YR)
        self.links.arrived(near.at[0, rows, CA], self.k4, p.YL)
        self.links.arrived(near.at[1, rows, CB], self.k5, p.YR)

    def keys(self):
        return [self.k0, self.k1, self.k2, self.k3, self.k4, self.k5]


class Spread:
    def __init__(self, links, place, out, start=0, size=SPAN):
        self.links, self.p, self.out, self.rows = links, place, out, pl.ds(start, size)

    def _go(self, y, columns, device):
        view = self.out.at[y, self.rows, columns]
        return self.links.go(view, view, device)

    def _wait(self, y, columns, k, device):
        self.links.arrived(self.out.at[y, self.rows, columns], k, device)

    def start(self):
        self.start_first()
        self.start_second()

    def start_first(self):
        p = self.p
        self.k0 = self._go(p.y, CA, p.YR)
        self.k1 = self._go(p.y, CB, p.YL)

    def start_second(self):
        p = self.p
        self.k2 = self._go(p.y, CB, p.YR)
        self.k3 = self._go(p.y, CA, p.YL)

    def forward(self):
        p = self.p
        self._wait(p.yl, CA, self.k0, p.YL)
        self.k4 = self._go(p.yl, CA, p.YR)
        self._wait(p.yr, CB, self.k1, p.YR)
        self.k5 = self._go(p.yr, CB, p.YL)

    def near(self):
        p = self.p
        self._wait(p.yl, CB, self.k2, p.YL)
        self._wait(p.yr, CA, self.k3, p.YR)

    def far(self):
        p = self.p
        self._wait(p.y2, CA, self.k4, p.YL)
        self._wait(p.y2, CB, self.k5, p.YR)


def dot(a, b):
    return jnp.dot(a, b, preferred_element_type=F32)


def dot_nt(a, b):
    return lax.dot_general(a, b, (((1,), (1,)), ((), ())), preferred_element_type=F32)


def dot_tn(a, b):
    return lax.dot_general(a, b, (((0,), (0,)), ((), ())), preferred_element_type=F32)


GELU_C = 0.7978845608028654
GELU_A = 0.044715


def gelu(v):
    return 0.5 * v * (1.0 + jnp.tanh(GELU_C * (v + GELU_A * v * v * v)))


def gelu_pair(v):
    t = jnp.tanh(GELU_C * (v + GELU_A * v * v * v))
    value = 0.5 * v * (1.0 + t)
    slope = 0.5 * (1.0 + t) + 0.5 * v * (1.0 - t * t) * (GELU_C * (1.0 + 3.0 * GELU_A * v * v))
    return value, slope


def tile_scan(a, b, reverse):
    row = lax.broadcasted_iota(jnp.int32, a.shape, 1)
    for step in (1, 2, 4):
        if reverse:
            shift, valid = 8 - step, row < 8 - step
        else:
            shift, valid = step, row >= step
        a_near, b_near = pltpu.roll(a, shift, 1), pltpu.roll(b, shift, 1)
        b = jnp.where(valid, a * b_near + b, b)
        a = jnp.where(valid, a * a_near, a)
    return a, b


def row_scan(a, b, reverse):
    tiles = SPAN // 8
    a, b = tile_scan(a.reshape(tiles, 8, LANES), b.reshape(tiles, 8, LANES), reverse)
    edge = 0 if reverse else 7
    order = range(tiles - 1, -1, -1) if reverse else range(tiles)
    out_a, out_b = [None] * tiles, [None] * tiles
    carry_a = carry_b = None
    for k in order:
        ak, bk = a[k], b[k]
        if carry_a is not None:
            bk = ak * carry_b + bk
            ak = ak * carry_a
        out_a[k], out_b[k] = ak, bk
        carry_a, carry_b = ak[edge : edge + 1], bk[edge : edge + 1]
    return jnp.concatenate(out_a, axis=0), jnp.concatenate(out_b, axis=0), carry_a, carry_b


def put_pair(ref, at, r, first, second):
    row = lax.broadcasted_iota(jnp.int32, (8, LANES), 0)
    ref[:, at] = jnp.where(row == r, first, jnp.where(row == ROWS + r, second, ref[:, at]))


def take_row(ref, at, r):
    row = lax.broadcasted_iota(jnp.int32, (8, LANES), 0)
    return jnp.sum(jnp.where(row == r, ref[:, at], 0.0), axis=0, keepdims=True)


def assemble_vectors(vectors, conv_weight, conv_bias, gate_bias, decay_param):
    vectors[0:4, :] = conv_weight[...].astype(F32)
    vectors[4:5, :] = conv_bias[...].astype(F32).reshape(1, CHAN)
    vectors[5:7, :] = gate_bias[...].astype(F32)
    decay = decay_param[...].astype(F32).reshape(1, CHAN)
    vectors[7:8, :] = -rate_scale * jnp.log1p(jnp.exp(decay))


def assemble_gates(gate_w, gate_blocks):
    for j in range(2):
        for h in range(HEADS):
            before, behind = 32 * h, 96 - 32 * h
            block = gate_blocks[j, h].astype(F32)
            parts = [jnp.zeros((BLK, before), F32)] if before else []
            parts += [block] + ([jnp.zeros((BLK, behind), F32)] if behind else [])
            wide = jnp.concatenate(parts, axis=1)
            tall = [jnp.zeros((before, 256), F32)] if before else []
            tall += [wide] + ([jnp.zeros((behind, 256), F32)] if behind else [])
            gate_w[j, h] = jnp.concatenate(tall, axis=0).astype(BF16)


def mix_forward_kernel(
    tokens,
    mix_in,
    mix_out,
    mlp_in,
    mlp_out,
    init_state,
    conv_state,
    fresh_rows,
    doc_start,
    gain_rows,
    conv_weight,
    conv_bias,
    gate_bias,
    decay_param,
    gate_blocks,
    mix_full_out,
    mlp_full,
    states_out,
    pre_out,
    ext_out,
    decay_out,
    input_out,
    conv_out,
    mixed_out,
    normed_in_out,
    entering_out,
    vectors_out,
    gate_w_out,
    normed_mid,
    after_own,
    mlp_own,
    gains,
    vectors,
    gate_w,
    mix_full,
    normed_in,
    pre,
    ext,
    decay_g,
    input_g,
    conv_low,
    cum_a,
    loc_b,
    states,
    mixed,
    rim_send,
    rim_recv,
    totals,
    totals_in,
    entering,
    part,
    far,
    near,
    local,
    send,
    recv,
):
    p = Place()
    links = Links(send, recv)
    mine = mix_full.at[p.x, p.c, p.z]
    for j in range(2):
        mine[:, j * CHAN : (j + 1) * CHAN] = mix_in[j]
    mine[:, 2 * CHAN :] = mix_out[...]
    greet([p.seq_at(d) for d in range(1, 8)] + [p.ZR, p.ZL, p.YR, p.YL])
    in_gather = Gather(links, p, mix_full.at[:, :, :, :, pl.ds(0, 2 * CHAN)], CHAN)
    out_gather = Gather(links, p, mix_full.at[:, :, :, :, pl.ds(2 * CHAN, CHAN)], 384)
    mlp_gather = Gather(links, p, mlp_full, MLP_CUT)
    in_gather.first()
    for j in range(2):
        mlp_own[:, j * MLP : (j + 1) * MLP] = mlp_in[j]
    mlp_own[:, 2 * MLP :] = mlp_out[...]
    own_mlp = pltpu.make_async_copy(mlp_own, mlp_full.at[p.x, p.c, p.z], local.at[0])
    own_mlp.start()
    gains[...] = gain_rows[...].astype(F32)
    assemble_vectors(vectors, conv_weight, conv_bias, gate_bias, decay_param)
    assemble_gates(gate_w, gate_blocks)

    def norm_rows(first, last):
        def one(k, carry):
            at = pl.ds(pl.multiple_of(k * 32, 32), 32)
            stream = tokens[at, :].astype(F32)
            scale = lax.rsqrt(jnp.mean(stream * stream, axis=-1, keepdims=True) + epsilon)
            normed_in[at, :] = (stream * scale * gains[0:1, :]).astype(BF16)
            return carry

        lax.fori_loop(first, last, one, 0)

    norm_rows(0, 8)
    in_gather.middle()
    in_gather.finish()
    in_gather.second()
    own_mlp.wait()
    norm_rows(8, 16)
    in_gather.middle()
    out_gather.first()
    mlp_gather.first()
    in_gather.finish()
    out_gather.middle()
    out_gather.finish()
    out_gather.second()
    in_gather.settle()
    saves = []

    def save(src, dst):
        copy = pltpu.make_async_copy(src, dst, local.at[2 + len(saves)])
        copy.start()
        saves.append(copy)

    save(normed_in, normed_in_out)
    save(vectors, vectors_out)
    save(gate_w, gate_w_out)

    def project(n, carry):
        at = pl.ds(pl.multiple_of(n * 256, 256), 256)
        pre[:, at] = dot(normed_in[...], mix_full[:, :, :, :, at].reshape(WIDTH, 256))
        return carry

    lax.fori_loop(2, 5, project, 0)
    for r in range(ROWS):
        ext[r, PAD:, :] = pre[r * SPAN : (r + 1) * SPAN, CHAN : 2 * CHAN].astype(BF16).astype(F32)
        rim_send[r] = ext[r, SPAN : SPAN + PAD, :]
    k_rim = links.go(rim_send, rim_recv, p.seq_at(1))
    lax.fori_loop(0, 2, project, 0)
    save(pre.at[:, pl.ds(0, CHAN)], pre_out)
    links.arrived(rim_recv, k_rim, p.seq_at(-1))
    at_start = p.s == 0
    for r in range(ROWS):
        keep = (1 - fresh_rows[r]).astype(F32)
        ext[r, 0:PAD, :] = jnp.where(at_start, 0.0, rim_recv[r])
        for j in range(CONV - 1):
            at = slice(PAD - 3 + j, PAD - 2 + j)
            first_rim = conv_state[j, r : r + 1, :].astype(F32) * keep
            ext[r, at, :] = jnp.where(at_start, first_rim, rim_recv[r, at, :])
    offset = p.s * SPAN

    def conv_chunk(i, carry):
        r, g = lax.rem(i, ROWS), lax.div(i, ROWS)
        at = pl.ds(pl.multiple_of(g * LANES, LANES), LANES)
        place = offset + lax.broadcasted_iota(jnp.int32, (SPAN, LANES), 0)
        begin = doc_start[r]
        here = place >= begin
        total = jnp.zeros((SPAN, LANES), F32) + vectors[4:5, at]
        for k in range(CONV):
            value = ext[r, PAD - 3 + k : PAD - 3 + k + SPAN, at]
            same = (place - (3 - k) >= begin) == here
            total = total + vectors[k : k + 1, at] * jnp.where(same, value, 0.0)
        rows = pl.ds(pl.multiple_of(r * SPAN, SPAN), SPAN)
        conv_low[rows, at] = total.astype(BF16)
        return carry

    lax.fori_loop(0, ROWS * GROUPS, conv_chunk, 0)
    save(ext, ext_out)
    save(conv_low, conv_out)

    for j, target in ((0, decay_g), (1, input_g)):
        held = None
        for g in range(GROUPS):
            total = held
            if g < HEADS:
                product = dot(conv_low[:, g * LANES : g * LANES + 256], gate_w[j, g])
                total = product[:, :LANES] if held is None else held + product[:, :LANES]
                held = product[:, LANES:]
            target[:, g * LANES : (g + 1) * LANES] = total

    def gate_chunk(i, carry):
        r, g = lax.rem(i, ROWS), lax.div(i, ROWS)
        at = pl.ds(pl.multiple_of(g * LANES, LANES), LANES)
        rows = pl.ds(pl.multiple_of(r * SPAN, SPAN), SPAN)
        gate_d = jax.nn.sigmoid(decay_g[rows, at] + vectors[5:6, at])
        gate_i = jax.nn.sigmoid(input_g[rows, at] + vectors[6:7, at])
        decay_g[rows, at] = gate_d
        input_g[rows, at] = gate_i
        decay_now = jnp.exp(gate_d * vectors[7:8, at])
        root = jnp.sqrt(jnp.maximum(1.0 - decay_now * decay_now, root_floor))
        fed = root * gate_i * conv_low[rows, at].astype(F32)
        place = offset + lax.broadcasted_iota(jnp.int32, (SPAN, LANES), 0)
        carried = jnp.where(place == doc_start[r], 0.0, decay_now)
        a, b, last_a, last_b = row_scan(carried, fed, False)
        cum_a[rows, at] = a
        loc_b[rows, at] = b
        put_pair(totals, at, r, last_a, last_b)
        return carry

    totals[...] = jnp.zeros_like(totals)
    lax.fori_loop(0, ROWS * GROUPS, gate_chunk, 0)
    keys = [links.go(totals, totals_in.at[p.s], p.seq_at(d)) for d in range(1, 8)]
    save(decay_g, decay_out)
    save(input_g, input_out)
    out_gather.middle()
    out_gather.finish()
    row = lax.broadcasted_iota(jnp.int32, (ROWS, CHAN), 0)
    kept = jnp.zeros((ROWS, CHAN), F32)
    for r in range(ROWS):
        kept = jnp.where(row == r, (1 - fresh_rows[r]).astype(F32), kept)
    state = init_state[...] * kept
    for d in range(1, 8):
        links.arrived(totals_in.at[p.seq_at(-d)["seq"]], keys[d - 1], p.seq_at(-d))
    mlp_gather.middle()
    mlp_gather.finish()
    mlp_gather.second()
    totals_in[p.s] = totals[...]
    for source in range(7):
        both = totals_in[source]
        state = jnp.where(source < p.s, both[0:ROWS] * state + both[ROWS:], state)
    entering[0:ROWS, :] = state
    entering[ROWS:, :] = jnp.zeros((8 - ROWS, CHAN), F32)

    def state_chunk(i, carry):
        r, g = lax.rem(i, ROWS), lax.div(i, ROWS)
        at = pl.ds(pl.multiple_of(g * LANES, LANES), LANES)
        rows = pl.ds(pl.multiple_of(r * SPAN, SPAN), SPAN)
        value = loc_b[rows, at] + cum_a[rows, at] * take_row(entering, at, r)
        states[rows, at] = value
        mixed[rows, at] = (value * gelu(pre[rows, at])).astype(BF16)
        return carry

    lax.fori_loop(0, ROWS * GROUPS, state_chunk, 0)
    save(states, states_out)
    save(mixed, mixed_out)
    save(entering, entering_out)

    out_gather.settle()
    save(mix_full, mix_full_out)

    def partial(n, carry):
        weights = mix_full[lax.div(n, 2), lax.rem(n, 2), :, :, 2 * CHAN :].reshape(256, CHAN)
        product = dot_nt(mixed[...], weights).astype(BF16)
        part[:, :, pl.ds(pl.multiple_of(n * 256, 256), 256)] = product.reshape(ROWS, SPAN, 256)
        return carry

    reduce = Reduce(links, p, part, far, near)
    lax.fori_loop(0, 4, partial, 0)
    reduce.send_first()
    lax.fori_loop(4, 8, partial, 0)
    reduce.send_second()
    mlp_gather.middle()
    reduce.merge()
    reduce.settle()

    def norm_mid(k, carry):
        at = pl.ds(pl.multiple_of(k * 16, 16), 16)
        total = part[p.y, at, :].astype(F32) + near[0, at, :].astype(F32) + near[1, at, :].astype(F32)
        row = pl.ds(pl.multiple_of(p.y * SPAN + k * 16, 16), 16)
        stream = tokens[row, :].astype(F32) + total
        scale = lax.rsqrt(jnp.mean(stream * stream, axis=-1, keepdims=True) + epsilon)
        after_own[at, :] = stream
        normed_mid[p.y, at, :] = (stream * scale * gains[1:2, :]).astype(BF16)
        return carry

    lax.fori_loop(0, SPAN // 16, norm_mid, 0)
    spread = Spread(links, p, normed_mid)
    spread.start()
    mlp_gather.finish()
    spread.forward()
    spread.near()
    spread.far()
    mlp_gather.settle()
    for copy in saves:
        copy.wait()
    links.drain()


def params(collective_id):
    return pltpu.CompilerParams(
        collective_id=collective_id, has_side_effects=True, vmem_limit_bytes=VMEM_BYTES
    )


def vmem():
    return pl.BlockSpec(memory_space=pltpu.VMEM)


def smem():
    return pl.BlockSpec(memory_space=pltpu.SMEM)


def anyspace():
    return pl.BlockSpec(memory_space=pl.ANY)


def mix_forward(*operands):
    shape = jax.ShapeDtypeStruct
    tc = (TOKENS, CHAN)
    ext_shape = (ROWS, PAD + SPAN, CHAN)
    outs = [
        shape((4, 2, 4, 64, MIX_COLS), BF16),
        shape((4, 2, 4, 64, MLP_COLS), BF16),
        shape(tc, F32),
        shape(tc, F32),
        shape(ext_shape, F32),
        shape(tc, F32),
        shape(tc, F32),
        shape(tc, BF16),
        shape(tc, BF16),
        shape((TOKENS, WIDTH), BF16),
        shape((8, CHAN), F32),
        shape((8, CHAN), F32),
        shape((2, HEADS, 256, 256), BF16),
        shape((ROWS, SPAN, WIDTH), BF16),
        shape((SPAN, WIDTH), F32),
    ]
    scratch = [
        pltpu.VMEM((64, MLP_COLS), BF16),
        pltpu.VMEM((2, WIDTH), F32),
        pltpu.VMEM((8, CHAN), F32),
        pltpu.VMEM((2, HEADS, 256, 256), BF16),
        pltpu.VMEM((4, 2, 4, 64, MIX_COLS), BF16),
        pltpu.VMEM((TOKENS, WIDTH), BF16),
        pltpu.VMEM((TOKENS, 2 * CHAN), F32),
        pltpu.VMEM(ext_shape, F32),
        pltpu.VMEM(tc, F32),
        pltpu.VMEM(tc, F32),
        pltpu.VMEM(tc, BF16),
        pltpu.VMEM(tc, F32),
        pltpu.VMEM(tc, F32),
        pltpu.VMEM(tc, F32),
        pltpu.VMEM(tc, BF16),
        pltpu.VMEM((ROWS, PAD, CHAN), F32),
        pltpu.VMEM((ROWS, PAD, CHAN), F32),
        pltpu.VMEM((8, CHAN), F32),
        pltpu.VMEM((8, 8, CHAN), F32),
        pltpu.VMEM((8, CHAN), F32),
        pltpu.VMEM((ROWS, SPAN, WIDTH), BF16),
        pltpu.VMEM((2, SPAN, HALF), BF16),
        pltpu.VMEM((2, SPAN, WIDTH), BF16),
        pltpu.SemaphoreType.DMA((20,)),
        pltpu.SemaphoreType.DMA((184,)),
        pltpu.SemaphoreType.DMA((184,)),
    ]
    return pl.pallas_call(
        mix_forward_kernel,
        out_shape=outs,
        in_specs=[vmem()] * 7 + [smem()] * 2 + [vmem()] * 6,
        out_specs=[anyspace()] * 13 + [vmem()] * 2,
        scratch_shapes=scratch,
        compiler_params=params(0),
        name="mix_forward",
    )(*operands)


def norm_back_rows(d_row, stream, gain_row):
    scale = lax.rsqrt(jnp.mean(stream * stream, axis=-1, keepdims=True) + epsilon)
    unit = stream * scale
    e = d_row * gain_row
    inner = jnp.mean(e * unit, axis=-1, keepdims=True)
    return scale * (e - unit * inner), d_row * unit


def own_sum(reduce, at):
    part, near = reduce.part, reduce.near
    return part[reduce.p.y, at, :].astype(F32) + near[0, at, :].astype(F32) + near[1, at, :].astype(F32)


def mlp_kernel(
    normed,
    upstream,
    gate_weights,
    up_weights,
    down_weights,
    states_in,
    d_gate_out,
    d_up_out,
    hidden_out,
    grads,
    states_out,
    normed_t,
    upstream_t,
    d_both,
):
    states_out[...] = states_in[...]

    @pl.when(pl.program_id(0) == 0)
    def _():
        def turn(n, carry):
            at = pl.ds(pl.multiple_of(n * 256, 256), 256)
            normed_t[at, :] = normed[:, at].T
            upstream_t[at, :] = upstream[:, at].T
            return carry

        lax.fori_loop(0, WIDTH // 256, turn, 0)

    gate = dot(normed[...], gate_weights[...])
    up = dot(normed[...], up_weights[...])
    d_hidden = dot(upstream[...], down_weights[...])
    act, slope = gelu_pair(gate)
    hidden = (act * up).astype(BF16)
    d_gate = (d_hidden * up * slope).astype(BF16)
    d_up = (d_hidden * act).astype(BF16)
    d_both[:, 0:CHUNK] = d_gate
    d_both[:, CHUNK : 2 * CHUNK] = d_up
    d_both[:, 2 * CHUNK :] = hidden
    d_gate_out[...] = d_gate
    d_up_out[...] = d_up
    hidden_out[...] = hidden

    def tile(n, carry):
        at = pl.ds(pl.multiple_of(n * 256, 256), 256)
        grads[at, 0 : 2 * CHUNK] = dot(normed_t[at, :], d_both[:, 0 : 2 * CHUNK]).astype(BF16)
        grads[at, 2 * CHUNK :] = dot(upstream_t[at, :], d_both[:, 2 * CHUNK :]).astype(BF16)
        return carry

    lax.fori_loop(0, WIDTH // 256, tile, 0, unroll=4)


def mlp_all(normed, upstream, weights, states):
    shape = jax.ShapeDtypeStruct
    whole = pl.BlockSpec((TOKENS, WIDTH), lambda f: (0, 0))
    part = lambda j: pl.BlockSpec((WIDTH, CHUNK), lambda f: (0, j * CHUNKS + f))
    block = pl.BlockSpec((WIDTH, 3 * CHUNK), lambda f: (0, f))
    column = pl.BlockSpec((TOKENS, CHUNK), lambda f: (0, f))
    row = pl.BlockSpec((1, SPAN, CHAN), lambda f: (jnp.minimum(f, ROWS - 1), 0, 0))
    return pl.pallas_call(
        mlp_kernel,
        grid=(CHUNKS,),
        out_shape=[shape((TOKENS, MLP), BF16)] * 3
        + [shape((WIDTH, MLP_COLS), BF16), shape((ROWS, SPAN, CHAN), F32)],
        in_specs=[whole, whole, part(0), part(1), part(2), row],
        out_specs=[column] * 3 + [block, row],
        scratch_shapes=[
            pltpu.VMEM((WIDTH, TOKENS), BF16),
            pltpu.VMEM((WIDTH, TOKENS), BF16),
            pltpu.VMEM((TOKENS, 3 * CHUNK), BF16),
        ],
        compiler_params=pltpu.CompilerParams(vmem_limit_bytes=VMEM_BYTES),
        cost_estimate=pl.CostEstimate(
            flops=12 * TOKENS * WIDTH * MLP, bytes_accessed=4 * WIDTH * MLP_COLS, transcendentals=TOKENS * MLP
        ),
        name="mlp_all",
    )(normed, upstream, weights, weights, weights, states)


class Scatter:
    def __init__(self, links, place, grads, sib, far, near, half_a, half_b, far_2, near_2):
        self.links, self.p = links, place
        self.grads, self.sib = grads, sib
        self.far, self.near, self.far_2, self.near_2 = far, near, far_2, near_2
        self.half_a, self.half_b = half_a, half_b
        self.sib_keys = {}

    def give(self, xx):
        p = self.p
        self.sib_keys[xx] = self.links.go(self.grads.at[xx, 1 - p.c], self.sib.at[xx], p.SIB)

    def take(self, xx):
        p, sib, grads = self.p, self.sib, self.grads
        self.links.arrived(sib.at[xx], self.sib_keys[xx], p.SIB)

        def one(j, carry):
            sib[xx, j] = (sib[xx, j].astype(F32) + grads[xx, p.c, j].astype(F32)).astype(BF16)
            return carry

        lax.fori_loop(0, 4, one, 0)

    def _ring(self, view, i, right, left, far, near, base):
        links = self.links
        ir, il, i2 = lax.rem(i + 1, 4), lax.rem(i + 3, 4), lax.rem(i + 2, 4)
        a, b = pl.ds(base, 16), pl.ds(base + 16, 16)
        na, nb = pl.ds(0, 16), pl.ds(16, 16)
        k0 = links.go(view(i2, a), far.at[0], right)
        k1 = links.go(view(i2, b), far.at[1], left)
        k2 = links.go(view(ir, b), near.at[0, :, nb], right)
        k3 = links.go(view(il, a), near.at[1, :, na], left)
        keys = []

        def merge():
            for way, k, row, at, source, target, to in (
                (0, k0, ir, a, left, right, na),
                (1, k1, il, b, right, left, nb),
            ):
                links.arrived(far.at[way], k, source)
                mine = view(row, at)

                def one(j, carry):
                    far[way, j] = (far[way, j].astype(F32) + mine[j].astype(F32)).astype(BF16)
                    return carry

                lax.fori_loop(0, far.shape[1], one, 0)
                keys.append(links.go(far.at[way], near.at[way, :, to], target))

        def settle():
            links.arrived(near.at[0, :, nb], k2, left)
            links.arrived(near.at[1, :, na], k3, right)
            links.arrived(near.at[0, :, na], keys[0], left)
            links.arrived(near.at[1, :, nb], keys[1], right)

        return merge, settle

    def first(self):
        p, sib = self.p, self.sib
        self.x_ring = self._ring(lambda j, r: sib.at[j, :, r], p.x, p.XR, p.XL, self.far.at[0], self.near.at[0], 0)
        self.z_ring = self._ring(lambda j, r: sib.at[:, j, r], p.z, p.ZR, p.ZL, self.far.at[1], self.near.at[1], 32)

    def merge(self):
        self.x_ring[0]()
        self.z_ring[0]()

    def turn(self):
        p, sib, near = self.p, self.sib, self.near
        self.x_ring[1]()

        def one_a(j, carry):
            total = sib[p.x, j, 0:32].astype(F32) + near[0, 0, j].astype(F32) + near[0, 1, j].astype(F32)
            self.half_a[j, 0] = total.astype(BF16)
            return carry

        lax.fori_loop(0, 4, one_a, 0)
        half_a, half_b = self.half_a, self.half_b
        self.ring_a = self._ring(
            lambda j, r: half_a.at[j, :, r], p.z, p.ZR, p.ZL, self.far_2.at[0], self.near_2.at[0], 0
        )
        self.z_ring[1]()

        def one_b(j, carry):
            total = sib[j, p.z, 32:64].astype(F32) + near[1, 0, j].astype(F32) + near[1, 1, j].astype(F32)
            self.half_b[j, 0] = total.astype(BF16)
            return carry

        lax.fori_loop(0, 4, one_b, 0)
        self.ring_b = self._ring(
            lambda j, r: half_b.at[j, :, r], p.x, p.XR, p.XL, self.far_2.at[1], self.near_2.at[1], 0
        )

    def merge_2(self):
        self.ring_a[0]()
        self.ring_b[0]()

    def finish(self, store):
        p, near = self.p, self.near_2
        self.ring_a[1]()
        store(0, self.half_a[p.z, 0].astype(F32) + near[0, 0, 0].astype(F32) + near[0, 1, 0].astype(F32))
        self.ring_b[1]()
        store(32, self.half_b[p.x, 0].astype(F32) + near[1, 0, 0].astype(F32) + near[1, 1, 0].astype(F32))

    @staticmethod
    def scratch(columns):
        return [
            pltpu.VMEM((4, 4, 64, columns), BF16),
            pltpu.VMEM((2, 2, 4, 16, columns), BF16),
            pltpu.VMEM((2, 2, 4, 32, columns), BF16),
            pltpu.VMEM((4, 1, 32, columns), BF16),
            pltpu.VMEM((4, 1, 32, columns), BF16),
            pltpu.VMEM((2, 2, 1, 16, columns), BF16),
            pltpu.VMEM((2, 2, 1, 32, columns), BF16),
        ]


def back_kernel(
    hbm_d_gate,
    hbm_d_up,
    hbm_hidden,
    mlp_full,
    mix_full,
    hbm_saved_0,
    hbm_saved_1,
    hbm_saved_2,
    hbm_saved_3,
    hbm_saved_4,
    hbm_saved_5,
    hbm_saved_6,
    hbm_saved_7,
    hbm_saved_8,
    entering,
    tokens,
    upstream,
    gain_rows,
    vectors,
    gate_w,
    doc_start,
    grad_tokens,
    block_out,
    grad_mix,
    small_sums,
    block_sums,
    gain_sums,
    hidden,
    states,
    pre,
    ext,
    decay_g,
    input_g,
    conv_low,
    mixed,
    normed_in,
    after_own,
    work,
    small_work,
    own_tokens,
    own_upstream,
    mid_part,
    out_part,
    d_after_low,
    d_after_own,
    gain_mid,
    d_mixed,
    tail_a,
    d_gates,
    d_both,
    small,
    rim_send,
    rim_recv,
    totals,
    totals_in,
    after,
    far_a,
    near_a,
    far_b,
    near_b,
    *rest,
):
    n_scatter = 7
    mix_scratch, rest = rest[:n_scatter], rest[n_scatter:]
    small_scratch, rest = rest[:n_scatter], rest[n_scatter:]
    saved = (
        (hbm_saved_0, states),
        (hbm_saved_1, pre),
        (hbm_saved_2, ext),
        (hbm_saved_3, decay_g),
        (hbm_saved_4, input_g),
        (hbm_saved_5, conv_low),
        (hbm_saved_6, mixed),
        (hbm_saved_7, normed_in),
        (hbm_saved_8, after_own),
    )
    back_steps(
        (hbm_d_gate, hbm_d_up, hbm_hidden), saved, mlp_full, mix_full, hidden, states, pre, ext, decay_g, input_g,
        conv_low, entering, mixed, normed_in, tokens, upstream, after_own, gain_rows, vectors, gate_w, doc_start,
        grad_tokens, block_out, grad_mix, small_sums, block_sums, gain_sums,
        work, small_work, own_tokens, own_upstream, mid_part, out_part, d_after_low, d_after_own, gain_mid,
        d_mixed, tail_a, d_gates, d_both, small, rim_send, rim_recv, totals, totals_in, after,
        far_a, near_a, far_b, near_b, mix_scratch, small_scratch, *rest,
    )


def back_steps(
    mlp_saved, saved, mlp_full, mix_full, hidden, states, pre, ext, decay_g, input_g,
    conv_low, entering, mixed, normed_in, tokens, upstream, after_own, gain_rows, vectors, gate_w, doc_start,
    grad_tokens, block_out, grad_mix, small_sums, block_sums, gain_sums,
    work, small_work, own_tokens, own_upstream, mid_part, out_part, d_after_low, d_after_own, gain_mid,
    d_mixed, tail_a, d_gates, d_both, small, rim_send, rim_recv, totals, totals_in, after,
    far_a, near_a, far_b, near_b, mix_scratch, small_scratch,
    small_all,
    gain_in,
    gain_y,
    gain_s,
    gain_z,
    local,
    tiles,
    send,
    recv,
):
    p = Place()
    links = Links(send, recv)
    sib = mix_scratch[0]
    early = (
        pltpu.make_async_copy(mlp_saved[0], sib.at[pl.ds(0, 2), :, :, pl.ds(0, MLP)], local.at[0]),
        pltpu.make_async_copy(mlp_saved[1], sib.at[pl.ds(2, 2), :, :, pl.ds(0, MLP)], local.at[1]),
    )
    for copy in early:
        copy.start()

    def weight_tile(n, j, slot):
        source = mlp_full.at[n // 2, n % 2, :, :, pl.ds(j * MLP, MLP)]
        return pltpu.make_async_copy(source, work.at[slot // 2, slot % 2, :, :, pl.ds(0, MLP)], tiles.at[slot])

    fetched = {}

    def fetch(n):
        for j in range(2):
            fetched[n, j] = weight_tile(n, j, (2 * n + j) % 8)
            fetched[n, j].start()

    for n in range(3):
        fetch(n)
    hidden_load = pltpu.make_async_copy(mlp_saved[2], hidden, local.at[2])
    hidden_load.start()
    saved_loads = [
        pltpu.make_async_copy(source, target, local.at[3 + k]) for k, (source, target) in enumerate(saved)
    ]
    load_tokens = pltpu.make_async_copy(tokens.at[p.y], own_tokens, local.at[12])
    load_tokens.start()
    load_upstream = pltpu.make_async_copy(upstream.at[p.y], own_upstream, local.at[13])
    load_upstream.start()
    others_y = [{"tensor": lax.rem(p.y + d, 4)} for d in (1, 2, 3)]
    others_z = [{"dp": lax.rem(p.z + d, 4)} for d in (1, 2, 3)]
    greet([p.seq_at(d) for d in range(1, 8)] + others_y + others_z)
    middles = [Reduce(links, p, mid_part, far_a, near_a, t, SPAN // 2) for t in (0, SPAN // 2)]
    for copy in early:
        copy.wait()

    def tile_of(slot):
        return work[slot // 2, slot % 2, :, :, 0:MLP].reshape(256, MLP)

    for n in range(8):
        if n + 3 < 8:
            fetch(n + 3)
        if n == 4:
            for middle in middles:
                middle.send_first()
        for j in range(2):
            fetched[n, j].wait()
        at = slice(n * 256, (n + 1) * 256)
        product = dot_nt(sib[0:2, :, :, 0:MLP].reshape(TOKENS, MLP), tile_of(2 * n % 8)) + dot_nt(
            sib[2:4, :, :, 0:MLP].reshape(TOKENS, MLP), tile_of((2 * n + 1) % 8)
        )
        mid_part[:, :, at] = product.astype(BF16).reshape(ROWS, SPAN, 256)
    for middle in middles:
        middle.send_second_far()
    middles[0].send_second_near()
    downs = [weight_tile(n, 2, n) for n in range(8)]
    for copy in downs:
        copy.start()
    middles[0].merge()
    middles[1].send_second_near()
    middles[1].merge()
    hidden_load.wait()
    for copy in downs:
        copy.wait()
    for copy in saved_loads:
        copy.start()

    def out_product(n, carry):
        weights = work[lax.div(n, 2), lax.rem(n, 2), :, :, 0:MLP].reshape(256, MLP)
        product = dot_nt(hidden[...], weights).astype(BF16)
        out_part[:, :, pl.ds(pl.multiple_of(n * 256, 256), 256)] = product.reshape(ROWS, SPAN, 256)
        return carry

    lax.fori_loop(0, 8, out_product, 0)
    load = pltpu.make_async_copy(mix_full, work, local.at[14])
    load.start()
    for copy in saved_loads:
        copy.wait()
    gain_mid[...] = jnp.zeros_like(gain_mid)
    gain_1 = gain_rows[1:2, :].astype(F32)
    load_upstream.wait()

    def middle_rows(k, carry):
        at = pl.ds(pl.multiple_of(k * 16, 16), 16)
        through, share = norm_back_rows(own_sum(middles[0], at), after_own[at, :], gain_1)
        gain_mid[...] += share[0:8] + share[8:16]
        total = own_upstream[at, :].astype(F32) + through
        d_after_own[at, :] = total
        d_after_low[p.y, at, :] = total.astype(BF16)
        return carry

    spreads_c = []
    for t, middle in enumerate(middles):
        middle.settle()
        lax.fori_loop(4 * t, 4 * t + 4, middle_rows, 0)
        links.sent(middle.keys())
        spreads_c.append(Spread(links, p, d_after_low, t * SPAN // 2, SPAN // 2))
        spreads_c[t].start()
    load.wait()
    rows_low = d_after_low.reshape(TOKENS, WIDTH)

    def mixed_row(row):
        rows = pl.ds(pl.multiple_of(row * SPAN, SPAN), SPAN)
        for start, size in ((0, 256), (256, 256), (512, 128)):
            weights = work[:, :, :, :, 2 * CHAN + start : 2 * CHAN + start + size].reshape(WIDTH, size)
            d_mixed[rows, start : start + size] = dot(d_after_low[row], weights)

    mixed_row(p.y)
    for spread_c in spreads_c:
        spread_c.forward()
    ahead = Reduce(links, p, out_part, far_b, near_b)
    ahead.send_first()
    ahead.send_second()
    for spread_c in spreads_c:
        spread_c.near()
    mixed_row(p.yl)
    mixed_row(p.yr)
    for spread_c in spreads_c:
        spread_c.far()
    mixed_row(p.y2)
    small[...] = jnp.zeros_like(small)
    totals[...] = jnp.zeros_like(totals)
    gain_in[...] = jnp.zeros_like(gain_in)
    offset = p.s * SPAN

    def chunk(i):
        r, g = lax.rem(i, ROWS), lax.div(i, ROWS)
        at = pl.ds(pl.multiple_of(g * LANES, LANES), LANES)
        rows = pl.ds(pl.multiple_of(r * SPAN, SPAN), SPAN)
        row = lax.broadcasted_iota(jnp.int32, (SPAN, LANES), 0)
        return r, g, at, rows, row

    def states_back(i, carry):
        r, g, at, rows, row = chunk(i)
        d_chunk = d_mixed[rows, at]
        value, slope = gelu_pair(pre[rows, at])
        d_both[rows, at] = (d_chunk * states[rows, at] * slope).astype(BF16)
        decay_now = jnp.exp(decay_g[rows, at] * vectors[7:8, at])
        carried = jnp.where(offset + row == doc_start[r], 0.0, decay_now)
        following = jnp.where(row == SPAN - 1, 1.0, pltpu.roll(carried, SPAN - 1, 0))
        a, b, first_a, first_b = row_scan(following, d_chunk * value, True)
        tail_a[rows, at] = a
        d_mixed[rows, at] = b
        put_pair(totals, at, r, carried[0:1] * first_a, carried[0:1] * first_b)
        return carry

    lax.fori_loop(0, ROWS * GROUPS, states_back, 0)
    keys = [links.go(totals, totals_in.at[p.s], p.seq_at(d)) for d in range(1, 8)]
    ahead.merge()
    state = jnp.zeros((ROWS, CHAN), F32)
    for d in range(1, 8):
        links.arrived(totals_in.at[p.seq_at(-d)["seq"]], keys[d - 1], p.seq_at(-d))
    totals_in[p.s] = totals[...]
    for source in range(7, 0, -1):
        both = totals_in[source]
        state = jnp.where(source > p.s, both[0:ROWS] * state + both[ROWS:], state)
    after[0:ROWS, :] = state
    after[ROWS:, :] = jnp.zeros((8 - ROWS, CHAN), F32)

    def gates_back(i, carry):
        r, g, at, rows, row = chunk(i)
        grads = d_mixed[rows, at] + tail_a[rows, at] * take_row(after, at, r)
        held = states[rows, at]
        previous = jnp.where(row == 0, take_row(entering, at, r), pltpu.roll(held, 1, 0))
        gate_d, gate_i = decay_g[rows, at], input_g[rows, at]
        rate = vectors[7:8, at]
        decay_now = jnp.exp(gate_d * rate)
        headroom = 1.0 - decay_now * decay_now
        root = jnp.sqrt(jnp.maximum(headroom, root_floor))
        conv = conv_low[rows, at].astype(F32)
        d_decay = jnp.where(offset + row == doc_start[r], 0.0, grads * previous) - jnp.where(
            headroom > root_floor, grads * gate_i * conv * decay_now / root, 0.0
        )
        d_log = d_decay * decay_now
        d_zero = d_log * rate * gate_d * (1.0 - gate_d)
        fed = grads * root
        d_one = fed * conv * gate_i * (1.0 - gate_i)
        d_gates[rows, pl.ds(pl.multiple_of(g * LANES, LANES), LANES)] = d_zero.astype(BF16)
        d_gates[rows, pl.ds(pl.multiple_of(CHAN + g * LANES, LANES), LANES)] = d_one.astype(BF16)
        tail_a[rows, at] = fed * gate_i
        small[5:6, at] += jnp.sum(d_zero, axis=0, keepdims=True)
        small[6:7, at] += jnp.sum(d_one, axis=0, keepdims=True)
        small[7:8, at] += jnp.sum(d_log * (-rate_scale * gate_d), axis=0, keepdims=True)
        return carry

    lax.fori_loop(0, ROWS * GROUPS, gates_back, 0)

    def ahead_rows(k, carry):
        at = pl.ds(pl.multiple_of(k * 16, 16), 16)
        block_out[p.y, at, :] = (after_own[at, :] + own_sum(ahead, at)).astype(BF16)
        return carry

    spread_b = Spread(links, p, block_out)

    d_conv = tail_a
    held = None
    for g in range(GROUPS):
        total = d_conv[:, g * LANES : (g + 1) * LANES]
        if held is not None:
            total = total + held
        if g < HEADS:
            lo = g * LANES
            product = dot_nt(d_gates[:, lo : lo + 256], gate_w[0, g]) + dot_nt(
                d_gates[:, CHAN + lo : CHAN + lo + 256], gate_w[1, g]
            )
            total = total + product[:, :LANES]
            held = product[:, LANES:]
        d_conv[:, g * LANES : (g + 1) * LANES] = total

    body = d_mixed

    def conv_back(i, carry):
        r, g, at, rows, row = chunk(i)
        d_chunk = d_conv[rows, at]
        begin = doc_start[r]
        place = offset + row
        here = place >= begin
        head = jnp.zeros((8, LANES), F32)
        total = jnp.zeros((SPAN, LANES), F32)
        for k in range(CONV):
            before = CONV - 1 - k
            same = (place - before >= begin) == here
            kept = jnp.where(same, d_chunk, 0.0)
            value = ext[r, PAD - before : PAD - before + SPAN, at]
            small[k : k + 1, at] += jnp.sum(kept * value, axis=0, keepdims=True)
            term = kept * vectors[k : k + 1, at]
            if before:
                total = total + jnp.where(row < SPAN - before, pltpu.roll(term, SPAN - before, 0), 0.0)
                head = head + jnp.where(
                    row[0:8] >= 8 - before, pltpu.roll(term[0:8], 8 - before, 0), 0.0
                )
            else:
                total = total + term
        small[4:5, at] += jnp.sum(d_chunk, axis=0, keepdims=True)
        body[rows, at] = total
        rim_send[r, :, at] = head
        return carry

    lax.fori_loop(0, ROWS * GROUPS, conv_back, 0)
    k_rim = links.go(rim_send, rim_recv, p.seq_at(-1))

    def blocks(j, h):
        lo = h * LANES
        product = dot_tn(conv_low[:, lo : lo + 256], d_gates[:, j * CHAN + lo : j * CHAN + lo + 256])
        for q in range(BLK // 32):
            row = (j * HEADS + h) * BLK + 32 * q
            n, inner = row // 64, row % 64
            piece = product[32 * (h + q) : 32 * (h + q + 1), :].astype(BF16)
            small_work[n // 8, (n // 4) % 2, n % 4, inner : inner + 32, :] = piece

    for j in range(2):
        for h in range(HEADS):
            blocks(j, h)
    for n in range(20, 32):
        small_work[n // 8, (n // 4) % 2, n % 4] = jnp.zeros((64, SMALL), BF16)
    for k, n in enumerate((20, 21, 22)):
        width = min(256, CHAN - 256 * k)
        both = jnp.concatenate([small[:, 256 * k : 256 * k + width], jnp.zeros((8, width), F32)], axis=0)
        small_work[n // 8, (n // 4) % 2, n % 4, 0:16, 0:width] = both.astype(BF16)
    small_scatter = Scatter(links, p, small_work, *small_scratch)
    for xx in range(4):
        small_scatter.give(xx)
    links.arrived(rim_recv, k_rim, p.seq_at(1))
    for r in range(ROWS):
        last = r * SPAN + SPAN - 8
        body[last : last + 8, :] += jnp.where(p.s == 7, 0.0, rim_recv[r])
    for r in range(ROWS):
        d_both[r * SPAN : (r + 1) * SPAN, CHAN:] = body[r * SPAN : (r + 1) * SPAN, :].astype(BF16)

    def first_part(n, carry):
        weights = work[lax.div(n, 2), lax.rem(n, 2), :, :, 0 : 2 * CHAN].reshape(256, 2 * CHAN)
        product = dot_nt(d_both[...], weights).astype(BF16)
        d_first[:, :, pl.ds(pl.multiple_of(n * 256, 256), 256)] = product.reshape(ROWS, SPAN, 256)
        return carry

    d_first = mid_part
    backs = [Reduce(links, p, d_first, far_a, near_a, t, SPAN // 2) for t in (0, SPAN // 2)]
    ahead.settle()
    lax.fori_loop(0, SPAN // 16, ahead_rows, 0)
    spread_b.start_first()
    lax.fori_loop(0, 4, first_part, 0)
    for back in backs:
        back.send_first()
    lax.fori_loop(4, 8, first_part, 0)
    for back in backs:
        back.send_second_far()
    backs[0].send_second_near()
    for xx in range(4):
        small_scatter.take(xx)
    small_scatter.first()

    def weight_grads(n):
        at = pl.ds(pl.multiple_of(n * 256, 256), 256)
        to = work.at[lax.div(n, 2), lax.rem(n, 2)]
        both = dot_tn(normed_in[:, at], d_both[...])
        to[:, :, 0 : 2 * CHAN] = both.astype(BF16).reshape(4, 64, 2 * CHAN)
        out = dot_tn(rows_low[:, at], mixed[...])
        to[:, :, 2 * CHAN : MIX_COLS] = out.astype(BF16).reshape(4, 64, CHAN)

    scatter = Scatter(links, p, work, *mix_scratch)

    def give(xx, carry):
        weight_grads(xx * 2 + 1 - p.c)
        return carry

    def keep(xx, carry):
        weight_grads(xx * 2 + p.c)
        return carry

    lax.fori_loop(0, 4, give, 0)
    for xx in range(4):
        scatter.give(xx)
    small_scatter.merge()
    backs[0].merge()
    backs[1].send_second_near()
    backs[1].merge()
    spread_b.start_second()
    lax.fori_loop(0, 4, keep, 0)
    small_scatter.turn()
    for xx in range(4):
        scatter.take(xx)
    scatter.first()
    def store_small(base, value):
        small_all[p.x, p.c, p.z, base : base + 32, :] = value.astype(BF16)

    small_scatter.merge_2()
    load_tokens.wait()
    gain = gain_rows[0:1, :].astype(F32)

    def back_rows(k, carry):
        at = pl.ds(pl.multiple_of(k * 16, 16), 16)
        through, share = norm_back_rows(own_sum(backs[0], at), own_tokens[at, :].astype(F32), gain)
        gain_in[...] += share[0:8] + share[8:16]
        grad_tokens[p.y, at, :] = (d_after_own[at, :] + through).astype(BF16)
        return carry

    spreads_a = []
    for t, back in enumerate(backs):
        back.settle()
        lax.fori_loop(4 * t, 4 * t + 4, back_rows, 0)
        spreads_a.append(Spread(links, p, grad_tokens, t * SPAN // 2, SPAN // 2))
        spreads_a[t].start()
    small_scatter.finish(store_small)
    small_gather = Gather(links, p, small_all, 128)
    small_gather.first()
    gain_y[p.y] = jnp.concatenate(
        [jnp.sum(gain_in[...], axis=0, keepdims=True), jnp.sum(gain_mid[...], axis=0, keepdims=True)], axis=0
    )
    y_keys = [links.go(gain_y.at[p.y], gain_y.at[p.y], device) for device in others_y]

    scatter.merge()
    small_gather.middle()
    small_gather.finish()
    small_gather.second()
    for spread_a in spreads_a:
        spread_a.forward()
    spread_b.forward()
    for d in (1, 2, 3):
        links.arrived(gain_y.at[lax.rem(p.y + 4 - d, 4)], y_keys[d - 1], others_y[0])
    gain_z[p.z] = gain_y[0] + gain_y[1] + gain_y[2] + gain_y[3]
    z_keys = [links.go(gain_z.at[p.z], gain_z.at[p.z], device) for device in others_z]
    scatter.turn()
    for d in (1, 2, 3):
        links.arrived(gain_z.at[lax.rem(p.z + 4 - d, 4)], z_keys[d - 1], others_z[0])
    gain_s[p.s] = gain_z[0] + gain_z[1] + gain_z[2] + gain_z[3]
    s_keys = [links.go(gain_s.at[p.s], gain_s.at[p.s], p.seq_at(d)) for d in range(1, 8)]
    small_gather.middle()
    small_gather.finish()
    scatter.merge_2()
    for d in range(1, 8):
        links.arrived(gain_s.at[p.seq_at(-d)["seq"]], s_keys[d - 1], p.seq_at(-d))
    total = gain_s[0]
    for s in range(1, 8):
        total = total + gain_s[s]
    gain_sums[...] = total
    spread_b.near()
    spread_b.far()
    small_gather.settle()
    for k, n in enumerate((20, 21, 22)):
        width = min(256, CHAN - 256 * k)
        value = small_all[n // 8, (n // 4) % 2, n % 4, 0:16, 0:width].astype(F32)
        small_sums[:, 256 * k : 256 * k + width] = value[0:8]
    for n in range(20):
        value = small_all[n // 8, (n // 4) % 2, n % 4].astype(F32)
        block_sums[64 * n : 64 * (n + 1), :] = value

    def store(base, value):
        grad_mix[base : base + 32, :] = value

    scatter.finish(store)
    for spread_a in spreads_a:
        spread_a.near()
        spread_a.far()
    links.drain()


def back_all(*operands):
    shape = jax.ShapeDtypeStruct
    tc = (TOKENS, CHAN)
    pair = [pltpu.VMEM((2, SPAN, HALF), BF16), pltpu.VMEM((2, SPAN, WIDTH), BF16)]
    return pl.pallas_call(
        back_kernel,
        out_shape=[
            shape((ROWS, SPAN, WIDTH), BF16),
            shape((ROWS, SPAN, WIDTH), BF16),
            shape((64, MIX_COLS), F32),
            shape((8, CHAN), F32),
            shape((2 * HEADS * BLK, 256), F32),
            shape((2, WIDTH), F32),
        ],
        in_specs=[anyspace()] * 14 + [vmem()] + [anyspace()] * 2 + [vmem()] * 3 + [smem()],
        out_specs=[vmem()] * 6,
        scratch_shapes=[
            pltpu.VMEM((TOKENS, MLP), BF16),
            pltpu.VMEM(tc, F32),
            pltpu.VMEM(tc, F32),
            pltpu.VMEM((ROWS, PAD + SPAN, CHAN), F32),
            pltpu.VMEM(tc, F32),
            pltpu.VMEM(tc, F32),
            pltpu.VMEM(tc, BF16),
            pltpu.VMEM(tc, BF16),
            pltpu.VMEM((TOKENS, WIDTH), BF16),
            pltpu.VMEM((SPAN, WIDTH), F32),
            pltpu.VMEM((4, 2, 4, 64, MIX_COLS), BF16),
            pltpu.VMEM((4, 2, 4, 64, SMALL), BF16),
            pltpu.VMEM((SPAN, WIDTH), BF16),
            pltpu.VMEM((SPAN, WIDTH), BF16),
            pltpu.VMEM((ROWS, SPAN, WIDTH), BF16),
            pltpu.VMEM((ROWS, SPAN, WIDTH), BF16),
            pltpu.VMEM((ROWS, SPAN, WIDTH), BF16),
            pltpu.VMEM((SPAN, WIDTH), F32),
            pltpu.VMEM((8, WIDTH), F32),
            pltpu.VMEM(tc, F32),
            pltpu.VMEM(tc, F32),
            pltpu.VMEM((TOKENS, 2 * CHAN), BF16),
            pltpu.VMEM((TOKENS, 2 * CHAN), BF16),
            pltpu.VMEM((8, CHAN), F32),
            pltpu.VMEM((ROWS, PAD, CHAN), F32),
            pltpu.VMEM((ROWS, PAD, CHAN), F32),
            pltpu.VMEM((8, CHAN), F32),
            pltpu.VMEM((8, 8, CHAN), F32),
            pltpu.VMEM((8, CHAN), F32),
        ]
        + pair * 2
        + Scatter.scratch(MIX_COLS)
        + Scatter.scratch(SMALL)
        + [
            pltpu.VMEM((4, 2, 4, 64, SMALL), BF16),
            pltpu.VMEM((8, WIDTH), F32),
            pltpu.VMEM((4, 2, WIDTH), F32),
            pltpu.VMEM((8, 2, WIDTH), F32),
            pltpu.VMEM((4, 2, WIDTH), F32),
            pltpu.SemaphoreType.DMA((15,)),
            pltpu.SemaphoreType.DMA((8,)),
            pltpu.SemaphoreType.DMA((224,)),
            pltpu.SemaphoreType.DMA((224,)),
        ],
        compiler_params=params(2),
        name="back_all",
    )(*operands)


def finish_kernel(
    block_in,
    tokens_in,
    mix_sum,
    small,
    blocks_in,
    gains_in,
    mlp_sum,
    decay_param,
    block_out,
    grad_tokens,
    grad_gains,
    grad_mix_in,
    grad_mix_out,
    grad_conv,
    grad_conv_bias,
    grad_blocks,
    grad_bias,
    grad_decay,
    grad_mlp_in,
    grad_mlp_out,
):
    step = pl.program_id(0)
    block_out[...] = block_in[...]
    grad_tokens[...] = tokens_in[...]
    for h in range(HEADS):

        @pl.when(step == h)
        def _():
            for j in range(2):
                grad_blocks[j, 0] = blocks_in[j, 0, :, 32 * h : 32 * h + BLK]

    @pl.when(step == 0)
    def _():
        grad_gains[...] = gains_in[...]
        for j in range(2):
            grad_mix_in[j] = mix_sum[:, j * CHAN : (j + 1) * CHAN]
        grad_mix_out[...] = mix_sum[:, 2 * CHAN :]
        grad_conv[...] = small[0:CONV, :]
        grad_bias[...] = small[CONV + 1 : CONV + 3, :]
        grad_conv_bias[...] = small[CONV : CONV + 1, :].reshape(CHAN)
        slope = jax.nn.sigmoid(decay_param[...].astype(F32))
        grad_decay[...] = small[CONV + 3 : CONV + 4, :].reshape(CHAN) * slope
        for f in range(CHUNKS):
            lo, at = 3 * f * CHUNK, pl.ds(f * CHUNK, CHUNK)
            for j in range(2):
                grad_mlp_in[j, :, at] = mlp_sum[:, lo + j * CHUNK : lo + (j + 1) * CHUNK].astype(F32)
            grad_mlp_out[:, at] = mlp_sum[:, lo + 2 * CHUNK : lo + 3 * CHUNK].astype(F32)


def finish(*operands):
    shape = jax.ShapeDtypeStruct
    row = lambda width: pl.BlockSpec((1, SPAN, width), lambda i: (i, 0, 0))
    whole = lambda *dims: pl.BlockSpec(dims, lambda i: (0,) * len(dims))
    head = lambda width: pl.BlockSpec((2, 1, BLK, width), lambda i: (0, i, 0, 0))
    return pl.pallas_call(
        finish_kernel,
        grid=(ROWS,),
        out_shape=[
            shape((ROWS, SPAN, WIDTH), BF16),
            shape((ROWS, SPAN, WIDTH), BF16),
            shape((2, WIDTH), F32),
            shape((2, 64, CHAN), F32),
            shape((64, CHAN), F32),
            shape((CONV, CHAN), F32),
            shape((CHAN,), F32),
            shape((2, HEADS, BLK, BLK), F32),
            shape((2, CHAN), F32),
            shape((CHAN,), F32),
            shape((2, 64, MLP), F32),
            shape((64, MLP), F32),
        ],
        in_specs=[
            row(WIDTH),
            row(WIDTH),
            whole(64, MIX_COLS),
            whole(8, CHAN),
            head(256),
            whole(2, WIDTH),
            whole(64, MLP_COLS),
            whole(CHAN),
        ],
        out_specs=[
            row(WIDTH),
            row(WIDTH),
            whole(2, WIDTH),
            whole(2, 64, CHAN),
            whole(64, CHAN),
            whole(CONV, CHAN),
            whole(CHAN),
            head(BLK),
            whole(2, CHAN),
            whole(CHAN),
            whole(2, 64, MLP),
            whole(64, MLP),
        ],
        compiler_params=pltpu.CompilerParams(vmem_limit_bytes=VMEM_BYTES),
        name="finish",
    )(*operands)


def per_device(
    tokens,
    init_state,
    conv_state,
    fresh_rows,
    doc_start,
    norm_gains,
    mix_in,
    mix_out,
    conv_weight,
    conv_bias,
    gate_blocks,
    gate_bias,
    decay_param,
    mlp_in,
    mlp_out,
    cotangent,
):
    (
        mix_full,
        mlp_full,
        states,
        pre,
        ext,
        decay_g,
        input_g,
        conv_low,
        mixed,
        normed_in,
        entering,
        vectors,
        gate_w,
        normed_mid,
        after_own,
    ) = mix_forward(
        tokens.reshape(TOKENS, WIDTH),
        mix_in,
        mix_out.T,
        mlp_in,
        mlp_out.T,
        init_state,
        conv_state.transpose(1, 0, 2),
        fresh_rows,
        doc_start,
        norm_gains,
        conv_weight,
        conv_bias,
        gate_bias,
        decay_param,
        gate_blocks,
    )
    d_gate, d_up, hidden, grad_mlp, states_out = mlp_all(
        normed_mid.reshape(TOKENS, WIDTH),
        cotangent.reshape(TOKENS, WIDTH),
        mlp_full.reshape(WIDTH, MLP_COLS),
        states.reshape(ROWS, SPAN, CHAN),
    )
    grad_mlp = lax.psum_scatter(grad_mlp, ("seq", "dp"), scatter_dimension=0, tiled=True)
    grad_tokens, block_out, grad_mix, small, blocks, grad_gains = back_all(
        d_gate.reshape(2, 4, 64, MLP),
        d_up.reshape(2, 4, 64, MLP),
        hidden,
        mlp_full,
        mix_full,
        states,
        pre,
        ext,
        decay_g,
        input_g,
        conv_low,
        mixed,
        normed_in,
        after_own,
        entering,
        tokens,
        cotangent,
        norm_gains,
        vectors,
        gate_w,
        doc_start,
    )
    (
        block_out,
        grad_tokens,
        grad_gains,
        grad_mix_in,
        grad_mix_out,
        grad_conv,
        grad_conv_bias,
        grad_blocks,
        grad_bias,
        grad_decay,
        grad_mlp_in,
        grad_mlp_out,
    ) = finish(
        block_out,
        grad_tokens,
        grad_mix,
        small,
        blocks.reshape(2, HEADS, BLK, 256),
        grad_gains,
        grad_mlp,
        decay_param,
    )
    return (
        block_out,
        states_out,
        grad_tokens,
        grad_gains,
        grad_mix_in,
        grad_mix_out.T,
        grad_conv,
        grad_conv_bias,
        grad_blocks,
        grad_bias,
        grad_decay,
        grad_mlp_in,
        grad_mlp_out.T,
    )


def solution(mesh):
    in_specs = (
        P("dp", "seq", None),
        P("dp", "tensor"),
        P("dp", None, "tensor"),
        P("dp"),
        P("dp"),
        P(),
        P(None, ("seq", "dp"), "tensor"),
        P("tensor", ("seq", "dp")),
        P(None, "tensor"),
        P("tensor"),
        P(None, "tensor", None, None),
        P(None, "tensor"),
        P("tensor"),
        P(None, ("seq", "dp"), "tensor"),
        P("tensor", ("seq", "dp")),
        P("dp", "seq", None),
    )
    out_specs = (
        P("dp", "seq", None),
        P("dp", "seq", "tensor"),
        P("dp", "seq", None),
        P(),
        P(None, ("seq", "dp"), "tensor"),
        P("tensor", ("seq", "dp")),
        P(None, "tensor"),
        P("tensor"),
        P(None, "tensor", None, None),
        P(None, "tensor"),
        P("tensor"),
        P(None, ("seq", "dp"), "tensor"),
        P("tensor", ("seq", "dp")),
    )
    return jax.shard_map(
        per_device, mesh=mesh, in_specs=in_specs, out_specs=out_specs, check_vma=False
    )
```
